512 devices in a mesh: row: 64 (over z, y), grp: 8 (over x, core).
Axes of the slice: x: 4, y: 4, z: 16, core: 2. Of those that a mesh axis runs over, the one named last changes fastest.
Arguments:
- design: float32 [131072, 2048], P('row', 'grp')
- rademacher: int32 [131072], P('row'), may hold values from 0 to 1
- target: float32 [131072], P('row'), may hold values from -6 to 6
- sample_rows: int32 [64, 8, 16], P('row', 'grp'), may hold values from 0 to 2047
- checksum_seeds: int32 [2048], P('grp'), may hold values from 1 to 16
Outputs:
- solution: float32 [2048], P('grp')
- residual: float32 [131072], P('row')
- checksum: float32 [2048], P('grp')
The draws below stay inside these ranges and needn't reach their ends.
Inputs may be any that keep to these rules, and one draw needn't show every extreme that they name: sample_rows holds row numbers within one index's block of 2048 rows; a row may be drawn more than once.
All inputs are finite; a program needn't handle non-finite values.
Results may differ from the reference program's by a relative error of at most 0.0003.
Values sent between devices are 32-bit elements; how exact they have to be, the bound alone decides.
No kernel may reach another device: no remote copies, remote signals or barrier semaphores. Data moves between devices by JAX's collectives and lax.ppermute only.
A program may use at most 64 MiB of HBM per device.

```python
import math
import jax
import jax.numpy as jnp
from jax import lax

NCOL = 2048
ROWS_DEV = 2048
SAMP_DEV = 16
TOTAL_ROWS = 131072
SAMPLES = 1024
N_ROW = 64
N_GRP = 8


def draw_design(key, part):
    key = jax.random.fold_in(key, 11)
    col_key = jax.random.fold_in(key, 0)
    value_key = jax.random.fold_in(key, 2)
    col_scale = jnp.exp(jax.random.uniform(col_key, (NCOL,), jnp.float32, 0.0, math.log(10.0)))
    values = jax.random.normal(value_key, (TOTAL_ROWS, NCOL), jnp.float32)
    return values * col_scale[None, :] / math.sqrt(TOTAL_ROWS)


def touch_ends(array, key, least, high):
    longest = array.shape.index(max(array.shape))
    spots = []
    for shift in (0, 1):
        where = [jax.random.randint(jax.random.fold_in(key, axis), (), 0, length) for axis, length in enumerate(array.shape)]
        where[longest] = (where[longest] + shift) % array.shape[longest]
        spots.append(tuple(where))
    return array.at[spots[0]].set(least).at[spots[1]].set(high)


def block_scale(rng, dims, pieces, smallest, top_value):
    factor_of = 1.0
    for dim, shards_of in pieces:
        steps = jax.random.uniform(jax.random.fold_in(jax.random.fold_in(rng, 6), dim), (shards_of,), jnp.float32, smallest / len(pieces), top_value / len(pieces))
        factor_of = factor_of * jnp.repeat(jnp.exp(steps), dims[dim] // shards_of).reshape((-1,) + (1,) * (len(dims) - 1 - dim))
    return factor_of


def normal_values(own_key, shape, deviation, bound, cuts=(), kind=jnp.bfloat16):
    array = jax.random.normal(own_key, shape, jnp.float32) * deviation
    if len(cuts) > 0:
        array = block_scale(own_key, shape, cuts, -0.22, 0.18) * array
    return jnp.clip(array, min=-bound, max=bound).astype(kind)


def setup_inputs(seed: int = 0) -> dict:
    key_list = jax.random.split(jax.random.key(seed), 6)
    return {
        "design": draw_design(jax.random.fold_in(key_list[5], 71), 0),
        "rademacher": touch_ends(jax.random.randint(key_list[1], (TOTAL_ROWS,), 0, 2), jax.random.fold_in(key_list[1], 1), 0, 1).astype(jnp.int32),
        "target": normal_values(key_list[2], (TOTAL_ROWS,), 1.0, 6.0, ((0, 64),), jnp.float32),
        "sample_rows": touch_ends(jax.random.randint(key_list[3], (N_ROW, N_GRP, SAMP_DEV), 0, ROWS_DEV), jax.random.fold_in(key_list[3], 1), 0, ROWS_DEV - 1).astype(jnp.int32),
        "checksum_seeds": touch_ends(jax.random.randint(key_list[4], (NCOL,), 1, 17), jax.random.fold_in(key_list[4], 1), 1, 16).astype(jnp.int32),
    }


def walsh(column_block):
    row_total = column_block.shape[0]
    stride_len = 1
    while stride_len < row_total:
        shaped = column_block.reshape(row_total // (2 * stride_len), 2, stride_len, column_block.shape[1])
        upper_part = shaped[:, 0]
        lower_part = shaped[:, 1]
        column_block = jnp.stack([upper_part + lower_part, upper_part - lower_part], axis=1).reshape(row_total, -1)
        stride_len = stride_len * 2
    return column_block

def solve_lower(factor, vector):
    return lax.linalg.triangular_solve(factor, vector[:, None], left_side=True, lower=True)[:, 0]

def solve_upper(factor, vector):
    return lax.linalg.triangular_solve(factor, vector[:, None], left_side=True, lower=True, transpose_a=True)[:, 0]

def reference(design, rademacher, target, sample_rows, checksum_seeds):
    highest = lax.Precision.HIGHEST
    group_cols = NCOL // N_GRP
    sign_vector = 1.0 - 2.0 * rademacher.astype(jnp.float32)
    norm_scale = 1.0 / math.sqrt(TOTAL_ROWS)
    offsets = (jnp.arange(N_ROW, dtype=jnp.int32) * ROWS_DEV)[:, None]
    factors = []
    check_parts = []
    for group_id in range(N_GRP):
        group_slab = design[:, group_id * group_cols:(group_id + 1) * group_cols]
        mixed = walsh(group_slab * sign_vector[:, None]) * norm_scale
        row_ids = (sample_rows[:, group_id, :].astype(jnp.int32) + offsets).reshape(-1)
        sampled = mixed[row_ids]
        gram_block = jnp.dot(sampled.T.astype(jnp.float32), sampled.astype(jnp.float32), precision=highest, preferred_element_type=jnp.float32) * (TOTAL_ROWS / SAMPLES)
        lower_factor = jnp.linalg.cholesky(gram_block)
        weights = checksum_seeds[group_id * group_cols:(group_id + 1) * group_cols].astype(jnp.float32) / 16.0
        check_parts.append(solve_lower(lower_factor, jnp.dot(gram_block, weights, precision=highest)))
        factors.append(lower_factor)
    checksum = jnp.concatenate(check_parts)
    beta_one = jnp.sqrt(jnp.sum(target * target))
    unit_left = target / beta_one
    back_sum = jnp.dot(unit_left, design, precision=highest)
    pre_right = jnp.concatenate([solve_lower(factors[g], back_sum[g * group_cols:(g + 1) * group_cols]) for g in range(N_GRP)])
    alpha_one = jnp.sqrt(jnp.sum(pre_right * pre_right))
    unit_right = pre_right / alpha_one
    direction = jnp.concatenate([solve_upper(factors[g], unit_right[g * group_cols:(g + 1) * group_cols]) for g in range(N_GRP)])
    forward_sum = jnp.dot(design, direction, precision=highest)
    left_gap = forward_sum - alpha_one * unit_left
    beta_two = jnp.sqrt(jnp.sum(left_gap * left_gap))
    step_size = alpha_one * beta_one / (alpha_one * alpha_one + beta_two * beta_two)
    solution = step_size * direction
    residual = target - step_size * forward_sum
    return (solution, residual, checksum)
```

```python
import jax
import jax.numpy as jnp
from jax import lax
from jax.experimental import pallas as pl
from jax.experimental.pallas import tpu as pltpu
from jax.sharding import Mesh, PartitionSpec as P

Z, Y, X, C = 16, 4, 4, 2
ROWS = ("z", "y")
GRPS = ("x", "c")
F32 = jnp.float32
BF16 = jnp.bfloat16


def parity_sign(bits):
    bits = jnp.bitwise_xor(bits, jnp.right_shift(bits, 8))
    bits = jnp.bitwise_xor(bits, jnp.right_shift(bits, 4))
    odd = jnp.bitwise_and(jnp.right_shift(0x6996, jnp.bitwise_and(bits, 15)), 1)
    return 1.0 - 2.0 * odd.astype(F32)


def split3(value):
    hi = value.astype(BF16)
    rest = value - hi.astype(F32)
    mid = rest.astype(BF16)
    lo = (rest - mid.astype(F32)).astype(BF16)
    return hi, mid, lo


def sketch_kernel(pos_ref, idx_ref, rad_ref, tgt_ref, slab_ref, out_ref, sgn_ref, x_ref):
    count = idx_ref.shape[0]
    height, breadth = slab_ref.shape
    hi, mid, lo = split3(slab_ref[...])
    x_ref[0] = hi
    x_ref[1] = mid
    x_ref[2] = lo
    picks = jnp.broadcast_to(idx_ref[...], (count, 128))
    lane = lax.broadcasted_iota(jnp.int32, (count, 128), 1)
    slot = lax.broadcasted_iota(jnp.int32, (count, 128), 0)
    far = parity_sign(jnp.bitwise_and(jnp.right_shift(slot, 4), pos_ref[0]))
    base = parity_sign(jnp.bitwise_and(picks, lane)) * far * 0.03125
    base = base.astype(BF16)
    flips = [
        (1.0 - 2.0 * jnp.bitwise_and(jnp.right_shift(picks, 7 + b), 1).astype(F32)).astype(BF16)
        for b in range(4)
    ]
    row_sign = (1.0 - 2.0 * rad_ref[...].astype(F32)).astype(BF16)
    gray = 0
    current = base
    for step in range(height // 128):
        new = step ^ (step >> 1)
        if step:
            current = current * flips[(new ^ gray).bit_length() - 1]
        gray = new
        sgn_ref[0:count, gray * 128 : (gray + 1) * 128] = (
            current * row_sign[:, gray * 128 : (gray + 1) * 128]
        )
    thi, tmid, tlo = split3(tgt_ref[...])
    sgn_ref[count : count + 16, :] = jnp.concatenate(
        [thi, tmid, tlo, jnp.zeros((13, height), BF16)], axis=0
    )

    def product(rows):
        total = jnp.dot(rows, x_ref[0], preferred_element_type=F32)
        total += jnp.dot(rows, x_ref[1], preferred_element_type=F32)
        return total + jnp.dot(rows, x_ref[2], preferred_element_type=F32)

    back = jnp.sum(product(sgn_ref[count : count + 16, :]), axis=0, keepdims=True)
    for part in range(Y):
        out_ref[part, 0:256, :] = product(sgn_ref[part * 256 : (part + 1) * 256, :])
        out_ref[part, 256:264, :] = jnp.broadcast_to(back, (8, breadth))


def sketch(position, picks, rademacher, target, design):
    height, breadth = design.shape
    vmem = pl.BlockSpec(memory_space=pltpu.VMEM)
    return pl.pallas_call(
        sketch_kernel,
        out_shape=jax.ShapeDtypeStruct((Y, 264, breadth), F32),
        in_specs=[pl.BlockSpec(memory_space=pltpu.SMEM), vmem, vmem, vmem, vmem],
        out_specs=vmem,
        scratch_shapes=[
            pltpu.VMEM((1024 + 16, height), BF16),
            pltpu.VMEM((3, height, breadth), BF16),
        ],
        compiler_params=pltpu.CompilerParams(vmem_limit_bytes=40 * 2**20),
        name="sketch",
    )(position, picks, rademacher, target, design)


def exchange(pieces, axes):
    return lax.all_to_all(pieces, axes, split_axis=0, concat_axis=0, tiled=True)


def share(value, axes, count):
    return exchange(jnp.broadcast_to(value[None], (count,) + value.shape), axes)


def solve_lower(factor, vector):
    return lax.linalg.triangular_solve(factor, vector[:, None], left_side=True, lower=True)[:, 0]


def solve_upper(factor, vector):
    return lax.linalg.triangular_solve(
        factor, vector[:, None], left_side=True, lower=True, transpose_a=True
    )[:, 0]


def body(design, rademacher, target, sample_rows, checksum_seeds):
    highest = lax.Precision.HIGHEST
    height, breadth = design.shape
    position = lax.axis_index(ROWS).astype(jnp.int32).reshape(1)
    picks = share(sample_rows.reshape(16), ROWS, Z * Y).reshape(Z * Y * 16, 1)
    parts = sketch(
        position, picks, rademacher.reshape(1, height), target.reshape(1, height), design
    )
    mine = jnp.sum(exchange(parts, "y"), axis=0)
    pieces = jnp.concatenate(
        [mine[:256].reshape(Z, 16, breadth), jnp.broadcast_to(mine[None, 256:], (Z, 8, breadth))],
        axis=1,
    )
    mine = jnp.sum(exchange(pieces, "z"), axis=0)
    back_sum = mine[16]
    rows = share(mine[:16], "z", Z).reshape(Z * 16, breadth)
    gram = jnp.dot(rows.T, rows, precision=highest, preferred_element_type=F32)
    gram = jnp.sum(share(gram, "y", Y), axis=0)
    lower_factor = jnp.linalg.cholesky(gram)
    weights = checksum_seeds.astype(F32) / 16.0
    checksum = solve_lower(lower_factor, jnp.dot(gram, weights, precision=highest))
    half = solve_lower(lower_factor, back_sum)
    direction = solve_upper(lower_factor, half)
    image = jnp.dot(design, direction, precision=highest)
    packed = jnp.concatenate([image, jnp.broadcast_to(jnp.sum(half * half), (128,))])
    packed = jnp.sum(share(packed, GRPS, X * C), axis=0)
    image = packed[:height]
    numer = packed[height]
    denom = jnp.sum(
        share(jnp.broadcast_to(jnp.sum(image * image), (1, 128)), ROWS, Z * Y), axis=(0, 1)
    )[0]
    step = numer / denom
    return (step * direction, target - step * image, checksum)


def solution(mesh):
    fine = Mesh(mesh.devices.reshape(Z, Y, X, C), ROWS + GRPS)
    in_specs = (P(ROWS, GRPS), P(ROWS), P(ROWS), P(ROWS, GRPS, None), P(GRPS))
    out_specs = (P(GRPS), P(ROWS), P(GRPS))
    return jax.shard_map(body, mesh=fine, in_specs=in_specs, out_specs=out_specs, check_vma=False)
```

```python
import jax
import jax.numpy as jnp
from jax import lax
from jax.experimental import pallas as pl
from jax.experimental.pallas import tpu as pltpu
from jax.sharding import Mesh, PartitionSpec as P

Z, Y, X, C = 16, 4, 4, 2
ROWS = ("z", "y")
GRPS = ("x", "c")
F32 = jnp.float32
BF16 = jnp.bfloat16


def parity_sign(bits):
    bits = jnp.bitwise_xor(bits, jnp.right_shift(bits, 8))
    bits = jnp.bitwise_xor(bits, jnp.right_shift(bits, 4))
    odd = jnp.bitwise_and(jnp.right_shift(0x6996, jnp.bitwise_and(bits, 15)), 1)
    return 1.0 - 2.0 * odd.astype(F32)


def split3(value):
    hi = value.astype(BF16)
    rest = value - hi.astype(F32)
    mid = rest.astype(BF16)
    lo = (rest - mid.astype(F32)).astype(BF16)
    return hi, mid, lo


def sketch_kernel(pos_ref, idx_ref, rad_ref, tgt_ref, slab_ref, out_ref, sgn_ref, x_ref):
    count = idx_ref.shape[0]
    height, breadth = slab_ref.shape
    hi, mid, lo = split3(slab_ref[...])
    x_ref[0] = hi
    x_ref[1] = mid
    x_ref[2] = lo
    picks = jnp.broadcast_to(idx_ref[...], (count, 128))
    lane = lax.broadcasted_iota(jnp.int32, (count, 128), 1)
    slot = lax.broadcasted_iota(jnp.int32, (count, 128), 0)
    far = parity_sign(jnp.bitwise_and(jnp.right_shift(slot, 4), pos_ref[0]))
    base = parity_sign(jnp.bitwise_and(picks, lane)) * far * 0.03125
    base = base.astype(BF16)
    flips = [
        (1.0 - 2.0 * jnp.bitwise_and(jnp.right_shift(picks, 7 + b), 1).astype(F32)).astype(BF16)
        for b in range(4)
    ]
    row_sign = (1.0 - 2.0 * rad_ref[...].astype(F32)).astype(BF16)
    gray = 0
    current = base
    for step in range(height // 128):
        new = step ^ (step >> 1)
        if step:
            current = current * flips[(new ^ gray).bit_length() - 1]
        gray = new
        sgn_ref[0:count, gray * 128 : (gray + 1) * 128] = (
            current * row_sign[:, gray * 128 : (gray + 1) * 128]
        )
    thi, tmid, tlo = split3(tgt_ref[...])
    sgn_ref[count : count + 16, :] = jnp.concatenate(
        [thi, tmid, tlo, jnp.zeros((13, height), BF16)], axis=0
    )

    def product(rows):
        total = jnp.dot(rows, x_ref[0], preferred_element_type=F32)
        total += jnp.dot(rows, x_ref[1], preferred_element_type=F32)
        return total + jnp.dot(rows, x_ref[2], preferred_element_type=F32)

    back = jnp.sum(product(sgn_ref[count : count + 16, :]), axis=0, keepdims=True)
    for part in range(Y):
        out_ref[part, 0:256, :] = product(sgn_ref[part * 256 : (part + 1) * 256, :])
        out_ref[part, 256:264, :] = jnp.broadcast_to(back, (8, breadth))


def sketch(position, picks, rademacher, target, design):
    height, breadth = design.shape
    vmem = pl.BlockSpec(memory_space=pltpu.VMEM)
    return pl.pallas_call(
        sketch_kernel,
        out_shape=jax.ShapeDtypeStruct((Y, 264, breadth), F32),
        in_specs=[pl.BlockSpec(memory_space=pltpu.SMEM), vmem, vmem, vmem, vmem],
        out_specs=vmem,
        scratch_shapes=[
            pltpu.VMEM((1024 + 16, height), BF16),
            pltpu.VMEM((3, height, breadth), BF16),
        ],
        compiler_params=pltpu.CompilerParams(vmem_limit_bytes=40 * 2**20),
        name="sketch",
    )(position, picks, rademacher, target, design)


def exchange(pieces, axes):
    return lax.all_to_all(pieces, axes, split_axis=0, concat_axis=0, tiled=True)


def share(value, axes, count):
    return exchange(jnp.broadcast_to(value[None], (count,) + value.shape), axes)


NB = 16


def row_bcast(value, row):
    return jnp.broadcast_to(value[row : row + 1, :], value.shape)


def dot_nt(left, right):
    return lax.dot_general(left, right, (((1,), (1,)), ((), ())), preferred_element_type=F32)


def dot_tn(left, right):
    return lax.dot_general(left, right, (((0,), (0,)), ((), ())), preferred_element_type=F32)


def factor_kernel(gram_ref, back_ref, seed_ref, slab_ref, image_ref, dir_ref, check_ref, work_ref):
    size = gram_ref.shape[1]
    height = slab_ref.shape[0]
    gram = gram_ref[0]
    for part in range(1, gram_ref.shape[0]):
        gram = gram + gram_ref[part]
    sub = lax.broadcasted_iota(jnp.int32, (128, size), 0)
    weights = seed_ref[...].astype(F32) * 0.0625
    weight_rows = jnp.where(sub == 1, jnp.broadcast_to(weights, (128, size)), 0.0).astype(BF16)
    back_rows = jnp.where(sub == 0, jnp.broadcast_to(back_ref[...], (128, size)), 0.0)
    eye = (
        lax.broadcasted_iota(jnp.int32, (size, size), 0)
        == lax.broadcasted_iota(jnp.int32, (size, size), 1)
    ).astype(BF16)
    extra = jnp.zeros((size, 128), F32)
    for term in split3(gram):
        extra = extra + dot_nt(term, weight_rows)
    for term in split3(back_rows):
        extra = extra + dot_nt(eye, term)
    work_ref[:, :size] = gram
    work_ref[:, size:] = extra

    wide = size + 128
    lane = lax.broadcasted_iota(jnp.int32, (NB, wide), 1)
    row = lax.broadcasted_iota(jnp.int32, (NB, wide), 0)
    small_row = lax.broadcasted_iota(jnp.int32, (NB, 128), 0)
    for block in range(size // NB):
        at = block * NB
        panel = work_ref[at : at + NB, :]
        cols = [jnp.broadcast_to(panel[:, at + j : at + j + 1], (NB, 128)) for j in range(NB)]
        panel = jnp.where((lane >= at) & (lane < at + NB), (lane - at == row).astype(F32), panel)
        scale = jnp.zeros((NB, 128), F32)
        for j in range(NB):
            pivot = row_bcast(cols[j], j)
            coef = jnp.where(small_row > j, cols[j] / pivot, 0.0)
            scale = jnp.where(small_row == j, pivot, scale)
            for later in range(j + 1, NB):
                cols[later] = cols[later] - coef * row_bcast(cols[later], j)
            panel = panel - jnp.tile(coef, (1, wide // 128)) * row_bcast(panel, j)
        panel = panel * jnp.tile(lax.rsqrt(scale), (1, wide // 128))
        work_ref[at : at + NB, :] = panel
        if at + NB < size:
            hi, mid, lo = split3(panel)
            zero = jnp.zeros((NB, size), BF16)
            keep = lane[:, :size] >= at + NB
            lhi, lmid, llo = [jnp.where(keep, term[:, :size], zero) for term in (hi, mid, lo)]
            left = jnp.concatenate([lhi, lhi, lmid, lhi, llo, lmid], axis=0)
            right = jnp.concatenate([hi, mid, hi, lo, hi, mid], axis=0)
            change = dot_tn(left, right)
            rest = size - at - NB
            wide_lane = lax.broadcasted_iota(jnp.int32, (rest, wide), 1)
            old = work_ref[at + NB :, :]
            old = jnp.where((wide_lane >= at) & (wide_lane < at + NB), 0.0, old)
            work_ref[at + NB :, :] = old - change[at + NB :, :]

    lower_inv = jnp.where(
        lax.broadcasted_iota(jnp.int32, (size, size), 0)
        >= lax.broadcasted_iota(jnp.int32, (size, size), 1),
        work_ref[:, :size],
        0.0,
    )
    half = work_ref[:, size : size + 1]
    check = work_ref[:, size + 1 : size + 2]
    direction = jnp.sum(lower_inv * half, axis=0, keepdims=True)
    diagonal = eye.astype(F32)
    check_ref[...] = jnp.sum(diagonal * check, axis=0, keepdims=True)
    dir_ref[...] = direction
    energy = jnp.sum(half * half, axis=0, keepdims=True)

    dhi, dmid, dlo = split3(direction)
    rows = jnp.concatenate([dhi, dmid, dlo, jnp.zeros((13, size), BF16)], axis=0)
    for part in range(height // 256):
        total = jnp.zeros((16, 256), F32)
        for term in split3(slab_ref[part * 256 : (part + 1) * 256, :]):
            total = total + dot_nt(rows, term)
        image = jnp.sum(total, axis=0, keepdims=True)
        image_ref[:, part * 256 : (part + 1) * 256] = jnp.broadcast_to(image, (8, 256))
    image_ref[:, height:] = jnp.broadcast_to(energy, (8, 128))


def factor(grams, back, seeds, design):
    height, breadth = design.shape
    vmem = pl.BlockSpec(memory_space=pltpu.VMEM)
    return pl.pallas_call(
        factor_kernel,
        out_shape=(
            jax.ShapeDtypeStruct((8, height + 128), F32),
            jax.ShapeDtypeStruct((1, breadth), F32),
            jax.ShapeDtypeStruct((1, breadth), F32),
        ),
        in_specs=[vmem] * 4,
        out_specs=(vmem, vmem, vmem),
        scratch_shapes=[pltpu.VMEM((breadth, breadth + 128), F32)],
        compiler_params=pltpu.CompilerParams(vmem_limit_bytes=40 * 2**20),
        name="factor",
    )(grams, back, seeds, design)


def body(design, rademacher, target, sample_rows, checksum_seeds):
    highest = lax.Precision.HIGHEST
    height, breadth = design.shape
    position = lax.axis_index(ROWS).astype(jnp.int32).reshape(1)
    picks = share(sample_rows.reshape(16), "y", Y).reshape(Y * 16)
    picks = share(picks, "z", Z).reshape(Z * Y * 16, 1)
    parts = sketch(
        position, picks, rademacher.reshape(1, height), target.reshape(1, height), design
    )
    mine = jnp.sum(exchange(parts, "y"), axis=0)
    pieces = jnp.concatenate(
        [mine[:256].reshape(Z, 16, breadth), jnp.broadcast_to(mine[None, 256:], (Z, 8, breadth))],
        axis=1,
    )
    mine = jnp.sum(exchange(pieces, "z"), axis=0)
    rows = lax.all_gather(mine[:16], "z", axis=0, tiled=True)
    gram = jnp.dot(rows.T, rows, precision=highest, preferred_element_type=F32)
    grams = share(gram, "y", Y)
    images, direction, checksum = factor(
        grams, mine[16:17], checksum_seeds.reshape(1, breadth), design
    )
    packed = jnp.sum(exchange(images, GRPS), axis=0)
    image = packed[:height]
    numer = packed[height]
    near = lax.psum(jnp.sum(image * image), "y")
    denom = jnp.sum(share(jnp.broadcast_to(near, (1, 128)), "z", Z), axis=(0, 1))[0]
    step = numer / denom
    return (
        step * direction.reshape(breadth),
        target - step * image,
        checksum.reshape(breadth),
    )


def solution(mesh):
    fine = Mesh(mesh.devices.reshape(Z, Y, X, C), ROWS + GRPS)
    in_specs = (P(ROWS, GRPS), P(ROWS), P(ROWS), P(ROWS, GRPS, None), P(GRPS))
    out_specs = (P(GRPS), P(ROWS), P(GRPS))
    return jax.shard_map(body, mesh=fine, in_specs=in_specs, out_specs=out_specs, check_vma=False)
```

```python
import jax
import jax.numpy as jnp
from jax import lax
from jax.experimental import pallas as pl
from jax.experimental.pallas import tpu as pltpu
from jax.sharding import Mesh, PartitionSpec as P

Z, Y, X, C = 16, 4, 4, 2
ROWS = ("z", "y")
GRPS = ("x", "c")
F32 = jnp.float32
BF16 = jnp.bfloat16


def parity_sign(bits):
    bits = jnp.bitwise_xor(bits, jnp.right_shift(bits, 8))
    bits = jnp.bitwise_xor(bits, jnp.right_shift(bits, 4))
    odd = jnp.bitwise_and(jnp.right_shift(0x6996, jnp.bitwise_and(bits, 15)), 1)
    return 1.0 - 2.0 * odd.astype(F32)


def split3(value):
    hi = value.astype(BF16)
    rest = value - hi.astype(F32)
    mid = rest.astype(BF16)
    lo = (rest - mid.astype(F32)).astype(BF16)
    return hi, mid, lo


def sketch_kernel(pos_ref, idx_ref, rad_ref, tgt_ref, slab_ref, *refs):
    out_refs, (sgn_ref, x_ref) = refs[:Y], refs[Y:]
    count = idx_ref.shape[0]
    height, breadth = slab_ref.shape
    hi, mid, lo = split3(slab_ref[...])
    x_ref[0] = hi
    x_ref[1] = mid
    x_ref[2] = lo
    picks = jnp.broadcast_to(idx_ref[...], (count, 128))
    lane = lax.broadcasted_iota(jnp.int32, (count, 128), 1)
    slot = lax.broadcasted_iota(jnp.int32, (count, 128), 0)
    place = jnp.right_shift(slot, 4)
    origin = jnp.bitwise_or(
        jnp.bitwise_or(
            jnp.left_shift(jnp.bitwise_and(place, 3), 4), jnp.bitwise_and(place, 12)
        ),
        jnp.right_shift(place, 4),
    )
    origin = jnp.bitwise_xor(origin, pos_ref[0])
    far = parity_sign(jnp.bitwise_and(origin, pos_ref[0]))
    base = parity_sign(jnp.bitwise_and(picks, lane)) * far * 0.03125
    base = base.astype(BF16)
    flips = [
        (1.0 - 2.0 * jnp.bitwise_and(jnp.right_shift(picks, 7 + b), 1).astype(F32)).astype(BF16)
        for b in range(4)
    ]
    row_sign = (1.0 - 2.0 * rad_ref[...].astype(F32)).astype(BF16)
    gray = 0
    current = base
    for step in range(height // 128):
        new = step ^ (step >> 1)
        if step:
            current = current * flips[(new ^ gray).bit_length() - 1]
        gray = new
        sgn_ref[0:count, gray * 128 : (gray + 1) * 128] = (
            current * row_sign[:, gray * 128 : (gray + 1) * 128]
        )
    thi, tmid, tlo = split3(tgt_ref[...])
    sgn_ref[count : count + 16, :] = jnp.concatenate(
        [thi, tmid, tlo, jnp.zeros((13, height), BF16)], axis=0
    )

    def product(rows):
        total = jnp.dot(rows, x_ref[0], preferred_element_type=F32)
        total += jnp.dot(rows, x_ref[1], preferred_element_type=F32)
        return total + jnp.dot(rows, x_ref[2], preferred_element_type=F32)

    back = jnp.sum(product(sgn_ref[count : count + 16, :]), axis=0, keepdims=True)
    for part, out_ref in enumerate(out_refs):
        out_ref[0:256, :] = product(sgn_ref[part * 256 : (part + 1) * 256, :])
        out_ref[256:264, :] = jnp.broadcast_to(back, (8, breadth))


def sketch(position, picks, rademacher, target, design):
    height, breadth = design.shape
    vmem = pl.BlockSpec(memory_space=pltpu.VMEM)
    return pl.pallas_call(
        sketch_kernel,
        out_shape=[jax.ShapeDtypeStruct((264, breadth), F32)] * Y,
        in_specs=[pl.BlockSpec(memory_space=pltpu.SMEM), vmem, vmem, vmem, vmem],
        out_specs=[vmem] * Y,
        scratch_shapes=[
            pltpu.VMEM((1024 + 16, height), BF16),
            pltpu.VMEM((3, height, breadth), BF16),
        ],
        compiler_params=pltpu.CompilerParams(vmem_limit_bytes=40 * 2**20),
        name="sketch",
    )(position, picks, rademacher, target, design)


def exchange(pieces, axes):
    return lax.all_to_all(pieces, axes, split_axis=0, concat_axis=0, tiled=True)


def swap(value, axis, mask):
    pairs = [(source, source ^ mask) for source in range(lax.axis_size(axis))]
    return lax.ppermute(value, axis, pairs)


def fan(pieces, axis, stride):
    return [pieces[0]] + [swap(pieces[j], axis, j * stride) for j in range(1, 4)]


def total(pieces):
    return (pieces[0] + pieces[1]) + (pieces[2] + pieces[3])


NB = 16


def row_bcast(value, row):
    return jnp.broadcast_to(value[row : row + 1, :], value.shape)


def dot_nt(left, right):
    return lax.dot_general(left, right, (((1,), (1,)), ((), ())), preferred_element_type=F32)


def dot_tn(left, right):
    return lax.dot_general(left, right, (((0,), (0,)), ((), ())), preferred_element_type=F32)


def gram_kernel(row0, row1, row2, row3, out_ref):
    rows = jnp.concatenate([row0[...], row1[...], row2[...], row3[...]], axis=0)
    hi, mid, lo = split3(rows)
    left = jnp.concatenate([hi, hi, mid, hi, lo, mid], axis=0)
    right = jnp.concatenate([hi, mid, hi, lo, hi, mid], axis=0)
    out_ref[0:128, :] = dot_tn(left[:, :128], right[:, :128])
    out_ref[128:256, :] = dot_tn(left[:, :128], right[:, 128:])
    out_ref[256:384, :] = dot_tn(left[:, 128:], right[:, 128:])


def gram_blocks(rows):
    vmem = pl.BlockSpec(memory_space=pltpu.VMEM)
    return pl.pallas_call(
        gram_kernel,
        out_shape=jax.ShapeDtypeStruct((384, 128), F32),
        in_specs=[vmem] * 4,
        out_specs=vmem,
        name="gram",
    )(*rows)


def factor_kernel(
    gram0, gram1, gram2, gram3, back_ref, seed_ref, slab_ref, image_ref, dir_ref, check_ref, work_ref
):
    size = slab_ref.shape[1]
    height = slab_ref.shape[0]
    blocks = (gram0[...] + gram1[...]) + (gram2[...] + gram3[...])
    corner = blocks[128:256]
    gram = jnp.concatenate(
        [
            jnp.concatenate([blocks[0:128], corner], axis=1),
            jnp.concatenate([corner.T, blocks[256:384]], axis=1),
        ],
        axis=0,
    )
    sub = lax.broadcasted_iota(jnp.int32, (128, size), 0)
    weights = seed_ref[...].astype(F32) * 0.0625
    weight_rows = jnp.where(sub == 1, jnp.broadcast_to(weights, (128, size)), 0.0).astype(BF16)
    back_rows = jnp.where(sub == 0, jnp.broadcast_to(back_ref[...], (128, size)), 0.0)
    eye = (
        lax.broadcasted_iota(jnp.int32, (size, size), 0)
        == lax.broadcasted_iota(jnp.int32, (size, size), 1)
    ).astype(BF16)
    extra = jnp.zeros((size, 128), F32)
    for term in split3(gram):
        extra = extra + dot_nt(term, weight_rows)
    for term in split3(back_rows):
        extra = extra + dot_nt(eye, term)
    work_ref[:, :size] = gram
    work_ref[:, size:] = extra

    wide = size + 128
    lane = lax.broadcasted_iota(jnp.int32, (NB, wide), 1)
    row = lax.broadcasted_iota(jnp.int32, (NB, wide), 0)
    small_row = lax.broadcasted_iota(jnp.int32, (NB, 128), 0)
    for block in range(size // NB):
        at = block * NB
        panel = work_ref[at : at + NB, :]
        cols = [jnp.broadcast_to(panel[:, at + j : at + j + 1], (NB, 128)) for j in range(NB)]
        panel = jnp.where((lane >= at) & (lane < at + NB), (lane - at == row).astype(F32), panel)
        scale = jnp.zeros((NB, 128), F32)
        for j in range(NB):
            pivot = row_bcast(cols[j], j)
            coef = jnp.where(small_row > j, cols[j] / pivot, 0.0)
            scale = jnp.where(small_row == j, pivot, scale)
            for later in range(j + 1, NB):
                cols[later] = cols[later] - coef * row_bcast(cols[later], j)
            panel = panel - jnp.tile(coef, (1, wide // 128)) * row_bcast(panel, j)
        panel = panel * jnp.tile(lax.rsqrt(scale), (1, wide // 128))
        work_ref[at : at + NB, :] = panel
        if at + NB < size:
            hi, mid, lo = split3(panel)
            zero = jnp.zeros((NB, size), BF16)
            keep = lane[:, :size] >= at + NB
            lhi, lmid, llo = [jnp.where(keep, term[:, :size], zero) for term in (hi, mid, lo)]
            left = jnp.concatenate([lhi, lhi, lmid, lhi, llo, lmid], axis=0)
            right = jnp.concatenate([hi, mid, hi, lo, hi, mid], axis=0)
            change = dot_tn(left, right)
            rest = size - at - NB
            wide_lane = lax.broadcasted_iota(jnp.int32, (rest, wide), 1)
            old = work_ref[at + NB :, :]
            old = jnp.where((wide_lane >= at) & (wide_lane < at + NB), 0.0, old)
            work_ref[at + NB :, :] = old - change[at + NB :, :]

    lower_inv = jnp.where(
        lax.broadcasted_iota(jnp.int32, (size, size), 0)
        >= lax.broadcasted_iota(jnp.int32, (size, size), 1),
        work_ref[:, :size],
        0.0,
    )
    half = work_ref[:, size : size + 1]
    check = work_ref[:, size + 1 : size + 2]
    direction = jnp.sum(lower_inv * half, axis=0, keepdims=True)
    diagonal = eye.astype(F32)
    check_ref[...] = jnp.sum(diagonal * check, axis=0, keepdims=True)
    dir_ref[...] = direction
    energy = jnp.sum(half * half, axis=0, keepdims=True)

    dhi, dmid, dlo = split3(direction)
    rows = jnp.concatenate([dhi, dmid, dlo, jnp.zeros((13, size), BF16)], axis=0)
    for part in range(height // 256):
        total = jnp.zeros((16, 256), F32)
        for term in split3(slab_ref[part * 256 : (part + 1) * 256, :]):
            total = total + dot_nt(rows, term)
        image = jnp.sum(total, axis=0, keepdims=True)
        image_ref[:, part * 256 : (part + 1) * 256] = jnp.broadcast_to(image, (8, 256))
    image_ref[:, height:] = jnp.broadcast_to(energy, (8, 128))


def factor(grams, back, seeds, design):
    height, breadth = design.shape
    vmem = pl.BlockSpec(memory_space=pltpu.VMEM)
    return pl.pallas_call(
        factor_kernel,
        out_shape=(
            jax.ShapeDtypeStruct((8, height + 128), F32),
            jax.ShapeDtypeStruct((1, breadth), F32),
            jax.ShapeDtypeStruct((1, breadth), F32),
        ),
        in_specs=[vmem] * 7,
        out_specs=(vmem, vmem, vmem),
        scratch_shapes=[pltpu.VMEM((breadth, breadth + 128), F32)],
        compiler_params=pltpu.CompilerParams(vmem_limit_bytes=40 * 2**20),
        name="factor",
    )(*grams, back, seeds, design)


def body(design, rademacher, target, sample_rows, checksum_seeds):
    height, breadth = design.shape
    position = lax.axis_index(ROWS).astype(jnp.int32).reshape(1)
    picks = sample_rows.reshape(1, 16)
    for axis, mask in (("z", 4), ("z", 8), ("z", 1), ("z", 2), ("y", 1), ("y", 2)):
        picks = jnp.concatenate([picks, swap(picks, axis, mask)], axis=0)
    parts = sketch(
        position,
        picks.reshape(Z * Y * 16, 1),
        rademacher.reshape(1, height),
        target.reshape(1, height),
        design,
    )
    mine = total(fan(parts, "y", 1))
    pieces = [jnp.concatenate([mine[64 * j : 64 * j + 64], mine[256:]]) for j in range(4)]
    mine = total(fan(pieces, "z", 1))
    pieces = [jnp.concatenate([mine[16 * j : 16 * j + 16], mine[64:]]) for j in range(4)]
    mine = total(fan(pieces, "z", 4))
    rows = jnp.concatenate(fan([mine[:16]] * 4, "z", 4))
    blocks = gram_blocks(fan([rows] * 4, "z", 1))
    images, direction, checksum = factor(
        fan([blocks] * 4, "y", 1), mine[16:17], checksum_seeds.reshape(1, breadth), design
    )
    packed = jnp.sum(exchange(images, GRPS), axis=0)
    image = packed[:height]
    numer = packed[height]
    denom = jnp.broadcast_to(jnp.sum(image * image), (1, 128))
    for axis, stride in (("y", 1), ("z", 1), ("z", 4)):
        denom = total(fan([denom] * 4, axis, stride))
    step = numer / denom[0, 0]
    return (
        step * direction.reshape(breadth),
        target - step * image,
        checksum.reshape(breadth),
    )


def solution(mesh):
    fine = Mesh(mesh.devices.reshape(Z, Y, X, C), ROWS + GRPS)
    in_specs = (P(ROWS, GRPS), P(ROWS), P(ROWS), P(ROWS, GRPS, None), P(GRPS))
    out_specs = (P(GRPS), P(ROWS), P(GRPS))
    return jax.shard_map(body, mesh=fine, in_specs=in_specs, out_specs=out_specs, check_vma=False)
```

```python
import functools

import jax
import jax.numpy as jnp
from jax import lax
from jax.experimental import pallas as pl
from jax.experimental.pallas import tpu as pltpu
from jax.sharding import Mesh, PartitionSpec as P

Z, Y, X, C = 16, 4, 4, 2
ROWS = ("z", "y")
GRPS = ("x", "c")
F32 = jnp.float32
BF16 = jnp.bfloat16
VMEM = pl.BlockSpec(memory_space=pltpu.VMEM)
SMEM = pl.BlockSpec(memory_space=pltpu.SMEM)


def cost(flops, size):
    return pl.CostEstimate(flops=flops, bytes_accessed=size, transcendentals=0)


def parity_sign(bits):
    bits = jnp.bitwise_xor(bits, jnp.right_shift(bits, 8))
    bits = jnp.bitwise_xor(bits, jnp.right_shift(bits, 4))
    odd = jnp.bitwise_and(jnp.right_shift(0x6996, jnp.bitwise_and(bits, 15)), 1)
    return 1.0 - 2.0 * odd.astype(F32)


def split3(value):
    hi = value.astype(BF16)
    rest = value - hi.astype(F32)
    mid = rest.astype(BF16)
    lo = (rest - mid.astype(F32)).astype(BF16)
    return hi, mid, lo


def prepare_kernel(tgt_ref, slab_ref, terms_ref, back_ref):
    height, breadth = slab_ref.shape
    rows = jnp.concatenate(list(split3(tgt_ref[...])) + [jnp.zeros((13, height), BF16)], axis=0)
    total = jnp.zeros((16, breadth), F32)
    for place, term in enumerate(split3(slab_ref[...])):
        terms_ref[place] = term
        total = total + jnp.dot(rows, term, preferred_element_type=F32)
    back_ref[...] = jnp.broadcast_to(jnp.sum(total, axis=0, keepdims=True), (8, breadth))


def prepare(target, design):
    height, breadth = design.shape
    return pl.pallas_call(
        prepare_kernel,
        out_shape=(
            jax.ShapeDtypeStruct((3, height, breadth), BF16),
            jax.ShapeDtypeStruct((8, breadth), F32),
        ),
        in_specs=[VMEM] * 2,
        out_specs=(VMEM,) * 2,
        compiler_params=pltpu.CompilerParams(vmem_limit_bytes=40 * 2**20),
        cost_estimate=cost(2**28, 2**23),
        name="prepare",
    )(target, design)


def sketch_kernel(part, pos_ref, idx_ref, rad_ref, terms_ref, *refs):
    out_ref, sgn_ref = refs[-2:]
    _, height, breadth = terms_ref.shape
    sources = Z * Y
    count = 512
    slot = lax.broadcasted_iota(jnp.int32, (count, 128), 0)
    lane = lax.broadcasted_iota(jnp.int32, (count, 128), 1)
    sample = jnp.left_shift(jnp.right_shift(slot, 7), 8) + part * 128 + jnp.bitwise_and(slot, 127)
    owner = jnp.right_shift(sample, 4)
    expand = (owner[:, :sources] == lane[:, :sources]).astype(BF16)
    mine = lane == jnp.bitwise_and(sample, 15)
    ones = jnp.ones((128, 128), BF16)
    drawn = idx_ref[...].reshape(sources, 128)
    picks = jnp.zeros((count, 128), jnp.int32)
    for piece, scale in ((jnp.right_shift(drawn, 7), 128), (jnp.bitwise_and(drawn, 127), 1)):
        spread = jnp.dot(expand, piece.astype(F32).astype(BF16), preferred_element_type=F32)
        spread = jnp.where(mine, spread, 0.0).astype(BF16)
        spread = jnp.dot(spread, ones, preferred_element_type=F32)
        picks = picks + spread.astype(jnp.int32) * scale
    far = parity_sign(jnp.bitwise_and(owner, pos_ref[0]))
    base = parity_sign(jnp.bitwise_and(jnp.bitwise_and(picks, lane), 127)) * far * 0.03125
    base = base.astype(BF16)
    flips = [
        (1.0 - 2.0 * jnp.bitwise_and(jnp.right_shift(picks, 7 + b), 1).astype(F32)).astype(BF16)
        for b in range(4)
    ]
    row_sign = (1.0 - 2.0 * rad_ref[...].astype(F32)).astype(BF16)
    gray = 0
    current = base
    for step in range(height // 128):
        new = step ^ (step >> 1)
        if step:
            current = current * flips[(new ^ gray).bit_length() - 1]
        gray = new
        sgn_ref[:, gray * 128 : (gray + 1) * 128] = (
            current * row_sign[:, gray * 128 : (gray + 1) * 128]
        )
    for piece in range(Y):
        rows = sgn_ref[piece * 128 : (piece + 1) * 128, :]
        total = jnp.dot(rows, terms_ref[0], preferred_element_type=F32)
        total += jnp.dot(rows, terms_ref[1], preferred_element_type=F32)
        total += jnp.dot(rows, terms_ref[2], preferred_element_type=F32)
        out_ref[piece, 0:128, :] = total
        if part == 0:
            out_ref[piece, 128:136, :] = refs[0][...]


def sketch(part, position, drawn, rademacher, terms, *back):
    _, height, breadth = terms.shape
    return pl.pallas_call(
        functools.partial(sketch_kernel, part),
        out_shape=jax.ShapeDtypeStruct((Y, 136 if part == 0 else 128, breadth), F32),
        in_specs=[SMEM] + [VMEM] * (3 + len(back)),
        out_specs=VMEM,
        scratch_shapes=[pltpu.VMEM((512, height), BF16)],
        compiler_params=pltpu.CompilerParams(vmem_limit_bytes=40 * 2**20),
        cost_estimate=cost(2**31, 2**22),
        name="sketch",
    )(position, drawn, rademacher, terms, *back)


def exchange(pieces, axes):
    return lax.all_to_all(pieces, axes, split_axis=0, concat_axis=0, tiled=True)


def share(value, axes, count):
    return exchange(jnp.broadcast_to(value[None], (count,) + value.shape), axes)


NB = 16


def row_bcast(value, row):
    return jnp.broadcast_to(value[row : row + 1, :], value.shape)


def dot_nt(left, right):
    return lax.dot_general(left, right, (((1,), (1,)), ((), ())), preferred_element_type=F32)


def dot_tn(left, right):
    return lax.dot_general(left, right, (((0,), (0,)), ((), ())), preferred_element_type=F32)


def gram_products(rows):
    hi, mid, lo = split3(rows)
    left = jnp.concatenate([hi, hi, mid, hi, lo, mid], axis=0)
    right = jnp.concatenate([hi, mid, hi, lo, hi, mid], axis=0)
    return (
        dot_tn(left[:, :128], right[:, :128]),
        dot_tn(left[:, :128], right[:, 128:]),
        dot_tn(left[:, 128:], right[:, 128:]),
    )


def gram_first_kernel(rows_ref, out_ref):
    for place, block in enumerate(gram_products(rows_ref[...])):
        out_ref[place * 128 : (place + 1) * 128, :] = block


def gram_last_kernel(rows_ref, old_ref, out_ref):
    for place, block in enumerate(gram_products(rows_ref[...])):
        block = block + old_ref[place * 128 : (place + 1) * 128, :]
        for copy in range(Y):
            out_ref[copy, place * 128 : (place + 1) * 128, :] = block


def gram_first(rows):
    return pl.pallas_call(
        gram_first_kernel,
        out_shape=jax.ShapeDtypeStruct((384, 128), F32),
        in_specs=[VMEM],
        out_specs=VMEM,
        cost_estimate=cost(2**27, 2**18),
        name="gram_first",
    )(rows)


def gram_last(rows, old):
    return pl.pallas_call(
        gram_last_kernel,
        out_shape=jax.ShapeDtypeStruct((Y, 384, 128), F32),
        in_specs=[VMEM] * 2,
        out_specs=VMEM,
        cost_estimate=cost(2**27, 2**20),
        name="gram_last",
    )(rows, old)


def factor_kernel(gram_ref, back_ref, seed_ref, slab_ref, image_ref, dir_ref, check_ref, work_ref):
    height, size = slab_ref.shape
    blocks = (gram_ref[0] + gram_ref[1]) + (gram_ref[2] + gram_ref[3])
    corner = blocks[128:256]
    gram = jnp.concatenate(
        [
            jnp.concatenate([blocks[0:128], corner], axis=1),
            jnp.concatenate([corner.T, blocks[256:384]], axis=1),
        ],
        axis=0,
    )
    sub = lax.broadcasted_iota(jnp.int32, (128, size), 0)
    weights = seed_ref[...].astype(F32) * 0.0625
    weight_rows = jnp.where(sub == 1, jnp.broadcast_to(weights, (128, size)), 0.0).astype(BF16)
    back_rows = jnp.where(sub == 0, jnp.broadcast_to(back_ref[...], (128, size)), 0.0)
    eye = (
        lax.broadcasted_iota(jnp.int32, (size, size), 0)
        == lax.broadcasted_iota(jnp.int32, (size, size), 1)
    ).astype(BF16)
    extra = jnp.zeros((size, 128), F32)
    for term in split3(gram):
        extra = extra + dot_nt(term, weight_rows)
    for term in split3(back_rows):
        extra = extra + dot_nt(eye, term)
    work_ref[:, :size] = gram
    work_ref[:, size:] = extra

    wide = size + 128
    lane = lax.broadcasted_iota(jnp.int32, (NB, wide), 1)
    row = lax.broadcasted_iota(jnp.int32, (NB, wide), 0)
    small_row = lax.broadcasted_iota(jnp.int32, (NB, 128), 0)
    for block in range(size // NB):
        at = block * NB
        panel = work_ref[at : at + NB, :]
        cols = [jnp.broadcast_to(panel[:, at + j : at + j + 1], (NB, 128)) for j in range(NB)]
        panel = jnp.where((lane >= at) & (lane < at + NB), (lane - at == row).astype(F32), panel)
        scale = jnp.zeros((NB, 128), F32)
        for j in range(NB):
            pivot = row_bcast(cols[j], j)
            coef = jnp.where(small_row > j, cols[j] / pivot, 0.0)
            scale = jnp.where(small_row == j, pivot, scale)
            for later in range(j + 1, NB):
                cols[later] = cols[later] - coef * row_bcast(cols[later], j)
            panel = panel - jnp.tile(coef, (1, wide // 128)) * row_bcast(panel, j)
        panel = panel * jnp.tile(lax.rsqrt(scale), (1, wide // 128))
        work_ref[at : at + NB, :] = panel
        if at + NB < size:
            hi, mid, lo = split3(panel)
            zero = jnp.zeros((NB, size), BF16)
            keep = lane[:, :size] >= at + NB
            lhi, lmid, llo = [jnp.where(keep, term[:, :size], zero) for term in (hi, mid, lo)]
            left = jnp.concatenate([lhi, lhi, lmid, lhi, llo, lmid], axis=0)
            right = jnp.concatenate([hi, mid, hi, lo, hi, mid], axis=0)
            change = dot_tn(left, right)
            rest = size - at - NB
            wide_lane = lax.broadcasted_iota(jnp.int32, (rest, wide), 1)
            old = work_ref[at + NB :, :]
            old = jnp.where((wide_lane >= at) & (wide_lane < at + NB), 0.0, old)
            work_ref[at + NB :, :] = old - change[at + NB :, :]

    lower_inv = jnp.where(
        lax.broadcasted_iota(jnp.int32, (size, size), 0)
        >= lax.broadcasted_iota(jnp.int32, (size, size), 1),
        work_ref[:, :size],
        0.0,
    )
    half = work_ref[:, size : size + 1]
    check = work_ref[:, size + 1 : size + 2]
    direction = jnp.sum(lower_inv * half, axis=0, keepdims=True)
    diagonal = eye.astype(F32)
    check_ref[...] = jnp.sum(diagonal * check, axis=0, keepdims=True)
    dir_ref[...] = direction
    energy = jnp.sum(half * half, axis=0, keepdims=True)

    dhi, dmid, dlo = split3(direction)
    rows = jnp.concatenate([dhi, dmid, dlo, jnp.zeros((13, size), BF16)], axis=0)
    for part in range(height // 256):
        total = jnp.zeros((16, 256), F32)
        for term in split3(slab_ref[part * 256 : (part + 1) * 256, :]):
            total = total + dot_nt(rows, term)
        image = jnp.sum(total, axis=0, keepdims=True)
        image_ref[:, part * 256 : (part + 1) * 256] = jnp.broadcast_to(image, (8, 256))
    image_ref[:, height:] = jnp.broadcast_to(energy, (8, 128))


def factor(grams, back, seeds, design):
    height, breadth = design.shape
    return pl.pallas_call(
        factor_kernel,
        out_shape=(
            jax.ShapeDtypeStruct((8, height + 128), F32),
            jax.ShapeDtypeStruct((1, breadth), F32),
            jax.ShapeDtypeStruct((1, breadth), F32),
        ),
        in_specs=[VMEM] * 4,
        out_specs=(VMEM,) * 3,
        scratch_shapes=[pltpu.VMEM((breadth, breadth + 128), F32)],
        compiler_params=pltpu.CompilerParams(vmem_limit_bytes=40 * 2**20),
        cost_estimate=cost(2**29, 2**22),
        name="factor",
    )(grams, back, seeds, design)


def merge_kernel(parts_ref, image_ref, energy_ref):
    width = parts_ref.shape[2]
    image = jnp.sum(parts_ref[...], axis=0)
    image_ref[...] = image
    body = image[:, : width - 128]
    energy = jnp.sum(body * body, axis=1, keepdims=True)
    energy_ref[...] = jnp.broadcast_to(energy.reshape(1, 1, 1), energy_ref.shape)


def merge(parts):
    width = parts.shape[2]
    return pl.pallas_call(
        merge_kernel,
        out_shape=(
            jax.ShapeDtypeStruct((1, width), F32),
            jax.ShapeDtypeStruct((Z * Y, 1, 128), F32),
        ),
        in_specs=[VMEM],
        out_specs=(VMEM,) * 2,
        name="merge",
    )(parts)


def finish_kernel(energy_ref, image_ref, tgt_ref, dir_ref, sol_ref, res_ref):
    height = tgt_ref.shape[1]
    step = image_ref[:, height:] / jnp.sum(energy_ref[...], axis=0)
    sol_ref[...] = jnp.tile(step, (1, dir_ref.shape[1] // 128)) * dir_ref[...]
    res_ref[...] = tgt_ref[...] - jnp.tile(step, (1, height // 128)) * image_ref[:, :height]


def finish(energies, image, target, direction):
    return pl.pallas_call(
        finish_kernel,
        out_shape=(
            jax.ShapeDtypeStruct(direction.shape, F32),
            jax.ShapeDtypeStruct(target.shape, F32),
        ),
        in_specs=[VMEM] * 4,
        out_specs=(VMEM,) * 2,
        name="finish",
    )(energies, image, target, direction)


def body(design, rademacher, target, sample_rows, checksum_seeds):
    height, breadth = design.shape
    position = lax.axis_index(ROWS).astype(jnp.int32).reshape(1)
    rademacher = rademacher.reshape(1, height)
    target = target.reshape(1, height)
    drawn = jnp.pad(sample_rows.reshape(1, 16), ((0, 0), (0, 112)))
    drawn = share(drawn, ROWS, Z * Y)
    terms, back = prepare(target, design)
    halves = [
        sketch(0, position, drawn, rademacher, terms, back),
        sketch(1, position, drawn, rademacher, terms),
    ]
    halves = [jnp.sum(exchange(half, "y"), axis=0) for half in halves]
    first = jnp.concatenate(
        [
            halves[0][:128].reshape(Z, 8, breadth),
            jnp.broadcast_to(halves[0][None, 128:], (Z, 8, breadth)),
        ],
        axis=1,
    )
    halves = [first, halves[1].reshape(Z, 8, breadth)]
    halves = [jnp.sum(exchange(half, "z"), axis=0) for half in halves]
    rows = [share(half[:8], "z", Z).reshape(Z * 8, breadth) for half in halves]
    grams = exchange(gram_last(rows[1], gram_first(rows[0])), "y")
    images, direction, checksum = factor(
        grams, halves[0][8:9], checksum_seeds.reshape(1, breadth), design
    )
    image, energy = merge(exchange(images.reshape(X * C, 1, height + 128), GRPS))
    solved, residual = finish(exchange(energy, ROWS), image, target, direction)
    return solved.reshape(breadth), residual.reshape(height), checksum.reshape(breadth)


def solution(mesh):
    fine = Mesh(mesh.devices.reshape(Z, Y, X, C), ROWS + GRPS)
    in_specs = (P(ROWS, GRPS), P(ROWS), P(ROWS), P(ROWS, GRPS, None), P(GRPS))
    out_specs = (P(GRPS), P(ROWS), P(GRPS))
    return jax.shard_map(body, mesh=fine, in_specs=in_specs, out_specs=out_specs, check_vma=False)
```

```python
import functools

import jax
import jax.numpy as jnp
from jax import lax
from jax.experimental import pallas as pl
from jax.experimental.pallas import tpu as pltpu
from jax.sharding import Mesh, PartitionSpec as P

ZB, ZA, Y, X, C = 8, 2, 4, 4, 2
SOURCES = ZB * ZA * Y
FAR = "zb"
NEAR = ("za", "y")
ROWS = (FAR,) + NEAR
GRPS = ("x", "c")
F32 = jnp.float32
BF16 = jnp.bfloat16
VMEM = pl.BlockSpec(memory_space=pltpu.VMEM)
SMEM = pl.BlockSpec(memory_space=pltpu.SMEM)


def cost(flops, size):
    return pl.CostEstimate(flops=flops, bytes_accessed=size, transcendentals=0)


def parity_sign(bits):
    bits = jnp.bitwise_xor(bits, jnp.right_shift(bits, 8))
    bits = jnp.bitwise_xor(bits, jnp.right_shift(bits, 4))
    odd = jnp.bitwise_and(jnp.right_shift(0x6996, jnp.bitwise_and(bits, 15)), 1)
    return 1.0 - 2.0 * odd.astype(F32)


def split3(value):
    hi = value.astype(BF16)
    rest = value - hi.astype(F32)
    mid = rest.astype(BF16)
    lo = (rest - mid.astype(F32)).astype(BF16)
    return hi, mid, lo


def prepare_kernel(tgt_ref, rad_ref, slab_ref, terms_ref, back_ref, sign_ref):
    height, breadth = slab_ref.shape
    rows = jnp.concatenate(list(split3(tgt_ref[...])) + [jnp.zeros((13, height), BF16)], axis=0)
    total = jnp.zeros((16, breadth), F32)
    for place, term in enumerate(split3(slab_ref[...])):
        terms_ref[place] = term
        total = total + jnp.dot(rows, term, preferred_element_type=F32)
    back_ref[...] = jnp.broadcast_to(jnp.sum(total, axis=0, keepdims=True), (8, breadth))
    sign_ref[...] = 1.0 - 2.0 * rad_ref[...].astype(F32)


def prepare(target, rademacher, design):
    height, breadth = design.shape
    return pl.pallas_call(
        prepare_kernel,
        out_shape=(
            jax.ShapeDtypeStruct((3, height, breadth), BF16),
            jax.ShapeDtypeStruct((8, breadth), F32),
            jax.ShapeDtypeStruct((1, height), F32),
        ),
        in_specs=[VMEM] * 3,
        out_specs=(VMEM,) * 3,
        compiler_params=pltpu.CompilerParams(vmem_limit_bytes=40 * 2**20),
        cost_estimate=cost(2**28, 2**23),
        name="prepare",
    )(target, rademacher, design)


def sketch_kernel(pos_ref, idx_ref, sign_ref, terms_ref, back_ref, out_ref, sgn_ref):
    _, height, breadth = terms_ref.shape
    per_owner = idx_ref.shape[2]
    count = SOURCES * per_owner
    sample = lax.broadcasted_iota(jnp.int32, (count, 128), 0)
    lane = lax.broadcasted_iota(jnp.int32, (count, 128), 1)
    owner = jnp.right_shift(sample, 4)
    expand = (owner[:, :SOURCES] == lane[:, :SOURCES]).astype(BF16)
    mine = (lane == jnp.bitwise_and(sample, 15))[:, :per_owner]
    ones = jnp.ones((per_owner, 128), BF16)
    drawn = idx_ref[...].reshape(SOURCES, per_owner)
    picks = jnp.zeros((count, 128), jnp.int32)
    for piece, scale in ((jnp.right_shift(drawn, 7), 128), (jnp.bitwise_and(drawn, 127), 1)):
        spread = jnp.dot(expand, piece.astype(F32).astype(BF16), preferred_element_type=F32)
        spread = jnp.where(mine, spread, 0.0).astype(BF16)
        spread = jnp.dot(spread, ones, preferred_element_type=F32)
        picks = picks + spread.astype(jnp.int32) * scale
    far = parity_sign(jnp.bitwise_and(owner, pos_ref[0]))
    base = parity_sign(jnp.bitwise_and(jnp.bitwise_and(picks, lane), 127)) * far * 0.03125
    base = base.astype(BF16)
    flips = [
        (1.0 - 2.0 * jnp.bitwise_and(jnp.right_shift(picks, 7 + b), 1).astype(F32)).astype(BF16)
        for b in range(4)
    ]
    row_sign = sign_ref[...].astype(BF16)
    gray = 0
    current = base
    for step in range(height // 128):
        new = step ^ (step >> 1)
        if step:
            current = current * flips[(new ^ gray).bit_length() - 1]
        gray = new
        sgn_ref[:, gray * 128 : (gray + 1) * 128] = (
            current * row_sign[:, gray * 128 : (gray + 1) * 128]
        )
    for piece in range(ZA * Y):
        if piece % 2 == 0:
            rows = sgn_ref[piece * 128 : (piece + 2) * 128, :]
            total = jnp.dot(rows, terms_ref[0], preferred_element_type=F32)
            total += jnp.dot(rows, terms_ref[1], preferred_element_type=F32)
            total += jnp.dot(rows, terms_ref[2], preferred_element_type=F32)
        out_ref[piece, 0:128, :] = total[(piece % 2) * 128 : (piece % 2 + 1) * 128, :]
        out_ref[piece, 128:136, :] = back_ref[...]


def sketch(position, drawn, signs, terms, back):
    _, height, breadth = terms.shape
    return pl.pallas_call(
        sketch_kernel,
        out_shape=jax.ShapeDtypeStruct((ZA * Y, 136, breadth), F32),
        in_specs=[SMEM] + [VMEM] * 4,
        out_specs=VMEM,
        scratch_shapes=[pltpu.VMEM((1024, height), BF16)],
        compiler_params=pltpu.CompilerParams(vmem_limit_bytes=40 * 2**20),
        cost_estimate=cost(2**31, 2**22),
        name="sketch",
    )(position, drawn, signs, terms, back)


def exchange(pieces, axes):
    return lax.all_to_all(pieces, axes, split_axis=0, concat_axis=0, tiled=True)


def share(value, axes, count):
    return exchange(jnp.broadcast_to(value[None], (count,) + value.shape), axes)


NB = 16


def row_bcast(value, row):
    return jnp.broadcast_to(value[row : row + 1, :], value.shape)


def dot_nt(left, right):
    return lax.dot_general(left, right, (((1,), (1,)), ((), ())), preferred_element_type=F32)


def dot_tn(left, right):
    return lax.dot_general(left, right, (((0,), (0,)), ((), ())), preferred_element_type=F32)


def gram_products(rows):
    hi, mid, lo = split3(rows)
    right = jnp.concatenate([hi, mid, hi, lo, hi, mid], axis=0)
    hi, mid, lo = split3(rows.T)
    left = jnp.concatenate([hi, hi, mid, hi, lo, mid], axis=1)
    top = jnp.dot(left[:128], right, preferred_element_type=F32)
    end = jnp.dot(left[128:], right[:, 128:], preferred_element_type=F32)
    return top[:, :128], top[:, 128:], end


def gram_first_kernel(rows_ref, out_ref):
    for place, block in enumerate(gram_products(rows_ref[...])):
        out_ref[place * 128 : (place + 1) * 128, :] = block


def gram_last_kernel(rows_ref, old_ref, out_ref):
    for place, block in enumerate(gram_products(rows_ref[...])):
        block = block + old_ref[place * 128 : (place + 1) * 128, :]
        for copy in range(Y):
            out_ref[copy, place * 128 : (place + 1) * 128, :] = block


def gram_first(rows):
    return pl.pallas_call(
        gram_first_kernel,
        out_shape=jax.ShapeDtypeStruct((384, 128), F32),
        in_specs=[VMEM],
        out_specs=VMEM,
        cost_estimate=cost(2**27, 2**18),
        name="gram_first",
    )(rows)


def gram_last(rows, old):
    return pl.pallas_call(
        gram_last_kernel,
        out_shape=jax.ShapeDtypeStruct((Y, 384, 128), F32),
        in_specs=[VMEM] * 2,
        out_specs=VMEM,
        cost_estimate=cost(2**27, 2**20),
        name="gram_last",
    )(rows, old)


def factor_kernel(gram_ref, back_ref, seed_ref, slab_ref, image_ref, dir_ref, check_ref, work_ref):
    height, size = slab_ref.shape
    blocks = (gram_ref[0] + gram_ref[1]) + (gram_ref[2] + gram_ref[3])
    corner = blocks[128:256]
    gram = jnp.concatenate(
        [
            jnp.concatenate([blocks[0:128], corner], axis=1),
            jnp.concatenate([corner.T, blocks[256:384]], axis=1),
        ],
        axis=0,
    )
    sub = lax.broadcasted_iota(jnp.int32, (128, size), 0)
    weights = seed_ref[...].astype(F32) * 0.0625
    weight_rows = jnp.where(sub == 1, jnp.broadcast_to(weights, (128, size)), 0.0).astype(BF16)
    back_rows = jnp.where(sub == 0, jnp.broadcast_to(back_ref[...], (128, size)), 0.0)
    eye = (
        lax.broadcasted_iota(jnp.int32, (size, size), 0)
        == lax.broadcasted_iota(jnp.int32, (size, size), 1)
    ).astype(BF16)
    extra = jnp.zeros((size, 128), F32)
    for term in split3(gram):
        extra = extra + dot_nt(term, weight_rows)
    for term in split3(back_rows):
        extra = extra + dot_nt(eye, term)
    work_ref[:, :size] = gram
    work_ref[:, size:] = extra

    wide = size + 128
    lane = lax.broadcasted_iota(jnp.int32, (NB, wide), 1)
    row = lax.broadcasted_iota(jnp.int32, (NB, wide), 0)
    small_row = lax.broadcasted_iota(jnp.int32, (NB, 128), 0)
    for block in range(size // NB):
        at = block * NB
        panel = work_ref[at : at + NB, :]
        cols = [jnp.broadcast_to(panel[:, at + j : at + j + 1], (NB, 128)) for j in range(NB)]
        panel = jnp.where((lane >= at) & (lane < at + NB), (lane - at == row).astype(F32), panel)
        scale = jnp.zeros((NB, 128), F32)
        for j in range(NB):
            pivot = row_bcast(cols[j], j)
            coef = jnp.where(small_row > j, cols[j] / pivot, 0.0)
            scale = jnp.where(small_row == j, pivot, scale)
            for later in range(j + 1, NB):
                cols[later] = cols[later] - coef * row_bcast(cols[later], j)
            panel = panel - jnp.tile(coef, (1, wide // 128)) * row_bcast(panel, j)
        panel = panel * jnp.tile(lax.rsqrt(scale), (1, wide // 128))
        work_ref[at : at + NB, :] = panel
        if at + NB < size:
            hi, mid, lo = split3(panel)
            zero = jnp.zeros((NB, size), BF16)
            keep = lane[:, :size] >= at + NB
            lhi, lmid, llo = [jnp.where(keep, term[:, :size], zero) for term in (hi, mid, lo)]
            left = jnp.concatenate([lhi, lhi, lmid, lhi, llo, lmid], axis=0)
            right = jnp.concatenate([hi, mid, hi, lo, hi, mid], axis=0)
            change = dot_tn(left, right)
            rest = size - at - NB
            wide_lane = lax.broadcasted_iota(jnp.int32, (rest, wide), 1)
            old = work_ref[at + NB :, :]
            old = jnp.where((wide_lane >= at) & (wide_lane < at + NB), 0.0, old)
            work_ref[at + NB :, :] = old - change[at + NB :, :]

    lower_inv = jnp.where(
        lax.broadcasted_iota(jnp.int32, (size, size), 0)
        >= lax.broadcasted_iota(jnp.int32, (size, size), 1),
        work_ref[:, :size],
        0.0,
    )
    half = work_ref[:, size : size + 1]
    check = work_ref[:, size + 1 : size + 2]
    direction = jnp.sum(lower_inv * half, axis=0, keepdims=True)
    diagonal = eye.astype(F32)
    check_ref[...] = jnp.sum(diagonal * check, axis=0, keepdims=True)
    dir_ref[...] = direction
    energy = jnp.sum(half * half, axis=0, keepdims=True)

    dhi, dmid, dlo = split3(direction)
    rows = jnp.concatenate([dhi, dmid, dlo, jnp.zeros((13, size), BF16)], axis=0)
    for part in range(height // 256):
        total = jnp.zeros((16, 256), F32)
        for term in split3(slab_ref[part * 256 : (part + 1) * 256, :]):
            total = total + dot_nt(rows, term)
        image = jnp.sum(total, axis=0, keepdims=True)
        for half in range(2):
            at = 2 * part + half
            image_ref[:, at : at + 1, :] = jnp.broadcast_to(
                image[None, :, half * 128 : (half + 1) * 128], (X * C, 1, 128)
            )
    image_ref[:, height // 128 :, :] = jnp.broadcast_to(energy[None], (X * C, 8, 128))


def factor(grams, back, seeds, design):
    height, breadth = design.shape
    return pl.pallas_call(
        factor_kernel,
        out_shape=(
            jax.ShapeDtypeStruct((X * C, height // 128 + 8, 128), F32),
            jax.ShapeDtypeStruct((1, breadth), F32),
            jax.ShapeDtypeStruct((1, breadth), F32),
        ),
        in_specs=[VMEM] * 4,
        out_specs=(VMEM,) * 3,
        scratch_shapes=[pltpu.VMEM((breadth, breadth + 128), F32)],
        compiler_params=pltpu.CompilerParams(vmem_limit_bytes=40 * 2**20),
        cost_estimate=cost(2**29, 2**22),
        name="factor",
    )(grams, back, seeds, design)


def merge_kernel(parts_ref, image_ref, energy_ref):
    image = jnp.sum(parts_ref[...], axis=0)
    image_ref[...] = image
    squares = jnp.sum(image[:-8] * image[:-8], axis=0, keepdims=True)
    energy = jnp.sum(squares, axis=1, keepdims=True)
    energy_ref[...] = jnp.broadcast_to(energy.reshape(1, 1, 1), energy_ref.shape)


def merge(parts):
    return pl.pallas_call(
        merge_kernel,
        out_shape=(
            jax.ShapeDtypeStruct(parts.shape[1:], F32),
            jax.ShapeDtypeStruct((SOURCES, 1, 128), F32),
        ),
        in_specs=[VMEM],
        out_specs=(VMEM,) * 2,
        name="merge",
    )(parts)


def finish_kernel(energy_ref, image_ref, tgt_ref, dir_ref, sol_ref, res_ref):
    height = tgt_ref.shape[0]
    step = image_ref[height : height + 1, :] / jnp.sum(energy_ref[...], axis=0)
    sol_ref[...] = jnp.tile(step, (1, dir_ref.shape[1] // 128)) * dir_ref[...]
    res_ref[...] = tgt_ref[...] - step * image_ref[:height]


def finish(energies, image, target, direction):
    return pl.pallas_call(
        finish_kernel,
        out_shape=(
            jax.ShapeDtypeStruct(direction.shape, F32),
            jax.ShapeDtypeStruct(target.shape, F32),
        ),
        in_specs=[VMEM] * 4,
        out_specs=(VMEM,) * 2,
        name="finish",
    )(energies, image, target, direction)


def body(design, rademacher, target, sample_rows, checksum_seeds):
    height, breadth = design.shape
    position = lax.axis_index(ROWS).astype(jnp.int32).reshape(1)
    drawn = share(sample_rows.reshape(1, 16), ROWS, SOURCES)
    terms, back, signs = prepare(
        target.reshape(1, height), rademacher.reshape(1, height), design
    )
    near = sketch(position, drawn, signs, terms, back)
    near = jnp.sum(exchange(near, NEAR), axis=0)
    pieces = jnp.concatenate(
        [
            near[:128].reshape(ZB, 16, breadth),
            jnp.broadcast_to(near[None, 128:], (ZB, 8, breadth)),
        ],
        axis=1,
    )
    mine = jnp.sum(exchange(pieces, FAR), axis=0)
    rows = share(mine[:16], FAR, ZB).reshape(ZB * 16, breadth)
    other = lax.ppermute(rows, "za", [(0, 1), (1, 0)])
    grams = exchange(gram_last(other, gram_first(rows)), "y")
    images, direction, checksum = factor(
        grams, mine[16:17], checksum_seeds.reshape(1, breadth), design
    )
    image, energy = merge(exchange(images, GRPS))
    solved, residual = finish(
        exchange(energy, ROWS), image, target.reshape(height // 128, 128), direction
    )
    return solved.reshape(breadth), residual.reshape(height), checksum.reshape(breadth)


def solution(mesh):
    fine = Mesh(mesh.devices.reshape(ZB, ZA, Y, X, C), ROWS + GRPS)
    in_specs = (P(ROWS, GRPS), P(ROWS), P(ROWS), P(ROWS, GRPS, None), P(GRPS))
    out_specs = (P(GRPS), P(ROWS), P(GRPS))
    return jax.shard_map(body, mesh=fine, in_specs=in_specs, out_specs=out_specs, check_vma=False)
```

```python
import functools

import jax
import jax.numpy as jnp
from jax import lax
from jax.experimental import pallas as pl
from jax.experimental.pallas import tpu as pltpu
from jax.sharding import Mesh, PartitionSpec as P

ZB, ZA, Y, X, C = 8, 2, 4, 4, 2
SOURCES = ZB * ZA * Y
FAR = "zb"
NEAR = ("za", "y")
ROWS = (FAR,) + NEAR
GRPS = ("x", "c")
F32 = jnp.float32
BF16 = jnp.bfloat16
VMEM = pl.BlockSpec(memory_space=pltpu.VMEM)
SMEM = pl.BlockSpec(memory_space=pltpu.SMEM)


def cost(flops, size):
    return pl.CostEstimate(flops=flops, bytes_accessed=size, transcendentals=0)


def parity_sign(bits):
    bits = jnp.bitwise_xor(bits, jnp.right_shift(bits, 8))
    bits = jnp.bitwise_xor(bits, jnp.right_shift(bits, 4))
    odd = jnp.bitwise_and(jnp.right_shift(0x6996, jnp.bitwise_and(bits, 15)), 1)
    return 1.0 - 2.0 * odd.astype(F32)


def split3(value):
    hi = value.astype(BF16)
    rest = value - hi.astype(F32)
    mid = rest.astype(BF16)
    lo = (rest - mid.astype(F32)).astype(BF16)
    return hi, mid, lo


def prepare_kernel(tgt_ref, rad_ref, slab_ref, terms_ref, back_ref, sign_ref):
    height, breadth = slab_ref.shape
    rows = jnp.concatenate(list(split3(tgt_ref[...])) + [jnp.zeros((13, height), BF16)], axis=0)
    total = jnp.zeros((16, breadth), F32)
    for place, term in enumerate(split3(slab_ref[...])):
        terms_ref[place] = term
        total = total + jnp.dot(rows, term, preferred_element_type=F32)
    back_ref[...] = jnp.broadcast_to(jnp.sum(total, axis=0, keepdims=True), (8, breadth))
    sign_ref[...] = 1.0 - 2.0 * rad_ref[...].astype(F32)


def prepare(target, rademacher, design):
    height, breadth = design.shape
    return pl.pallas_call(
        prepare_kernel,
        out_shape=(
            jax.ShapeDtypeStruct((3, height, breadth), BF16),
            jax.ShapeDtypeStruct((8, breadth), F32),
            jax.ShapeDtypeStruct((1, height), F32),
        ),
        in_specs=[VMEM] * 3,
        out_specs=(VMEM,) * 3,
        compiler_params=pltpu.CompilerParams(vmem_limit_bytes=40 * 2**20),
        cost_estimate=cost(2**28, 2**23),
        name="prepare",
    )(target, rademacher, design)


def sketch_kernel(pos_ref, idx_ref, sign_ref, terms_ref, back_ref, out_ref, sgn_ref):
    _, height, breadth = terms_ref.shape
    per_owner = idx_ref.shape[2]
    count = 256
    slot = lax.broadcasted_iota(jnp.int32, (count, 128), 0)
    lane = lax.broadcasted_iota(jnp.int32, (count, 128), 1)
    mine = (lane == jnp.bitwise_and(slot, 15))[:, :per_owner]
    ones = jnp.ones((per_owner, 128), BF16)
    drawn = idx_ref[...].reshape(SOURCES, per_owner)
    digits = [
        (piece.astype(F32).astype(BF16), scale)
        for piece, scale in ((jnp.right_shift(drawn, 7), 128), (jnp.bitwise_and(drawn, 127), 1))
    ]
    row_sign = sign_ref[...].astype(BF16)
    for part in range(SOURCES * per_owner // count):
        owner = jnp.right_shift(slot, 4) + part * (count // 16)
        expand = (owner[:, :SOURCES] == lane[:, :SOURCES]).astype(BF16)
        picks = jnp.zeros((count, 128), jnp.int32)
        for digit, scale in digits:
            spread = jnp.dot(expand, digit, preferred_element_type=F32)
            spread = jnp.where(mine, spread, 0.0).astype(BF16)
            spread = jnp.dot(spread, ones, preferred_element_type=F32)
            picks = picks + spread.astype(jnp.int32) * scale
        far = parity_sign(jnp.bitwise_and(owner, pos_ref[0]))
        base = parity_sign(jnp.bitwise_and(jnp.bitwise_and(picks, lane), 127)) * far * 0.03125
        flips = [
            (1.0 - 2.0 * jnp.bitwise_and(jnp.right_shift(picks, 7 + b), 1).astype(F32)).astype(BF16)
            for b in range(4)
        ]
        gray = 0
        current = base.astype(BF16)
        for step in range(height // 128):
            new = step ^ (step >> 1)
            if step:
                current = current * flips[(new ^ gray).bit_length() - 1]
            gray = new
            sgn_ref[part, :, gray * 128 : (gray + 1) * 128] = (
                current * row_sign[:, gray * 128 : (gray + 1) * 128]
            )
        total = jnp.dot(sgn_ref[part], terms_ref[0], preferred_element_type=F32)
        total += jnp.dot(sgn_ref[part], terms_ref[1], preferred_element_type=F32)
        total += jnp.dot(sgn_ref[part], terms_ref[2], preferred_element_type=F32)
        for half in range(2):
            piece = 2 * part + half
            out_ref[piece, 0:128, :] = total[half * 128 : (half + 1) * 128, :]
            out_ref[piece, 128:136, :] = back_ref[...]


def sketch(position, drawn, signs, terms, back):
    _, height, breadth = terms.shape
    return pl.pallas_call(
        sketch_kernel,
        out_shape=jax.ShapeDtypeStruct((ZA * Y, 136, breadth), F32),
        in_specs=[SMEM] + [VMEM] * 4,
        out_specs=VMEM,
        scratch_shapes=[pltpu.VMEM((4, 256, height), BF16)],
        compiler_params=pltpu.CompilerParams(vmem_limit_bytes=40 * 2**20),
        cost_estimate=cost(2**31, 2**22),
        name="sketch",
    )(position, drawn, signs, terms, back)


def exchange(pieces, axes):
    return lax.all_to_all(pieces, axes, split_axis=0, concat_axis=0, tiled=True)


def share(value, axes, count):
    return exchange(jnp.broadcast_to(value[None], (count,) + value.shape), axes)


NB = 16


def row_bcast(value, row):
    return jnp.broadcast_to(value[row : row + 1, :], value.shape)


def dot_nt(left, right):
    return lax.dot_general(left, right, (((1,), (1,)), ((), ())), preferred_element_type=F32)


def dot_tn(left, right):
    return lax.dot_general(left, right, (((0,), (0,)), ((), ())), preferred_element_type=F32)


def gram_products(rows):
    hi, mid, lo = split3(rows)
    right = jnp.concatenate([hi, mid, hi, lo, hi, mid], axis=0)
    hi, mid, lo = split3(rows.T)
    left = jnp.concatenate([hi, hi, mid, hi, lo, mid], axis=1)
    top = jnp.dot(left[:128], right, preferred_element_type=F32)
    end = jnp.dot(left[128:], right[:, 128:], preferred_element_type=F32)
    return top[:, :128], top[:, 128:], end


def gram_first_kernel(rows_ref, out_ref):
    for place, block in enumerate(gram_products(rows_ref[...])):
        out_ref[place * 128 : (place + 1) * 128, :] = block


def gram_last_kernel(rows_ref, old_ref, out_ref):
    first, corner, last = [
        block + old_ref[place * 128 : (place + 1) * 128, :]
        for place, block in enumerate(gram_products(rows_ref[...]))
    ]
    row = lax.broadcasted_iota(jnp.int32, (128, 128), 0)
    lane = lax.broadcasted_iota(jnp.int32, (128, 128), 1)
    mixed = jnp.where(row <= lane, first, last)
    diagonal = jnp.sum(jnp.where(row == lane, last, 0.0), axis=0, keepdims=True)
    for copy in range(Y):
        out_ref[copy, 0:128, :] = mixed
        out_ref[copy, 128:256, :] = corner
        out_ref[copy, 256:264, :] = jnp.broadcast_to(diagonal, (8, 128))


def gram_first(rows):
    return pl.pallas_call(
        gram_first_kernel,
        out_shape=jax.ShapeDtypeStruct((384, 128), F32),
        in_specs=[VMEM],
        out_specs=VMEM,
        cost_estimate=cost(2**27, 2**18),
        compiler_params=pltpu.CompilerParams(vmem_limit_bytes=4 * 2**20),
        name="gram_first",
    )(rows)


def gram_last(rows, old):
    return pl.pallas_call(
        gram_last_kernel,
        out_shape=jax.ShapeDtypeStruct((Y, 264, 128), F32),
        in_specs=[VMEM] * 2,
        out_specs=VMEM,
        cost_estimate=cost(2**27, 2**20),
        compiler_params=pltpu.CompilerParams(vmem_limit_bytes=4 * 2**20),
        name="gram_last",
    )(rows, old)


def factor_kernel(gram_ref, back_ref, seed_ref, slab_ref, image_ref, dir_ref, check_ref, work_ref):
    height, size = slab_ref.shape
    blocks = (gram_ref[0] + gram_ref[1]) + (gram_ref[2] + gram_ref[3])
    mixed, corner, diagonal = blocks[:128], blocks[128:256], blocks[256:257]
    turned = mixed.T
    row = lax.broadcasted_iota(jnp.int32, (128, 128), 0)
    lane = lax.broadcasted_iota(jnp.int32, (128, 128), 1)
    first = jnp.where(row <= lane, mixed, turned)
    last = jnp.where(row == lane, diagonal, jnp.where(row > lane, mixed, turned))
    gram = jnp.concatenate(
        [
            jnp.concatenate([first, corner], axis=1),
            jnp.concatenate([corner.T, last], axis=1),
        ],
        axis=0,
    )
    sub = lax.broadcasted_iota(jnp.int32, (128, size), 0)
    weights = seed_ref[...].astype(F32) * 0.0625
    weight_rows = jnp.where(sub == 1, jnp.broadcast_to(weights, (128, size)), 0.0).astype(BF16)
    back_rows = jnp.where(sub == 0, jnp.broadcast_to(back_ref[...], (128, size)), 0.0)
    eye = (
        lax.broadcasted_iota(jnp.int32, (size, size), 0)
        == lax.broadcasted_iota(jnp.int32, (size, size), 1)
    ).astype(BF16)
    extra = jnp.zeros((size, 128), F32)
    for term in split3(gram):
        extra = extra + dot_nt(term, weight_rows)
    for term in split3(back_rows):
        extra = extra + dot_nt(eye, term)
    work_ref[:, :size] = gram
    work_ref[:, size:] = extra

    wide = size + 128
    lane = lax.broadcasted_iota(jnp.int32, (NB, wide), 1)
    row = lax.broadcasted_iota(jnp.int32, (NB, wide), 0)
    small_row = lax.broadcasted_iota(jnp.int32, (NB, 128), 0)
    for block in range(size // NB):
        at = block * NB
        panel = work_ref[at : at + NB, :]
        cols = [jnp.broadcast_to(panel[:, at + j : at + j + 1], (NB, 128)) for j in range(NB)]
        panel = jnp.where((lane >= at) & (lane < at + NB), (lane - at == row).astype(F32), panel)
        scale = jnp.zeros((NB, 128), F32)
        for j in range(NB):
            pivot = row_bcast(cols[j], j)
            coef = jnp.where(small_row > j, cols[j] / pivot, 0.0)
            scale = jnp.where(small_row == j, pivot, scale)
            for later in range(j + 1, NB):
                cols[later] = cols[later] - coef * row_bcast(cols[later], j)
            panel = panel - jnp.tile(coef, (1, wide // 128)) * row_bcast(panel, j)
        panel = panel * jnp.tile(lax.rsqrt(scale), (1, wide // 128))
        work_ref[at : at + NB, :] = panel
        if at + NB < size:
            hi, mid, lo = split3(panel)
            zero = jnp.zeros((NB, size), BF16)
            keep = lane[:, :size] >= at + NB
            lhi, lmid, llo = [jnp.where(keep, term[:, :size], zero) for term in (hi, mid, lo)]
            left = jnp.concatenate([lhi, lhi, lmid, lhi, llo, lmid], axis=0)
            right = jnp.concatenate([hi, mid, hi, lo, hi, mid], axis=0)
            change = dot_tn(left, right)
            rest = size - at - NB
            wide_lane = lax.broadcasted_iota(jnp.int32, (rest, wide), 1)
            old = work_ref[at + NB :, :]
            old = jnp.where((wide_lane >= at) & (wide_lane < at + NB), 0.0, old)
            work_ref[at + NB :, :] = old - change[at + NB :, :]

    lower_inv = jnp.where(
        lax.broadcasted_iota(jnp.int32, (size, size), 0)
        >= lax.broadcasted_iota(jnp.int32, (size, size), 1),
        work_ref[:, :size],
        0.0,
    )
    half = work_ref[:, size : size + 1]
    check = work_ref[:, size + 1 : size + 2]
    direction = jnp.sum(lower_inv * half, axis=0, keepdims=True)
    diagonal = eye.astype(F32)
    check_ref[...] = jnp.sum(diagonal * check, axis=0, keepdims=True)
    dir_ref[...] = direction
    energy = jnp.sum(half * half, axis=0, keepdims=True)

    dhi, dmid, dlo = split3(direction)
    rows = jnp.concatenate([dhi, dmid, dlo, jnp.zeros((13, size), BF16)], axis=0)
    for part in range(height // 256):
        total = jnp.zeros((16, 256), F32)
        for term in split3(slab_ref[part * 256 : (part + 1) * 256, :]):
            total = total + dot_nt(rows, term)
        image = jnp.sum(total, axis=0, keepdims=True)
        for half in range(2):
            at = 2 * part + half
            image_ref[:, at : at + 1, :] = jnp.broadcast_to(
                image[None, :, half * 128 : (half + 1) * 128], (X * C, 1, 128)
            )
    image_ref[:, height // 128 :, :] = jnp.broadcast_to(energy[None], (X * C, 8, 128))


def factor(grams, back, seeds, design):
    height, breadth = design.shape
    return pl.pallas_call(
        factor_kernel,
        out_shape=(
            jax.ShapeDtypeStruct((X * C, height // 128 + 8, 128), F32),
            jax.ShapeDtypeStruct((1, breadth), F32),
            jax.ShapeDtypeStruct((1, breadth), F32),
        ),
        in_specs=[VMEM] * 4,
        out_specs=(VMEM,) * 3,
        scratch_shapes=[pltpu.VMEM((breadth, breadth + 128), F32)],
        compiler_params=pltpu.CompilerParams(vmem_limit_bytes=40 * 2**20),
        cost_estimate=cost(2**29, 2**22),
        name="factor",
    )(grams, back, seeds, design)


def merge_kernel(parts_ref, image_ref, energy_ref):
    image = jnp.sum(parts_ref[...], axis=0)
    image_ref[...] = image
    squares = jnp.sum(image[:-8] * image[:-8], axis=0, keepdims=True)
    energy = jnp.sum(squares, axis=1, keepdims=True)
    energy_ref[...] = jnp.broadcast_to(energy.reshape(1, 1, 1), energy_ref.shape)


def merge(parts):
    return pl.pallas_call(
        merge_kernel,
        out_shape=(
            jax.ShapeDtypeStruct(parts.shape[1:], F32),
            jax.ShapeDtypeStruct((SOURCES, 1, 128), F32),
        ),
        in_specs=[VMEM],
        out_specs=(VMEM,) * 2,
        compiler_params=pltpu.CompilerParams(vmem_limit_bytes=4 * 2**20),
        name="merge",
    )(parts)


def finish_kernel(energy_ref, image_ref, tgt_ref, dir_ref, sol_ref, res_ref):
    height = tgt_ref.shape[0]
    step = image_ref[height : height + 1, :] / jnp.sum(energy_ref[...], axis=0)
    sol_ref[...] = jnp.tile(step, (1, dir_ref.shape[1] // 128)) * dir_ref[...]
    res_ref[...] = tgt_ref[...] - step * image_ref[:height]


def finish(energies, image, target, direction):
    return pl.pallas_call(
        finish_kernel,
        out_shape=(
            jax.ShapeDtypeStruct(direction.shape, F32),
            jax.ShapeDtypeStruct(target.shape, F32),
        ),
        in_specs=[VMEM] * 4,
        out_specs=(VMEM,) * 2,
        compiler_params=pltpu.CompilerParams(vmem_limit_bytes=4 * 2**20),
        name="finish",
    )(energies, image, target, direction)


def body(design, rademacher, target, sample_rows, checksum_seeds):
    height, breadth = design.shape
    position = lax.axis_index(ROWS).astype(jnp.int32).reshape(1)
    drawn = share(sample_rows.reshape(1, 16), ROWS, SOURCES)
    terms, back, signs = prepare(
        target.reshape(1, height), rademacher.reshape(1, height), design
    )
    near = sketch(position, drawn, signs, terms, back)
    near = jnp.sum(exchange(near, NEAR), axis=0)
    pieces = jnp.concatenate(
        [
            near[:128].reshape(ZB, 16, breadth),
            jnp.broadcast_to(near[None, 128:], (ZB, 8, breadth)),
        ],
        axis=1,
    )
    mine = jnp.sum(exchange(pieces, FAR), axis=0)
    rows = share(mine[:16], FAR, ZB).reshape(ZB * 16, breadth)
    other = lax.ppermute(rows, "za", [(0, 1), (1, 0)])
    grams = exchange(gram_last(other, gram_first(rows)), "y")
    images, direction, checksum = factor(
        grams, mine[16:17], checksum_seeds.reshape(1, breadth), design
    )
    image, energy = merge(exchange(images, GRPS))
    solved, residual = finish(
        exchange(energy, ROWS), image, target.reshape(height // 128, 128), direction
    )
    return solved.reshape(breadth), residual.reshape(height), checksum.reshape(breadth)


def solution(mesh):
    fine = Mesh(mesh.devices.reshape(ZB, ZA, Y, X, C), ROWS + GRPS)
    in_specs = (P(ROWS, GRPS), P(ROWS), P(ROWS), P(ROWS, GRPS, None), P(GRPS))
    out_specs = (P(GRPS), P(ROWS), P(GRPS))
    return jax.shard_map(body, mesh=fine, in_specs=in_specs, out_specs=out_specs, check_vma=False)
```

```python
import functools

import jax
import jax.numpy as jnp
from jax import lax
from jax.experimental import pallas as pl
from jax.experimental.pallas import tpu as pltpu
from jax.sharding import Mesh, PartitionSpec as P

ZB, ZA, Y, X, C = 8, 2, 4, 4, 2
SOURCES = ZB * ZA * Y
FAR = "zb"
NEAR = ("za", "y")
ROWS = (FAR,) + NEAR
GRPS = ("x", "c")
F32 = jnp.float32
BF16 = jnp.bfloat16
VMEM = pl.BlockSpec(memory_space=pltpu.VMEM)
SMEM = pl.BlockSpec(memory_space=pltpu.SMEM)


def cost(flops, size):
    return pl.CostEstimate(flops=flops, bytes_accessed=size, transcendentals=0)


def parity_sign(bits):
    bits = jnp.bitwise_xor(bits, jnp.right_shift(bits, 8))
    bits = jnp.bitwise_xor(bits, jnp.right_shift(bits, 4))
    odd = jnp.bitwise_and(jnp.right_shift(0x6996, jnp.bitwise_and(bits, 15)), 1)
    return 1.0 - 2.0 * odd.astype(F32)


def split3(value):
    hi = value.astype(BF16)
    rest = value - hi.astype(F32)
    mid = rest.astype(BF16)
    lo = (rest - mid.astype(F32)).astype(BF16)
    return hi, mid, lo


def prepare_kernel(tgt_ref, rad_ref, slab_ref, terms_ref, back_ref, sign_ref):
    height, breadth = slab_ref.shape
    rows = jnp.concatenate(list(split3(tgt_ref[...])) + [jnp.zeros((13, height), BF16)], axis=0)
    total = jnp.zeros((16, breadth), F32)
    for place, term in enumerate(split3(slab_ref[...])):
        terms_ref[place] = term
        total = total + jnp.dot(rows, term, preferred_element_type=F32)
    back_ref[...] = jnp.broadcast_to(jnp.sum(total, axis=0, keepdims=True), (8, breadth))
    sign_ref[...] = 1.0 - 2.0 * rad_ref[...].astype(F32)


def prepare(target, rademacher, design):
    height, breadth = design.shape
    return pl.pallas_call(
        prepare_kernel,
        out_shape=(
            jax.ShapeDtypeStruct((3, height, breadth), BF16),
            jax.ShapeDtypeStruct((8, breadth), F32),
            jax.ShapeDtypeStruct((1, height), F32),
        ),
        in_specs=[VMEM] * 3,
        out_specs=(VMEM,) * 3,
        compiler_params=pltpu.CompilerParams(vmem_limit_bytes=40 * 2**20),
        cost_estimate=cost(2**28, 2**23),
        name="prepare",
    )(target, rademacher, design)


def sketch_kernel(pos_ref, idx_ref, sign_ref, terms_ref, back_ref, out_ref, sgn_ref):
    _, height, breadth = terms_ref.shape
    per_owner = idx_ref.shape[2]
    count = SOURCES * per_owner
    sample = lax.broadcasted_iota(jnp.int32, (count, 128), 0)
    lane = lax.broadcasted_iota(jnp.int32, (count, 128), 1)
    owner = jnp.right_shift(sample, 4)
    expand = (owner[:, :SOURCES] == lane[:, :SOURCES]).astype(BF16)
    mine = (lane == jnp.bitwise_and(sample, 15))[:, :per_owner]
    ones = jnp.ones((per_owner, 128), BF16)
    drawn = idx_ref[...].reshape(SOURCES, per_owner)
    picks = jnp.zeros((count, 128), jnp.int32)
    for piece, scale in ((jnp.right_shift(drawn, 7), 128), (jnp.bitwise_and(drawn, 127), 1)):
        spread = jnp.dot(expand, piece.astype(F32).astype(BF16), preferred_element_type=F32)
        spread = jnp.where(mine, spread, 0.0).astype(BF16)
        spread = jnp.dot(spread, ones, preferred_element_type=F32)
        picks = picks + spread.astype(jnp.int32) * scale
    far = parity_sign(jnp.bitwise_and(owner, pos_ref[0]))
    base = parity_sign(jnp.bitwise_and(jnp.bitwise_and(picks, lane), 127)) * far * 0.03125
    flips = [
        (1.0 - 2.0 * jnp.bitwise_and(jnp.right_shift(picks, 7 + b), 1).astype(F32)).astype(BF16)
        for b in range(4)
    ]
    row_sign = sign_ref[...].astype(BF16)
    gray = 0
    current = base.astype(BF16)
    for step in range(height // 128):
        new = step ^ (step >> 1)
        if step:
            current = current * flips[(new ^ gray).bit_length() - 1]
        gray = new
        sgn_ref[:, gray * 128 : (gray + 1) * 128] = (
            current * row_sign[:, gray * 128 : (gray + 1) * 128]
        )
    total = jnp.dot(sgn_ref[...], terms_ref[0], preferred_element_type=F32)
    total += jnp.dot(sgn_ref[...], terms_ref[1], preferred_element_type=F32)
    total += jnp.dot(sgn_ref[...], terms_ref[2], preferred_element_type=F32)
    for piece in range(ZA * Y):
        out_ref[piece, 0:128, :] = total[piece * 128 : (piece + 1) * 128, :]
        out_ref[piece, 128:136, :] = back_ref[...]


def sketch(position, drawn, signs, terms, back):
    _, height, breadth = terms.shape
    return pl.pallas_call(
        sketch_kernel,
        out_shape=jax.ShapeDtypeStruct((ZA * Y, 136, breadth), F32),
        in_specs=[SMEM] + [VMEM] * 4,
        out_specs=VMEM,
        scratch_shapes=[pltpu.VMEM((1024, height), BF16)],
        compiler_params=pltpu.CompilerParams(vmem_limit_bytes=40 * 2**20),
        cost_estimate=cost(2**31, 2**22),
        name="sketch",
    )(position, drawn, signs, terms, back)


def exchange(pieces, axes):
    return lax.all_to_all(pieces, axes, split_axis=0, concat_axis=0, tiled=True)


def share(value, axes, count):
    return exchange(jnp.broadcast_to(value[None], (count,) + value.shape), axes)


NB = 16


def spread_row(value, row):
    return jnp.broadcast_to(value[row : row + 1, :], (8, value.shape[1]))


def dot_nt(left, right):
    return lax.dot_general(left, right, (((1,), (1,)), ((), ())), preferred_element_type=F32)


def dot_tn(left, right):
    return lax.dot_general(left, right, (((0,), (0,)), ((), ())), preferred_element_type=F32)


def gram_products(rows):
    hi, mid, lo = split3(rows)
    right = jnp.concatenate([hi, mid, hi, lo, hi, mid], axis=0)
    hi, mid, lo = split3(rows.T)
    left = jnp.concatenate([hi, hi, mid, hi, lo, mid], axis=1)
    top = jnp.dot(left[:128], right, preferred_element_type=F32)
    end = jnp.dot(left[128:], right[:, 128:], preferred_element_type=F32)
    return top[:, :128], top[:, 128:], end


def gram_kernel(rows_ref, out_ref):
    first, corner, last = gram_products(rows_ref[...])
    row = lax.broadcasted_iota(jnp.int32, (128, 128), 0)
    lane = lax.broadcasted_iota(jnp.int32, (128, 128), 1)
    mixed = jnp.where(row <= lane, first, last)
    diagonal = jnp.sum(jnp.where(row == lane, last, 0.0), axis=0, keepdims=True)
    for copy in range(ZA * Y):
        out_ref[copy, 0:128, :] = mixed
        out_ref[copy, 128:256, :] = corner
        out_ref[copy, 256:264, :] = jnp.broadcast_to(diagonal, (8, 128))


def gram(rows):
    return pl.pallas_call(
        gram_kernel,
        out_shape=jax.ShapeDtypeStruct((ZA * Y, 264, 128), F32),
        in_specs=[VMEM],
        out_specs=VMEM,
        cost_estimate=cost(2**27, 2**20),
        compiler_params=pltpu.CompilerParams(vmem_limit_bytes=4 * 2**20),
        name="gram",
    )(rows)


def factor_kernel(
    gram_ref, back_ref, seed_ref, terms_ref, image_ref, dir_ref, check_ref, work_ref
):
    _, height, size = terms_ref.shape
    blocks = jnp.sum(gram_ref[...], axis=0)
    mixed, corner, diagonal = blocks[:128], blocks[128:256], blocks[256:257]
    turned = mixed.T
    row = lax.broadcasted_iota(jnp.int32, (128, 128), 0)
    lane = lax.broadcasted_iota(jnp.int32, (128, 128), 1)
    first = jnp.where(row <= lane, mixed, turned)
    last = jnp.where(row == lane, diagonal, jnp.where(row > lane, mixed, turned))
    gram = jnp.concatenate(
        [
            jnp.concatenate([first, corner], axis=1),
            jnp.concatenate([corner.T, last], axis=1),
        ],
        axis=0,
    )
    sub = lax.broadcasted_iota(jnp.int32, (128, size), 0)
    weights = seed_ref[...].astype(F32) * 0.0625
    weight_rows = jnp.where(sub == 1, jnp.broadcast_to(weights, (128, size)), 0.0).astype(BF16)
    back_rows = jnp.where(sub == 0, jnp.broadcast_to(back_ref[...], (128, size)), 0.0)
    eye = (
        lax.broadcasted_iota(jnp.int32, (size, size), 0)
        == lax.broadcasted_iota(jnp.int32, (size, size), 1)
    ).astype(BF16)
    extra = jnp.zeros((size, 128), F32)
    for term in split3(gram):
        extra = extra + dot_nt(term, weight_rows)
    for term in split3(back_rows):
        extra = extra + dot_nt(eye, term)
    work_ref[:, :size] = gram
    work_ref[:, size:] = extra

    wide = size + 128
    lane = lax.broadcasted_iota(jnp.int32, (NB, wide), 1)
    row = lax.broadcasted_iota(jnp.int32, (NB, wide), 0)
    half_row = lax.broadcasted_iota(jnp.int32, (8, 128), 0)
    tiles = wide // 128
    for block in range(size // NB):
        at = block * NB
        panel = work_ref[at : at + NB, :]
        top = {j: jnp.broadcast_to(panel[:8, at + j : at + j + 1], (8, 128)) for j in range(8)}
        end = {j: jnp.broadcast_to(panel[8:, at + j : at + j + 1], (8, 128)) for j in range(NB)}

        def entry(i, j):
            return spread_row(top[j], i) if i < 8 else spread_row(end[j], i - 8)

        panel = jnp.where((lane >= at) & (lane < at + NB), (lane - at == row).astype(F32), panel)
        halves = [panel[:8], panel[8:]]
        scales = [jnp.zeros((8, 128), F32)] * 2
        pivot = entry(0, 0)
        for j in range(NB):
            inverse = 1.0 / pivot
            here = j // 8
            scales[here] = jnp.where(half_row == j % 8, pivot, scales[here])
            if j + 1 == NB:
                break
            across = {c: entry(c, j) for c in range(j + 1, NB)}
            pivot = entry(j + 1, j + 1) - across[j + 1] * across[j + 1] * inverse
            source = jnp.tile(inverse, (1, tiles)) * spread_row(halves[here], j % 8)
            if j < 7:
                below = jnp.where(half_row > j, top[j], 0.0)
                halves[0] = halves[0] - jnp.tile(below, (1, tiles)) * source
                for c in range(j + 1, 8):
                    top[c] = top[c] - below * (across[c] * inverse)
            below = end[j] if j < 8 else jnp.where(half_row > j - 8, end[j], 0.0)
            halves[1] = halves[1] - jnp.tile(below, (1, tiles)) * source
            for c in range(j + 1, NB):
                end[c] = end[c] - below * (across[c] * inverse)
        panel = jnp.concatenate(
            [
                half * jnp.tile(lax.rsqrt(scale), (1, tiles))
                for half, scale in zip(halves, scales)
            ],
            axis=0,
        )
        work_ref[at : at + NB, :] = panel
        if at + NB < size:
            hi, mid, lo = split3(panel)
            zero = jnp.zeros((NB, size), BF16)
            keep = lane[:, :size] >= at + NB
            lhi, lmid, llo = [jnp.where(keep, term[:, :size], zero) for term in (hi, mid, lo)]
            left = jnp.concatenate([lhi, lhi, lmid, lhi, llo, lmid], axis=0)
            right = jnp.concatenate([hi, mid, hi, lo, hi, mid], axis=0)
            change = dot_tn(left, right)
            rest = size - at - NB
            wide_lane = lax.broadcasted_iota(jnp.int32, (rest, wide), 1)
            old = work_ref[at + NB :, :]
            old = jnp.where((wide_lane >= at) & (wide_lane < at + NB), 0.0, old)
            work_ref[at + NB :, :] = old - change[at + NB :, :]

    lower_inv = jnp.where(
        lax.broadcasted_iota(jnp.int32, (size, size), 0)
        >= lax.broadcasted_iota(jnp.int32, (size, size), 1),
        work_ref[:, :size],
        0.0,
    )
    half = work_ref[:, size : size + 1]
    check = work_ref[:, size + 1 : size + 2]
    direction = jnp.sum(lower_inv * half, axis=0, keepdims=True)
    diagonal = eye.astype(F32)
    check_ref[...] = jnp.sum(diagonal * check, axis=0, keepdims=True)
    dir_ref[...] = direction
    energy = jnp.sum(half * half, axis=0, keepdims=True)

    dhi, dmid, dlo = split3(direction)
    rows = jnp.concatenate([dhi, dmid, dlo, jnp.zeros((13, size), BF16)], axis=0)
    for part in range(height // 256):
        total = jnp.zeros((16, 256), F32)
        for term in range(3):
            total = total + dot_nt(rows, terms_ref[term, part * 256 : (part + 1) * 256, :])
        image = jnp.sum(total, axis=0, keepdims=True)
        for half in range(2):
            at = 2 * part + half
            image_ref[:, at : at + 1, :] = jnp.broadcast_to(
                image[None, :, half * 128 : (half + 1) * 128], (X * C, 1, 128)
            )
    image_ref[:, height // 128 :, :] = jnp.broadcast_to(energy[None], (X * C, 8, 128))


def factor(grams, back, seeds, terms):
    _, height, breadth = terms.shape
    return pl.pallas_call(
        factor_kernel,
        out_shape=(
            jax.ShapeDtypeStruct((X * C, height // 128 + 8, 128), F32),
            jax.ShapeDtypeStruct((1, breadth), F32),
            jax.ShapeDtypeStruct((1, breadth), F32),
        ),
        in_specs=[VMEM] * 4,
        out_specs=(VMEM,) * 3,
        scratch_shapes=[pltpu.VMEM((breadth, breadth + 128), F32)],
        compiler_params=pltpu.CompilerParams(vmem_limit_bytes=40 * 2**20),
        cost_estimate=cost(2**29, 2**22),
        name="factor",
    )(grams, back, seeds, terms)


def merge_kernel(parts_ref, image_ref, energy_ref):
    image = jnp.sum(parts_ref[...], axis=0)
    image_ref[...] = image
    squares = jnp.sum(image[:-8] * image[:-8], axis=0, keepdims=True)
    energy = jnp.sum(squares, axis=1, keepdims=True)
    energy_ref[...] = jnp.broadcast_to(energy.reshape(1, 1, 1), energy_ref.shape)


def merge(parts):
    return pl.pallas_call(
        merge_kernel,
        out_shape=(
            jax.ShapeDtypeStruct(parts.shape[1:], F32),
            jax.ShapeDtypeStruct((SOURCES, 1, 128), F32),
        ),
        in_specs=[VMEM],
        out_specs=(VMEM,) * 2,
        compiler_params=pltpu.CompilerParams(vmem_limit_bytes=4 * 2**20),
        name="merge",
    )(parts)


def finish_kernel(energy_ref, image_ref, tgt_ref, dir_ref, sol_ref, res_ref):
    height = tgt_ref.shape[0]
    step = image_ref[height : height + 1, :] / jnp.sum(energy_ref[...], axis=0)
    sol_ref[...] = jnp.tile(step, (1, dir_ref.shape[1] // 128)) * dir_ref[...]
    res_ref[...] = tgt_ref[...] - step * image_ref[:height]


def finish(energies, image, target, direction):
    return pl.pallas_call(
        finish_kernel,
        out_shape=(
            jax.ShapeDtypeStruct(direction.shape, F32),
            jax.ShapeDtypeStruct(target.shape, F32),
        ),
        in_specs=[VMEM] * 4,
        out_specs=(VMEM,) * 2,
        compiler_params=pltpu.CompilerParams(vmem_limit_bytes=4 * 2**20),
        name="finish",
    )(energies, image, target, direction)


def body(design, rademacher, target, sample_rows, checksum_seeds):
    height, breadth = design.shape
    position = lax.axis_index(ROWS).astype(jnp.int32).reshape(1)
    drawn = share(sample_rows.reshape(1, 16), ROWS, SOURCES)
    terms, back, signs = prepare(
        target.reshape(1, height), rademacher.reshape(1, height), design
    )
    near = sketch(position, drawn, signs, terms, back)
    near = jnp.sum(exchange(near, NEAR), axis=0)
    rows = lax.psum(near, FAR)
    images, direction, checksum = factor(
        exchange(gram(rows[:128]), NEAR), rows[128:129], checksum_seeds.reshape(1, breadth), terms
    )
    image, energy = merge(exchange(images, GRPS))
    solved, residual = finish(
        exchange(energy, ROWS), image, target.reshape(height // 128, 128), direction
    )
    return solved.reshape(breadth), residual.reshape(height), checksum.reshape(breadth)


def solution(mesh):
    fine = Mesh(mesh.devices.reshape(ZB, ZA, Y, X, C), ROWS + GRPS)
    in_specs = (P(ROWS, GRPS), P(ROWS), P(ROWS), P(ROWS, GRPS, None), P(GRPS))
    out_specs = (P(GRPS), P(ROWS), P(GRPS))
    return jax.shard_map(body, mesh=fine, in_specs=in_specs, out_specs=out_specs, check_vma=False)
```

```python
import functools

import jax
import jax.numpy as jnp
from jax import lax
from jax.experimental import pallas as pl
from jax.experimental.pallas import tpu as pltpu
from jax.sharding import Mesh, PartitionSpec as P

ZB, ZA, Y, X, C = 8, 2, 4, 4, 2
SOURCES = ZB * ZA * Y
FAR = "zb"
NEAR = ("za", "y")
ROWS = (FAR,) + NEAR
GRPS = ("x", "c")
F32 = jnp.float32
BF16 = jnp.bfloat16
VMEM = pl.BlockSpec(memory_space=pltpu.VMEM)
SMEM = pl.BlockSpec(memory_space=pltpu.SMEM)


def cost(flops, size):
    return pl.CostEstimate(flops=flops, bytes_accessed=size, transcendentals=0)


def parity_sign(bits):
    bits = jnp.bitwise_xor(bits, jnp.right_shift(bits, 8))
    bits = jnp.bitwise_xor(bits, jnp.right_shift(bits, 4))
    odd = jnp.bitwise_and(jnp.right_shift(0x6996, jnp.bitwise_and(bits, 15)), 1)
    return 1.0 - 2.0 * odd.astype(F32)


def split3(value):
    hi = value.astype(BF16)
    rest = value - hi.astype(F32)
    mid = rest.astype(BF16)
    lo = (rest - mid.astype(F32)).astype(BF16)
    return hi, mid, lo


def prepare_kernel(tgt_ref, rad_ref, slab_ref, terms_ref, back_ref, sign_ref):
    height, breadth = slab_ref.shape
    rows = jnp.concatenate(list(split3(tgt_ref[...])) + [jnp.zeros((13, height), BF16)], axis=0)
    total = jnp.zeros((16, breadth), F32)
    for place, term in enumerate(split3(slab_ref[...])):
        terms_ref[place] = term
        total = total + jnp.dot(rows, term, preferred_element_type=F32)
    back_ref[...] = jnp.broadcast_to(jnp.sum(total, axis=0, keepdims=True), (8, breadth))
    sign_ref[...] = 1.0 - 2.0 * rad_ref[...].astype(F32)


def prepare(target, rademacher, design):
    height, breadth = design.shape
    return pl.pallas_call(
        prepare_kernel,
        out_shape=(
            jax.ShapeDtypeStruct((3, height, breadth), BF16),
            jax.ShapeDtypeStruct((8, breadth), F32),
            jax.ShapeDtypeStruct((1, height), F32),
        ),
        in_specs=[VMEM] * 3,
        out_specs=(VMEM,) * 3,
        compiler_params=pltpu.CompilerParams(vmem_limit_bytes=40 * 2**20),
        cost_estimate=cost(2**28, 2**23),
        name="prepare",
    )(target, rademacher, design)


def sketch_kernel(pos_ref, idx_ref, sign_ref, terms_ref, back_ref, out_ref, sgn_ref):
    _, height, breadth = terms_ref.shape
    per_owner = idx_ref.shape[2]
    count = SOURCES * per_owner
    sample = lax.broadcasted_iota(jnp.int32, (count, 128), 0)
    lane = lax.broadcasted_iota(jnp.int32, (count, 128), 1)
    owner = jnp.right_shift(sample, 4)
    expand = (owner[:, :SOURCES] == lane[:, :SOURCES]).astype(BF16)
    mine = (lane == jnp.bitwise_and(sample, 15))[:, :per_owner]
    ones = jnp.ones((per_owner, 128), BF16)
    drawn = idx_ref[...].reshape(SOURCES, per_owner)
    picks = jnp.zeros((count, 128), jnp.int32)
    for piece, scale in ((jnp.right_shift(drawn, 7), 128), (jnp.bitwise_and(drawn, 127), 1)):
        spread = jnp.dot(expand, piece.astype(F32).astype(BF16), preferred_element_type=F32)
        spread = jnp.where(mine, spread, 0.0).astype(BF16)
        spread = jnp.dot(spread, ones, preferred_element_type=F32)
        picks = picks + spread.astype(jnp.int32) * scale
    far = parity_sign(jnp.bitwise_and(owner, pos_ref[0]))
    base = parity_sign(jnp.bitwise_and(jnp.bitwise_and(picks, lane), 127)) * far * 0.03125
    flips = [
        (1.0 - 2.0 * jnp.bitwise_and(jnp.right_shift(picks, 7 + b), 1).astype(F32)).astype(BF16)
        for b in range(4)
    ]
    row_sign = sign_ref[...].astype(BF16)
    gray = 0
    current = base.astype(BF16)
    for step in range(height // 128):
        new = step ^ (step >> 1)
        if step:
            current = current * flips[(new ^ gray).bit_length() - 1]
        gray = new
        sgn_ref[:, gray * 128 : (gray + 1) * 128] = (
            current * row_sign[:, gray * 128 : (gray + 1) * 128]
        )
    total = jnp.dot(sgn_ref[...], terms_ref[0], preferred_element_type=F32)
    total += jnp.dot(sgn_ref[...], terms_ref[1], preferred_element_type=F32)
    total += jnp.dot(sgn_ref[...], terms_ref[2], preferred_element_type=F32)
    for piece in range(ZA * Y):
        out_ref[piece, 0:128, :] = total[piece * 128 : (piece + 1) * 128, :]
        out_ref[piece, 128:136, :] = back_ref[...]


def sketch(position, drawn, signs, terms, back):
    _, height, breadth = terms.shape
    return pl.pallas_call(
        sketch_kernel,
        out_shape=jax.ShapeDtypeStruct((ZA * Y, 136, breadth), F32),
        in_specs=[SMEM] + [VMEM] * 4,
        out_specs=VMEM,
        scratch_shapes=[pltpu.VMEM((1024, height), BF16)],
        compiler_params=pltpu.CompilerParams(vmem_limit_bytes=40 * 2**20),
        cost_estimate=cost(2**31, 2**22),
        name="sketch",
    )(position, drawn, signs, terms, back)


def exchange(pieces, axes):
    return lax.all_to_all(pieces, axes, split_axis=0, concat_axis=0, tiled=True)


def share(value, axes, count):
    return exchange(jnp.broadcast_to(value[None], (count,) + value.shape), axes)


NB = 32


def spread_row(value, row):
    return jnp.broadcast_to(value[row : row + 1, :], (8, value.shape[1]))


def dot_nt(left, right):
    return lax.dot_general(left, right, (((1,), (1,)), ((), ())), preferred_element_type=F32)


def dot_tn(left, right):
    return lax.dot_general(left, right, (((0,), (0,)), ((), ())), preferred_element_type=F32)


def deal_kernel(parts_ref, out_ref):
    total = jnp.sum(parts_ref[...], axis=0)
    for copy in range(ZB):
        rows = total[16 * copy : 16 * copy + 16]
        out_ref[copy, 0:16, :] = rows[:, :128]
        out_ref[copy, 16:32, :] = rows[:, 128:]
        out_ref[copy, 32:33, :] = total[128:129, :128]
        out_ref[copy, 33:34, :] = total[128:129, 128:]
        out_ref[copy, 34:40, :] = jnp.zeros((6, 128), F32)


def deal(parts):
    return pl.pallas_call(
        deal_kernel,
        out_shape=jax.ShapeDtypeStruct((ZB, 40, 128), F32),
        in_specs=[VMEM],
        out_specs=VMEM,
        compiler_params=pltpu.CompilerParams(vmem_limit_bytes=8 * 2**20),
        name="deal",
    )(parts)


def fold_kernel(parts_ref, rows_ref, back_ref):
    total = jnp.sum(parts_ref[...], axis=0)
    for copy in range(ZB):
        rows_ref[copy, :, 0:128] = total[0:16]
        rows_ref[copy, :, 128:256] = total[16:32]
    back_ref[:, 0:128] = total[32:33]
    back_ref[:, 128:256] = total[33:34]


def fold(parts):
    return pl.pallas_call(
        fold_kernel,
        out_shape=(
            jax.ShapeDtypeStruct((ZB, 16, 256), F32),
            jax.ShapeDtypeStruct((1, 256), F32),
        ),
        in_specs=[VMEM],
        out_specs=(VMEM,) * 2,
        compiler_params=pltpu.CompilerParams(vmem_limit_bytes=4 * 2**20),
        name="fold",
    )(parts)


def gram_products(rows):
    hi, mid, lo = split3(rows)
    right = jnp.concatenate([hi, mid, hi, lo, hi, mid], axis=0)
    hi, mid, lo = split3(rows.T)
    left = jnp.concatenate([hi, hi, mid, hi, lo, mid], axis=1)
    top = jnp.dot(left[:128], right, preferred_element_type=F32)
    end = jnp.dot(left[128:], right[:, 128:], preferred_element_type=F32)
    return top[:, :128], top[:, 128:], end


def gram_kernel(rows_ref, out_ref):
    first, corner, last = gram_products(rows_ref[...])
    row = lax.broadcasted_iota(jnp.int32, (128, 128), 0)
    lane = lax.broadcasted_iota(jnp.int32, (128, 128), 1)
    mixed = jnp.where(row <= lane, first, last)
    diagonal = jnp.sum(jnp.where(row == lane, last, 0.0), axis=0, keepdims=True)
    for copy in range(ZA * Y):
        out_ref[copy, 0:128, :] = mixed
        out_ref[copy, 128:256, :] = corner
        out_ref[copy, 256:264, :] = jnp.broadcast_to(diagonal, (8, 128))


def gram(rows):
    return pl.pallas_call(
        gram_kernel,
        out_shape=jax.ShapeDtypeStruct((ZA * Y, 264, 128), F32),
        in_specs=[VMEM],
        out_specs=VMEM,
        cost_estimate=cost(2**27, 2**20),
        compiler_params=pltpu.CompilerParams(vmem_limit_bytes=4 * 2**20),
        name="gram",
    )(rows)


def factor_kernel(gram_ref, back_ref, seed_ref, slab_ref, image_ref, dir_ref, check_ref, work_ref):
    height, size = slab_ref.shape
    blocks = jnp.sum(gram_ref[...], axis=0)
    mixed, corner, diagonal = blocks[:128], blocks[128:256], blocks[256:257]
    turned = mixed.T
    row = lax.broadcasted_iota(jnp.int32, (128, 128), 0)
    lane = lax.broadcasted_iota(jnp.int32, (128, 128), 1)
    first = jnp.where(row <= lane, mixed, turned)
    last = jnp.where(row == lane, diagonal, jnp.where(row > lane, mixed, turned))
    gram = jnp.concatenate(
        [
            jnp.concatenate([first, corner], axis=1),
            jnp.concatenate([corner.T, last], axis=1),
        ],
        axis=0,
    )
    sub = lax.broadcasted_iota(jnp.int32, (128, size), 0)
    weights = seed_ref[...].astype(F32) * 0.0625
    weight_rows = jnp.where(sub == 1, jnp.broadcast_to(weights, (128, size)), 0.0).astype(BF16)
    back_rows = jnp.where(sub == 0, jnp.broadcast_to(back_ref[...], (128, size)), 0.0)
    eye = (
        lax.broadcasted_iota(jnp.int32, (size, size), 0)
        == lax.broadcasted_iota(jnp.int32, (size, size), 1)
    ).astype(BF16)
    extra = jnp.zeros((size, 128), F32)
    for term in split3(gram):
        extra = extra + dot_nt(term, weight_rows)
    for term in split3(back_rows):
        extra = extra + dot_nt(eye, term)
    work_ref[:, :size] = gram
    work_ref[:, size:] = extra

    wide = size + 128
    lane = lax.broadcasted_iota(jnp.int32, (NB, wide), 1)
    row = lax.broadcasted_iota(jnp.int32, (NB, wide), 0)
    half_row = lax.broadcasted_iota(jnp.int32, (8, 128), 0)
    wide_half = lax.broadcasted_iota(jnp.int32, (8, wide), 1)
    half_count = NB // 8
    tiles = wide // 128
    for block in range(size // NB):
        at = block * NB
        halves = [work_ref[at + 8 * h : at + 8 * h + 8, :] for h in range(half_count)]
        scales = [jnp.zeros((8, 128), F32)] * half_count
        for phase in range(2):
            base = 16 * phase
            begin = at + base
            cols = {
                (c, h): jnp.broadcast_to(halves[h][:, at + c : at + c + 1], (8, 128))
                for c in range(base, base + 16)
                for h in range(c // 8, half_count)
            }
            for h in range(2 * phase, half_count):
                unit = (wide_half - begin == half_row[:, :1] + (8 * h - base)).astype(F32)
                inside = (wide_half >= begin) & (wide_half < begin + 16)
                halves[h] = jnp.where(inside, unit, halves[h])
            pivot = spread_row(cols[base, base // 8], 0)
            for j in range(base, base + 16):
                inverse = 1.0 / pivot
                here = j // 8
                scales[here] = jnp.where(half_row == j % 8, pivot, scales[here])
                if j + 1 == NB:
                    break
                across = {
                    c: spread_row(cols[j, c // 8], c % 8) for c in range(j + 1, base + 16)
                }
                if j + 1 < base + 16:
                    pivot = (
                        spread_row(cols[j + 1, (j + 1) // 8], (j + 1) % 8)
                        - across[j + 1] * across[j + 1] * inverse
                    )
                source = jnp.tile(inverse, (1, tiles)) * spread_row(halves[here], j % 8)
                for h in range((j + 1) // 8, half_count):
                    below = cols[j, h]
                    if h == here:
                        below = jnp.where(half_row > j % 8, below, 0.0)
                    halves[h] = halves[h] - jnp.tile(below, (1, tiles)) * source
                    for c in range(j + 1, base + 16):
                        if c // 8 <= h:
                            cols[c, h] = cols[c, h] - below * (across[c] * inverse)
        panel = jnp.concatenate(
            [
                half * jnp.tile(lax.rsqrt(scale), (1, tiles))
                for half, scale in zip(halves, scales)
            ],
            axis=0,
        )
        work_ref[at : at + NB, :] = panel
        if at + NB < size:
            hi, mid, lo = split3(panel)
            zero = jnp.zeros((NB, size), BF16)
            keep = lane[:, :size] >= at + NB
            lhi, lmid, llo = [jnp.where(keep, term[:, :size], zero) for term in (hi, mid, lo)]
            left = jnp.concatenate([lhi, lhi, lmid, lhi, llo, lmid], axis=0)
            blank = (row < 16) & (lane >= at + 16) & (lane < at + NB)
            hi, mid, lo = [
                jnp.where(blank, jnp.zeros((NB, wide), BF16), term) for term in (hi, mid, lo)
            ]
            right = jnp.concatenate([hi, mid, hi, lo, hi, mid], axis=0)
            change = dot_tn(left, right)
            rest = size - at - NB
            wide_lane = lax.broadcasted_iota(jnp.int32, (rest, wide), 1)
            old = work_ref[at + NB :, :]
            old = jnp.where((wide_lane >= at) & (wide_lane < at + NB), 0.0, old)
            work_ref[at + NB :, :] = old - change[at + NB :, :]

    lower_inv = jnp.where(
        lax.broadcasted_iota(jnp.int32, (size, size), 0)
        >= lax.broadcasted_iota(jnp.int32, (size, size), 1),
        work_ref[:, :size],
        0.0,
    )
    half = work_ref[:, size : size + 1]
    check = work_ref[:, size + 1 : size + 2]
    direction = jnp.sum(lower_inv * half, axis=0, keepdims=True)
    diagonal = eye.astype(F32)
    check_ref[...] = jnp.sum(diagonal * check, axis=0, keepdims=True)
    dir_ref[...] = direction
    energy = jnp.sum(half * half, axis=0, keepdims=True)

    dhi, dmid, dlo = split3(direction)
    rows = jnp.concatenate([dhi, dmid, dlo, jnp.zeros((13, size), BF16)], axis=0)
    for part in range(height // 256):
        total = jnp.zeros((16, 256), F32)
        for term in split3(slab_ref[part * 256 : (part + 1) * 256, :]):
            total = total + dot_nt(rows, term)
        image = jnp.sum(total, axis=0, keepdims=True)
        for half in range(2):
            at = 2 * part + half
            image_ref[:, at : at + 1, :] = jnp.broadcast_to(
                image[None, :, half * 128 : (half + 1) * 128], (X * C, 1, 128)
            )
    image_ref[:, height // 128 :, :] = jnp.broadcast_to(energy[None], (X * C, 8, 128))


def factor(grams, back, seeds, design):
    height, breadth = design.shape
    return pl.pallas_call(
        factor_kernel,
        out_shape=(
            jax.ShapeDtypeStruct((X * C, height // 128 + 8, 128), F32),
            jax.ShapeDtypeStruct((1, breadth), F32),
            jax.ShapeDtypeStruct((1, breadth), F32),
        ),
        in_specs=[VMEM] * 4,
        out_specs=(VMEM,) * 3,
        scratch_shapes=[pltpu.VMEM((breadth, breadth + 128), F32)],
        compiler_params=pltpu.CompilerParams(vmem_limit_bytes=40 * 2**20),
        cost_estimate=cost(2**29, 2**22),
        name="factor",
    )(grams, back, seeds, design)


def merge_kernel(parts_ref, image_ref, energy_ref):
    image = jnp.sum(parts_ref[...], axis=0)
    image_ref[...] = image
    squares = jnp.sum(image[:-8] * image[:-8], axis=0, keepdims=True)
    energy = jnp.sum(squares, axis=1, keepdims=True)
    energy_ref[...] = jnp.broadcast_to(energy.reshape(1, 1, 1), energy_ref.shape)


def merge(parts):
    return pl.pallas_call(
        merge_kernel,
        out_shape=(
            jax.ShapeDtypeStruct(parts.shape[1:], F32),
            jax.ShapeDtypeStruct((SOURCES, 1, 128), F32),
        ),
        in_specs=[VMEM],
        out_specs=(VMEM,) * 2,
        compiler_params=pltpu.CompilerParams(vmem_limit_bytes=4 * 2**20),
        name="merge",
    )(parts)


def finish_kernel(energy_ref, image_ref, tgt_ref, dir_ref, sol_ref, res_ref):
    height = tgt_ref.shape[0]
    step = image_ref[height : height + 1, :] / jnp.sum(energy_ref[...], axis=0)
    sol_ref[...] = jnp.tile(step, (1, dir_ref.shape[1] // 128)) * dir_ref[...]
    res_ref[...] = tgt_ref[...] - step * image_ref[:height]


def finish(energies, image, target, direction):
    return pl.pallas_call(
        finish_kernel,
        out_shape=(
            jax.ShapeDtypeStruct(direction.shape, F32),
            jax.ShapeDtypeStruct(target.shape, F32),
        ),
        in_specs=[VMEM] * 4,
        out_specs=(VMEM,) * 2,
        compiler_params=pltpu.CompilerParams(vmem_limit_bytes=4 * 2**20),
        name="finish",
    )(energies, image, target, direction)


def body(design, rademacher, target, sample_rows, checksum_seeds):
    height, breadth = design.shape
    position = lax.axis_index(ROWS).astype(jnp.int32).reshape(1)
    drawn = share(sample_rows.reshape(1, 16), ROWS, SOURCES)
    terms, back, signs = prepare(
        target.reshape(1, height), rademacher.reshape(1, height), design
    )
    near = sketch(position, drawn, signs, terms, back)
    pieces = deal(exchange(near, NEAR))
    rows, back = fold(exchange(pieces, FAR))
    rows = exchange(rows, FAR).reshape(ZB * 16, breadth)
    images, direction, checksum = factor(
        exchange(gram(rows), NEAR), back, checksum_seeds.reshape(1, breadth), design
    )
    image, energy = merge(exchange(images, GRPS))
    solved, residual = finish(
        exchange(energy, ROWS), image, target.reshape(height // 128, 128), direction
    )
    return solved.reshape(breadth), residual.reshape(height), checksum.reshape(breadth)


def solution(mesh):
    fine = Mesh(mesh.devices.reshape(ZB, ZA, Y, X, C), ROWS + GRPS)
    in_specs = (P(ROWS, GRPS), P(ROWS), P(ROWS), P(ROWS, GRPS, None), P(GRPS))
    out_specs = (P(GRPS), P(ROWS), P(GRPS))
    return jax.shard_map(body, mesh=fine, in_specs=in_specs, out_specs=out_specs, check_vma=False)
```

```python
import functools

import jax
import jax.numpy as jnp
from jax import lax
from jax.experimental import pallas as pl
from jax.experimental.pallas import tpu as pltpu
from jax.sharding import Mesh, PartitionSpec as P

ZB, ZA, Y, X, C = 8, 2, 4, 4, 2
SOURCES = ZB * ZA * Y
FAR = "zb"
NEAR = ("za", "y")
ROWS = (FAR,) + NEAR
GRPS = ("x", "c")
F32 = jnp.float32
BF16 = jnp.bfloat16
VMEM = pl.BlockSpec(memory_space=pltpu.VMEM)
SMEM = pl.BlockSpec(memory_space=pltpu.SMEM)


def cost(flops, size):
    return pl.CostEstimate(flops=flops, bytes_accessed=size, transcendentals=0)


def parity_sign(bits):
    bits = jnp.bitwise_xor(bits, jnp.right_shift(bits, 8))
    bits = jnp.bitwise_xor(bits, jnp.right_shift(bits, 4))
    odd = jnp.bitwise_and(jnp.right_shift(0x6996, jnp.bitwise_and(bits, 15)), 1)
    return 1.0 - 2.0 * odd.astype(F32)


def split3(value):
    hi = value.astype(BF16)
    rest = value - hi.astype(F32)
    mid = rest.astype(BF16)
    lo = (rest - mid.astype(F32)).astype(BF16)
    return hi, mid, lo


def mix_kernel(tgt_ref, rad_ref, slab_ref, mixed_ref, back_ref, work_ref):
    height, breadth = slab_ref.shape
    block = 256
    blocks = height // block
    row = lax.broadcasted_iota(jnp.int32, (block, block), 0)
    lane = lax.broadcasted_iota(jnp.int32, (block, block), 1)
    table = parity_sign(jnp.bitwise_and(row, lane)) * 0.03125
    rows = jnp.concatenate(list(split3(tgt_ref[...])) + [jnp.zeros((13, height), BF16)], axis=0)
    back = jnp.zeros((16, breadth), F32)
    for place in range(blocks):
        at = place * block
        sign = 1.0 - 2.0 * rad_ref[:, at : at + block].astype(F32)
        left = (table * sign).astype(BF16)
        total = jnp.zeros((block, breadth), F32)
        for term in split3(slab_ref[at : at + block, :]):
            total = total + jnp.dot(left, term, preferred_element_type=F32)
            back = back + jnp.dot(rows[:, at : at + block], term, preferred_element_type=F32)
        work_ref[at : at + block, :] = total
    back_ref[...] = jnp.broadcast_to(jnp.sum(back, axis=0, keepdims=True), (8, breadth))
    for chunk in range(block // 8):
        tiles = [work_ref[b * block + chunk * 8 : b * block + chunk * 8 + 8, :] for b in range(blocks)]
        stride = 1
        while stride < blocks:
            tiles = [
                tiles[b] + tiles[b ^ stride] if b & stride == 0 else tiles[b ^ stride] - tiles[b]
                for b in range(blocks)
            ]
            stride *= 2
        for b in range(blocks):
            mixed_ref[b * block + chunk * 8 : b * block + chunk * 8 + 8, :] = tiles[b]


def mix(target, rademacher, design):
    height, breadth = design.shape
    return pl.pallas_call(
        mix_kernel,
        out_shape=(
            jax.ShapeDtypeStruct((height, breadth), F32),
            jax.ShapeDtypeStruct((8, breadth), F32),
        ),
        in_specs=[VMEM] * 3,
        out_specs=(VMEM,) * 2,
        scratch_shapes=[pltpu.VMEM((height, breadth), F32)],
        compiler_params=pltpu.CompilerParams(vmem_limit_bytes=24 * 2**20),
        cost_estimate=cost(2**30, 2**23),
        name="mix",
    )(target, rademacher, design)


def pick_kernel(pos_ref, idx_ref, mixed_ref, back_ref, out_ref):
    per_owner = idx_ref.shape[2]
    owners = 128 // per_owner

    def one(piece, carry):
        for near in range(owners):
            owner = piece * owners + near
            odd = jnp.bitwise_and(owner, pos_ref[0])
            for shift in (4, 2, 1):
                odd = jnp.bitwise_xor(odd, jnp.right_shift(odd, shift))
            sign = (1 - 2 * jnp.bitwise_and(odd, 1)).astype(F32)
            for slot in range(per_owner):
                at = near * per_owner + slot
                drawn = mixed_ref[pl.ds(idx_ref[owner, 0, slot], 1), :]
                out_ref[piece, at : at + 1, :] = drawn * sign
        out_ref[piece, 128:136, :] = back_ref[...]
        return carry

    lax.fori_loop(0, out_ref.shape[0], one, 0)


def pick(position, drawn, mixed, back):
    return pl.pallas_call(
        pick_kernel,
        out_shape=jax.ShapeDtypeStruct((ZA * Y, 136, mixed.shape[1]), F32),
        in_specs=[SMEM] * 2 + [VMEM] * 2,
        out_specs=VMEM,
        compiler_params=pltpu.CompilerParams(vmem_limit_bytes=8 * 2**20),
        cost_estimate=cost(2**20, 2**21),
        name="pick",
    )(position, drawn, mixed, back)


def exchange(pieces, axes):
    return lax.all_to_all(pieces, axes, split_axis=0, concat_axis=0, tiled=True)


def share(value, axes, count):
    return exchange(jnp.broadcast_to(value[None], (count,) + value.shape), axes)


NB = 32


def spread_row(value, row):
    return jnp.broadcast_to(value[row : row + 1, :], (8, value.shape[1]))


def dot_nt(left, right):
    return lax.dot_general(left, right, (((1,), (1,)), ((), ())), preferred_element_type=F32)


def dot_tn(left, right):
    return lax.dot_general(left, right, (((0,), (0,)), ((), ())), preferred_element_type=F32)


def deal_kernel(parts_ref, out_ref):
    total = jnp.sum(parts_ref[...], axis=0)
    for copy in range(ZB):
        rows = total[16 * copy : 16 * copy + 16]
        out_ref[copy, 0:16, :] = rows[:, :128]
        out_ref[copy, 16:32, :] = rows[:, 128:]
        out_ref[copy, 32:33, :] = total[128:129, :128]
        out_ref[copy, 33:34, :] = total[128:129, 128:]
        out_ref[copy, 34:40, :] = jnp.zeros((6, 128), F32)


def deal(parts):
    return pl.pallas_call(
        deal_kernel,
        out_shape=jax.ShapeDtypeStruct((ZB, 40, 128), F32),
        in_specs=[VMEM],
        out_specs=VMEM,
        compiler_params=pltpu.CompilerParams(vmem_limit_bytes=8 * 2**20),
        name="deal",
    )(parts)


def fold_kernel(parts_ref, rows_ref, back_ref):
    total = jnp.sum(parts_ref[...], axis=0)
    for copy in range(ZB):
        rows_ref[copy, :, 0:128] = total[0:16]
        rows_ref[copy, :, 128:256] = total[16:32]
    back_ref[:, 0:128] = total[32:33]
    back_ref[:, 128:256] = total[33:34]


def fold(parts):
    return pl.pallas_call(
        fold_kernel,
        out_shape=(
            jax.ShapeDtypeStruct((ZB, 16, 256), F32),
            jax.ShapeDtypeStruct((1, 256), F32),
        ),
        in_specs=[VMEM],
        out_specs=(VMEM,) * 2,
        compiler_params=pltpu.CompilerParams(vmem_limit_bytes=4 * 2**20),
        name="fold",
    )(parts)


def gram_products(rows):
    hi, mid, lo = split3(rows)
    right = jnp.concatenate([hi, mid, hi, lo, hi, mid], axis=0)
    hi, mid, lo = split3(rows.T)
    left = jnp.concatenate([hi, hi, mid, hi, lo, mid], axis=1)
    top = jnp.dot(left[:128], right, preferred_element_type=F32)
    end = jnp.dot(left[128:], right[:, 128:], preferred_element_type=F32)
    return top[:, :128], top[:, 128:], end


def gram_kernel(rows_ref, out_ref):
    first, corner, last = gram_products(rows_ref[...])
    row = lax.broadcasted_iota(jnp.int32, (128, 128), 0)
    lane = lax.broadcasted_iota(jnp.int32, (128, 128), 1)
    mixed = jnp.where(row <= lane, first, last)
    diagonal = jnp.sum(jnp.where(row == lane, last, 0.0), axis=0, keepdims=True)
    for copy in range(ZA * Y):
        out_ref[copy, 0:128, :] = mixed
        out_ref[copy, 128:256, :] = corner
        out_ref[copy, 256:264, :] = jnp.broadcast_to(diagonal, (8, 128))


def gram(rows):
    return pl.pallas_call(
        gram_kernel,
        out_shape=jax.ShapeDtypeStruct((ZA * Y, 264, 128), F32),
        in_specs=[VMEM],
        out_specs=VMEM,
        cost_estimate=cost(2**27, 2**20),
        compiler_params=pltpu.CompilerParams(vmem_limit_bytes=4 * 2**20),
        name="gram",
    )(rows)


def factor_kernel(gram_ref, back_ref, seed_ref, slab_ref, image_ref, dir_ref, check_ref, work_ref):
    height, size = slab_ref.shape
    blocks = jnp.sum(gram_ref[...], axis=0)
    mixed, corner, diagonal = blocks[:128], blocks[128:256], blocks[256:257]
    turned = mixed.T
    row = lax.broadcasted_iota(jnp.int32, (128, 128), 0)
    lane = lax.broadcasted_iota(jnp.int32, (128, 128), 1)
    first = jnp.where(row <= lane, mixed, turned)
    last = jnp.where(row == lane, diagonal, jnp.where(row > lane, mixed, turned))
    gram = jnp.concatenate(
        [
            jnp.concatenate([first, corner], axis=1),
            jnp.concatenate([corner.T, last], axis=1),
        ],
        axis=0,
    )
    sub = lax.broadcasted_iota(jnp.int32, (128, size), 0)
    weights = seed_ref[...].astype(F32) * 0.0625
    weight_rows = jnp.where(sub == 1, jnp.broadcast_to(weights, (128, size)), 0.0).astype(BF16)
    back_rows = jnp.where(sub == 0, jnp.broadcast_to(back_ref[...], (128, size)), 0.0)
    eye = (
        lax.broadcasted_iota(jnp.int32, (size, size), 0)
        == lax.broadcasted_iota(jnp.int32, (size, size), 1)
    ).astype(BF16)
    extra = jnp.zeros((size, 128), F32)
    for term in split3(gram):
        extra = extra + dot_nt(term, weight_rows)
    for term in split3(back_rows):
        extra = extra + dot_nt(eye, term)
    work_ref[:, :size] = gram
    work_ref[:, size:] = extra

    wide = size + 128
    lane = lax.broadcasted_iota(jnp.int32, (NB, wide), 1)
    row = lax.broadcasted_iota(jnp.int32, (NB, wide), 0)
    half_row = lax.broadcasted_iota(jnp.int32, (8, 128), 0)
    wide_half = lax.broadcasted_iota(jnp.int32, (8, wide), 1)
    half_count = NB // 8
    tiles = wide // 128
    for block in range(size // NB):
        at = block * NB
        halves = [work_ref[at + 8 * h : at + 8 * h + 8, :] for h in range(half_count)]
        scales = [jnp.zeros((8, 128), F32)] * half_count
        for phase in range(2):
            base = 16 * phase
            begin = at + base
            cols = {
                (c, h): jnp.broadcast_to(halves[h][:, at + c : at + c + 1], (8, 128))
                for c in range(base, base + 16)
                for h in range(c // 8, half_count)
            }
            for h in range(2 * phase, half_count):
                unit = (wide_half - begin == half_row[:, :1] + (8 * h - base)).astype(F32)
                inside = (wide_half >= begin) & (wide_half < begin + 16)
                halves[h] = jnp.where(inside, unit, halves[h])
            pivot = spread_row(cols[base, base // 8], 0)
            for j in range(base, base + 16):
                inverse = 1.0 / pivot
                here = j // 8
                scales[here] = jnp.where(half_row == j % 8, pivot, scales[here])
                if j + 1 == NB:
                    break
                across = {
                    c: spread_row(cols[j, c // 8], c % 8) for c in range(j + 1, base + 16)
                }
                if j + 1 < base + 16:
                    pivot = (
                        spread_row(cols[j + 1, (j + 1) // 8], (j + 1) % 8)
                        - across[j + 1] * across[j + 1] * inverse
                    )
                source = jnp.tile(inverse, (1, tiles)) * spread_row(halves[here], j % 8)
                for h in range((j + 1) // 8, half_count):
                    below = cols[j, h]
                    if h == here:
                        below = jnp.where(half_row > j % 8, below, 0.0)
                    halves[h] = halves[h] - jnp.tile(below, (1, tiles)) * source
                    for c in range(j + 1, base + 16):
                        if c // 8 <= h:
                            cols[c, h] = cols[c, h] - below * (across[c] * inverse)
        panel = jnp.concatenate(
            [
                half * jnp.tile(lax.rsqrt(scale), (1, tiles))
                for half, scale in zip(halves, scales)
            ],
            axis=0,
        )
        work_ref[at : at + NB, :] = panel
        if at + NB < size:
            hi, mid, lo = split3(panel)
            zero = jnp.zeros((NB, size), BF16)
            keep = lane[:, :size] >= at + NB
            lhi, lmid, llo = [jnp.where(keep, term[:, :size], zero) for term in (hi, mid, lo)]
            left = jnp.concatenate([lhi, lhi, lmid, lhi, llo, lmid], axis=0)
            blank = (row < 16) & (lane >= at + 16) & (lane < at + NB)
            hi, mid, lo = [
                jnp.where(blank, jnp.zeros((NB, wide), BF16), term) for term in (hi, mid, lo)
            ]
            right = jnp.concatenate([hi, mid, hi, lo, hi, mid], axis=0)
            change = dot_tn(left, right)
            rest = size - at - NB
            wide_lane = lax.broadcasted_iota(jnp.int32, (rest, wide), 1)
            old = work_ref[at + NB :, :]
            old = jnp.where((wide_lane >= at) & (wide_lane < at + NB), 0.0, old)
            work_ref[at + NB :, :] = old - change[at + NB :, :]

    lower_inv = jnp.where(
        lax.broadcasted_iota(jnp.int32, (size, size), 0)
        >= lax.broadcasted_iota(jnp.int32, (size, size), 1),
        work_ref[:, :size],
        0.0,
    )
    half = work_ref[:, size : size + 1]
    check = work_ref[:, size + 1 : size + 2]
    direction = jnp.sum(lower_inv * half, axis=0, keepdims=True)
    diagonal = eye.astype(F32)
    check_ref[...] = jnp.sum(diagonal * check, axis=0, keepdims=True)
    dir_ref[...] = direction
    energy = jnp.sum(half * half, axis=0, keepdims=True)

    dhi, dmid, dlo = split3(direction)
    rows = jnp.concatenate([dhi, dmid, dlo, jnp.zeros((13, size), BF16)], axis=0)
    for part in range(height // 256):
        total = jnp.zeros((16, 256), F32)
        for term in split3(slab_ref[part * 256 : (part + 1) * 256, :]):
            total = total + dot_nt(rows, term)
        image = jnp.sum(total, axis=0, keepdims=True)
        for half in range(2):
            at = 2 * part + half
            image_ref[:, at : at + 1, :] = jnp.broadcast_to(
                image[None, :, half * 128 : (half + 1) * 128], (X * C, 1, 128)
            )
    image_ref[:, height // 128 :, :] = jnp.broadcast_to(energy[None], (X * C, 8, 128))


def factor(grams, back, seeds, design):
    height, breadth = design.shape
    return pl.pallas_call(
        factor_kernel,
        out_shape=(
            jax.ShapeDtypeStruct((X * C, height // 128 + 8, 128), F32),
            jax.ShapeDtypeStruct((1, breadth), F32),
            jax.ShapeDtypeStruct((1, breadth), F32),
        ),
        in_specs=[VMEM] * 4,
        out_specs=(VMEM,) * 3,
        scratch_shapes=[pltpu.VMEM((breadth, breadth + 128), F32)],
        compiler_params=pltpu.CompilerParams(vmem_limit_bytes=40 * 2**20),
        cost_estimate=cost(2**29, 2**22),
        name="factor",
    )(grams, back, seeds, design)


def merge_kernel(parts_ref, image_ref, energy_ref):
    image = jnp.sum(parts_ref[...], axis=0)
    image_ref[...] = image
    squares = jnp.sum(image[:-8] * image[:-8], axis=0, keepdims=True)
    energy = jnp.sum(squares, axis=1, keepdims=True)
    energy_ref[...] = jnp.broadcast_to(energy.reshape(1, 1, 1), energy_ref.shape)


def merge(parts):
    return pl.pallas_call(
        merge_kernel,
        out_shape=(
            jax.ShapeDtypeStruct(parts.shape[1:], F32),
            jax.ShapeDtypeStruct((SOURCES, 1, 128), F32),
        ),
        in_specs=[VMEM],
        out_specs=(VMEM,) * 2,
        compiler_params=pltpu.CompilerParams(vmem_limit_bytes=4 * 2**20),
        name="merge",
    )(parts)


def finish_kernel(energy_ref, image_ref, tgt_ref, dir_ref, sol_ref, res_ref):
    height = tgt_ref.shape[0]
    step = image_ref[height : height + 1, :] / jnp.sum(energy_ref[...], axis=0)
    sol_ref[...] = jnp.tile(step, (1, dir_ref.shape[1] // 128)) * dir_ref[...]
    res_ref[...] = tgt_ref[...] - step * image_ref[:height]


def finish(energies, image, target, direction):
    return pl.pallas_call(
        finish_kernel,
        out_shape=(
            jax.ShapeDtypeStruct(direction.shape, F32),
            jax.ShapeDtypeStruct(target.shape, F32),
        ),
        in_specs=[VMEM] * 4,
        out_specs=(VMEM,) * 2,
        compiler_params=pltpu.CompilerParams(vmem_limit_bytes=4 * 2**20),
        name="finish",
    )(energies, image, target, direction)


def body(design, rademacher, target, sample_rows, checksum_seeds):
    height, breadth = design.shape
    position = lax.axis_index(ROWS).astype(jnp.int32).reshape(1)
    drawn = share(sample_rows.reshape(1, 16), ROWS, SOURCES)
    mixed, back = mix(target.reshape(1, height), rademacher.reshape(1, height), design)
    near = pick(position, drawn, mixed, back)
    pieces = deal(exchange(near, NEAR))
    rows, back = fold(exchange(pieces, FAR))
    rows = exchange(rows, FAR).reshape(ZB * 16, breadth)
    images, direction, checksum = factor(
        exchange(gram(rows), NEAR), back, checksum_seeds.reshape(1, breadth), design
    )
    image, energy = merge(exchange(images, GRPS))
    solved, residual = finish(
        exchange(energy, ROWS), image, target.reshape(height // 128, 128), direction
    )
    return solved.reshape(breadth), residual.reshape(height), checksum.reshape(breadth)


def solution(mesh):
    fine = Mesh(mesh.devices.reshape(ZB, ZA, Y, X, C), ROWS + GRPS)
    in_specs = (P(ROWS, GRPS), P(ROWS), P(ROWS), P(ROWS, GRPS, None), P(GRPS))
    out_specs = (P(GRPS), P(ROWS), P(GRPS))
    return jax.shard_map(body, mesh=fine, in_specs=in_specs, out_specs=out_specs, check_vma=False)
```

```python
import functools

import jax
import jax.numpy as jnp
from jax import lax
from jax.experimental import pallas as pl
from jax.experimental.pallas import tpu as pltpu
from jax.sharding import Mesh, PartitionSpec as P

ZB, ZA, Y, X, C = 8, 2, 4, 4, 2
SOURCES = ZB * ZA * Y
FAR = "zb"
NEAR = ("za", "y")
ROWS = (FAR,) + NEAR
GRPS = ("x", "c")
F32 = jnp.float32
BF16 = jnp.bfloat16
VMEM = pl.BlockSpec(memory_space=pltpu.VMEM)
SMEM = pl.BlockSpec(memory_space=pltpu.SMEM)


def cost(flops, size):
    return pl.CostEstimate(flops=flops, bytes_accessed=size, transcendentals=0)


def parity_sign(bits):
    bits = jnp.bitwise_xor(bits, jnp.right_shift(bits, 8))
    bits = jnp.bitwise_xor(bits, jnp.right_shift(bits, 4))
    odd = jnp.bitwise_and(jnp.right_shift(0x6996, jnp.bitwise_and(bits, 15)), 1)
    return 1.0 - 2.0 * odd.astype(F32)


def split3(value):
    hi = value.astype(BF16)
    rest = value - hi.astype(F32)
    mid = rest.astype(BF16)
    lo = (rest - mid.astype(F32)).astype(BF16)
    return hi, mid, lo


def mix_kernel(tgt_ref, rad_ref, slab_ref, mixed_ref, back_ref, work_ref):
    height, breadth = slab_ref.shape
    block = 256
    blocks = height // block
    row = lax.broadcasted_iota(jnp.int32, (block, block), 0)
    lane = lax.broadcasted_iota(jnp.int32, (block, block), 1)
    table = parity_sign(jnp.bitwise_and(row, lane)) * 0.03125
    rows = jnp.concatenate(list(split3(tgt_ref[...])) + [jnp.zeros((13, height), BF16)], axis=0)
    back = jnp.zeros((16, breadth), F32)
    for place in range(blocks):
        at = place * block
        sign = 1.0 - 2.0 * rad_ref[:, at : at + block].astype(F32)
        left = (table * sign).astype(BF16)
        total = jnp.zeros((block, breadth), F32)
        for term in split3(slab_ref[at : at + block, :]):
            total = total + jnp.dot(left, term, preferred_element_type=F32)
            back = back + jnp.dot(rows[:, at : at + block], term, preferred_element_type=F32)
        work_ref[at : at + block, :] = total
    back = jnp.sum(back, axis=0, keepdims=True)
    for copy in range(4):
        back_ref[2 * copy : 2 * copy + 1, :] = back[:, :128]
        back_ref[2 * copy + 1 : 2 * copy + 2, :] = back[:, 128:]
    for chunk in range(block // 8):
        tiles = [work_ref[b * block + chunk * 8 : b * block + chunk * 8 + 8, :] for b in range(blocks)]
        stride = 1
        while stride < blocks:
            tiles = [
                tiles[b] + tiles[b ^ stride] if b & stride == 0 else tiles[b ^ stride] - tiles[b]
                for b in range(blocks)
            ]
            stride *= 2
        for b in range(blocks):
            at = 2 * (b * block + chunk * 8)
            mixed_ref[pl.ds(at, 8, stride=2), :] = tiles[b][:, :128]
            mixed_ref[pl.ds(at + 1, 8, stride=2), :] = tiles[b][:, 128:]


def mix(target, rademacher, design):
    height, breadth = design.shape
    return pl.pallas_call(
        mix_kernel,
        out_shape=(
            jax.ShapeDtypeStruct((2 * height, 128), F32),
            jax.ShapeDtypeStruct((8, 128), F32),
        ),
        in_specs=[VMEM] * 3,
        out_specs=(VMEM,) * 2,
        scratch_shapes=[pltpu.VMEM((height, breadth), F32)],
        compiler_params=pltpu.CompilerParams(vmem_limit_bytes=24 * 2**20),
        cost_estimate=cost(2**30, 2**23),
        name="mix",
    )(target, rademacher, design)


def pick_kernel(pos_ref, idx_ref, mixed_ref, back_ref, out_ref):
    per_owner = idx_ref.shape[2]
    owners = 128 // per_owner

    def one(piece, carry):
        for near in range(owners):
            owner = piece * owners + near
            odd = jnp.bitwise_and(owner, pos_ref[0])
            for shift in (4, 2, 1):
                odd = jnp.bitwise_xor(odd, jnp.right_shift(odd, shift))
            sign = (1 - 2 * jnp.bitwise_and(odd, 1)).astype(F32)
            for slot in range(per_owner):
                drawn = mixed_ref[idx_ref[owner, 0, slot]]
                out_ref[piece, near * per_owner + slot] = drawn * sign
        out_ref[piece, 128:132] = back_ref[...]
        return carry

    lax.fori_loop(0, out_ref.shape[0], one, 0)


def pick(position, drawn, mixed, back):
    return pl.pallas_call(
        pick_kernel,
        out_shape=jax.ShapeDtypeStruct((ZA * Y, 132, 2, 128), F32),
        in_specs=[SMEM] * 2 + [VMEM] * 2,
        out_specs=VMEM,
        compiler_params=pltpu.CompilerParams(vmem_limit_bytes=8 * 2**20),
        cost_estimate=cost(2**20, 2**21),
        name="pick",
    )(position, drawn, mixed, back)


def exchange(pieces, axes):
    return lax.all_to_all(pieces, axes, split_axis=0, concat_axis=0, tiled=True)


def share(value, axes, count):
    return exchange(jnp.broadcast_to(value[None], (count,) + value.shape), axes)


NB = 32


def spread_row(value, row):
    return jnp.broadcast_to(value[row : row + 1, :], (8, value.shape[1]))


def dot_nt(left, right):
    return lax.dot_general(left, right, (((1,), (1,)), ((), ())), preferred_element_type=F32)


def dot_tn(left, right):
    return lax.dot_general(left, right, (((0,), (0,)), ((), ())), preferred_element_type=F32)


def deal_kernel(parts_ref, out_ref):
    total = jnp.sum(parts_ref[...], axis=0)
    for copy in range(ZB):
        out_ref[copy, 0:32, :] = total[32 * copy : 32 * copy + 32]
        out_ref[copy, 32:40, :] = total[256:264]


def deal(parts):
    return pl.pallas_call(
        deal_kernel,
        out_shape=jax.ShapeDtypeStruct((ZB, 40, 128), F32),
        in_specs=[VMEM],
        out_specs=VMEM,
        compiler_params=pltpu.CompilerParams(vmem_limit_bytes=8 * 2**20),
        name="deal",
    )(parts)


def fold_kernel(parts_ref, rows_ref, back_ref):
    total = jnp.sum(parts_ref[...], axis=0)
    for copy in range(ZB):
        rows_ref[copy] = total[0:32]
    back_ref[:, 0:128] = total[32:33]
    back_ref[:, 128:256] = total[33:34]


def fold(parts):
    return pl.pallas_call(
        fold_kernel,
        out_shape=(
            jax.ShapeDtypeStruct((ZB, 32, 128), F32),
            jax.ShapeDtypeStruct((1, 256), F32),
        ),
        in_specs=[VMEM],
        out_specs=(VMEM,) * 2,
        compiler_params=pltpu.CompilerParams(vmem_limit_bytes=4 * 2**20),
        name="fold",
    )(parts)


def gram_products(rows):
    hi, mid, lo = split3(rows)
    right = jnp.concatenate([hi, mid, hi, lo, hi, mid], axis=0)
    hi, mid, lo = split3(rows.T)
    left = jnp.concatenate([hi, hi, mid, hi, lo, mid], axis=1)
    top = jnp.dot(left[:128], right, preferred_element_type=F32)
    end = jnp.dot(left[128:], right[:, 128:], preferred_element_type=F32)
    return top[:, :128], top[:, 128:], end


def gram_kernel(rows_ref, out_ref):
    count = rows_ref.shape[0] // 2
    rows = [rows_ref[pl.ds(half, count, stride=2), :] for half in range(2)]
    first, corner, last = gram_products(jnp.concatenate(rows, axis=1))
    row = lax.broadcasted_iota(jnp.int32, (128, 128), 0)
    lane = lax.broadcasted_iota(jnp.int32, (128, 128), 1)
    mixed = jnp.where(row <= lane, first, last)
    diagonal = jnp.sum(jnp.where(row == lane, last, 0.0), axis=0, keepdims=True)
    for copy in range(ZA * Y):
        out_ref[copy, 0:128, :] = mixed
        out_ref[copy, 128:256, :] = corner
        out_ref[copy, 256:264, :] = jnp.broadcast_to(diagonal, (8, 128))


def gram(rows):
    return pl.pallas_call(
        gram_kernel,
        out_shape=jax.ShapeDtypeStruct((ZA * Y, 264, 128), F32),
        in_specs=[VMEM],
        out_specs=VMEM,
        cost_estimate=cost(2**27, 2**20),
        compiler_params=pltpu.CompilerParams(vmem_limit_bytes=4 * 2**20),
        name="gram",
    )(rows)


def factor_kernel(gram_ref, back_ref, seed_ref, slab_ref, image_ref, dir_ref, check_ref, work_ref):
    height, size = slab_ref.shape
    blocks = jnp.sum(gram_ref[...], axis=0)
    mixed, corner, diagonal = blocks[:128], blocks[128:256], blocks[256:257]
    turned = mixed.T
    row = lax.broadcasted_iota(jnp.int32, (128, 128), 0)
    lane = lax.broadcasted_iota(jnp.int32, (128, 128), 1)
    first = jnp.where(row <= lane, mixed, turned)
    last = jnp.where(row == lane, diagonal, jnp.where(row > lane, mixed, turned))
    gram = jnp.concatenate(
        [
            jnp.concatenate([first, corner], axis=1),
            jnp.concatenate([corner.T, last], axis=1),
        ],
        axis=0,
    )
    sub = lax.broadcasted_iota(jnp.int32, (128, size), 0)
    weights = seed_ref[...].astype(F32) * 0.0625
    weight_rows = jnp.where(sub == 1, jnp.broadcast_to(weights, (128, size)), 0.0).astype(BF16)
    back_rows = jnp.where(sub == 0, jnp.broadcast_to(back_ref[...], (128, size)), 0.0)
    eye = (
        lax.broadcasted_iota(jnp.int32, (size, size), 0)
        == lax.broadcasted_iota(jnp.int32, (size, size), 1)
    ).astype(BF16)
    extra = jnp.zeros((size, 128), F32)
    for term in split3(gram):
        extra = extra + dot_nt(term, weight_rows)
    for term in split3(back_rows):
        extra = extra + dot_nt(eye, term)
    work_ref[:, :size] = gram
    work_ref[:, size:] = extra

    wide = size + 128
    lane = lax.broadcasted_iota(jnp.int32, (NB, wide), 1)
    row = lax.broadcasted_iota(jnp.int32, (NB, wide), 0)
    half_row = lax.broadcasted_iota(jnp.int32, (8, 128), 0)
    wide_half = lax.broadcasted_iota(jnp.int32, (8, wide), 1)
    half_count = NB // 8
    tiles = wide // 128
    for block in range(size // NB):
        at = block * NB
        halves = [work_ref[at + 8 * h : at + 8 * h + 8, :] for h in range(half_count)]
        scales = [jnp.zeros((8, 128), F32)] * half_count
        for phase in range(2):
            base = 16 * phase
            begin = at + base
            cols = {
                (c, h): jnp.broadcast_to(halves[h][:, at + c : at + c + 1], (8, 128))
                for c in range(base, base + 16)
                for h in range(c // 8, half_count)
            }
            for h in range(2 * phase, half_count):
                unit = (wide_half - begin == half_row[:, :1] + (8 * h - base)).astype(F32)
                inside = (wide_half >= begin) & (wide_half < begin + 16)
                halves[h] = jnp.where(inside, unit, halves[h])
            pivot = spread_row(cols[base, base // 8], 0)
            for j in range(base, base + 16):
                inverse = pl.reciprocal(pivot, approx=True)
                for _ in range(2):
                    inverse = inverse * (2.0 - pivot * inverse)
                here = j // 8
                scales[here] = jnp.where(half_row == j % 8, pivot, scales[here])
                if j + 1 == NB:
                    break
                across = {
                    c: spread_row(cols[j, c // 8], c % 8) for c in range(j + 1, base + 16)
                }
                if j + 1 < base + 16:
                    pivot = (
                        spread_row(cols[j + 1, (j + 1) // 8], (j + 1) % 8)
                        - across[j + 1] * across[j + 1] * inverse
                    )
                source = jnp.tile(inverse, (1, tiles)) * spread_row(halves[here], j % 8)
                for h in range((j + 1) // 8, half_count):
                    below = cols[j, h]
                    if h == here:
                        below = jnp.where(half_row > j % 8, below, 0.0)
                    halves[h] = halves[h] - jnp.tile(below, (1, tiles)) * source
                    for c in range(j + 1, base + 16):
                        if c // 8 <= h:
                            cols[c, h] = cols[c, h] - below * (across[c] * inverse)
        panel = jnp.concatenate(
            [
                half * jnp.tile(lax.rsqrt(scale), (1, tiles))
                for half, scale in zip(halves, scales)
            ],
            axis=0,
        )
        work_ref[at : at + NB, :] = panel
        if at + NB < size:
            hi, mid, lo = split3(panel)
            zero = jnp.zeros((NB, size), BF16)
            keep = lane[:, :size] >= at + NB
            lhi, lmid, llo = [jnp.where(keep, term[:, :size], zero) for term in (hi, mid, lo)]
            left = jnp.concatenate([lhi, lhi, lmid, lhi, llo, lmid], axis=0)
            blank = (row < 16) & (lane >= at + 16) & (lane < at + NB)
            hi, mid, lo = [
                jnp.where(blank, jnp.zeros((NB, wide), BF16), term) for term in (hi, mid, lo)
            ]
            right = jnp.concatenate([hi, mid, hi, lo, hi, mid], axis=0)
            change = dot_tn(left, right)
            rest = size - at - NB
            wide_lane = lax.broadcasted_iota(jnp.int32, (rest, wide), 1)
            old = work_ref[at + NB :, :]
            old = jnp.where((wide_lane >= at) & (wide_lane < at + NB), 0.0, old)
            work_ref[at + NB :, :] = old - change[at + NB :, :]

    lower_inv = jnp.where(
        lax.broadcasted_iota(jnp.int32, (size, size), 0)
        >= lax.broadcasted_iota(jnp.int32, (size, size), 1),
        work_ref[:, :size],
        0.0,
    )
    half = work_ref[:, size : size + 1]
    check = work_ref[:, size + 1 : size + 2]
    direction = jnp.sum(lower_inv * half, axis=0, keepdims=True)
    diagonal = eye.astype(F32)
    check_ref[...] = jnp.sum(diagonal * check, axis=0, keepdims=True)
    dir_ref[...] = direction
    energy = jnp.sum(half * half, axis=0, keepdims=True)

    dhi, dmid, dlo = split3(direction)
    rows = jnp.concatenate([dhi, dmid, dlo, jnp.zeros((13, size), BF16)], axis=0)
    for part in range(height // 256):
        total = jnp.zeros((16, 256), F32)
        for term in split3(slab_ref[part * 256 : (part + 1) * 256, :]):
            total = total + dot_nt(rows, term)
        image = jnp.sum(total, axis=0, keepdims=True)
        for half in range(2):
            at = 2 * part + half
            image_ref[:, at : at + 1, :] = jnp.broadcast_to(
                image[None, :, half * 128 : (half + 1) * 128], (X * C, 1, 128)
            )
    image_ref[:, height // 128 :, :] = jnp.broadcast_to(energy[None], (X * C, 8, 128))


def factor(grams, back, seeds, design):
    height, breadth = design.shape
    return pl.pallas_call(
        factor_kernel,
        out_shape=(
            jax.ShapeDtypeStruct((X * C, height // 128 + 8, 128), F32),
            jax.ShapeDtypeStruct((1, breadth), F32),
            jax.ShapeDtypeStruct((1, breadth), F32),
        ),
        in_specs=[VMEM] * 4,
        out_specs=(VMEM,) * 3,
        scratch_shapes=[pltpu.VMEM((breadth, breadth + 128), F32)],
        compiler_params=pltpu.CompilerParams(vmem_limit_bytes=40 * 2**20),
        cost_estimate=cost(2**29, 2**22),
        name="factor",
    )(grams, back, seeds, design)


def merge_kernel(parts_ref, image_ref, energy_ref):
    image = jnp.sum(parts_ref[...], axis=0)
    image_ref[...] = image
    squares = jnp.sum(image[:-8] * image[:-8], axis=0, keepdims=True)
    energy = jnp.sum(squares, axis=1, keepdims=True)
    energy_ref[...] = jnp.broadcast_to(energy.reshape(1, 1, 1), energy_ref.shape)


def merge(parts):
    return pl.pallas_call(
        merge_kernel,
        out_shape=(
            jax.ShapeDtypeStruct(parts.shape[1:], F32),
            jax.ShapeDtypeStruct((SOURCES, 1, 128), F32),
        ),
        in_specs=[VMEM],
        out_specs=(VMEM,) * 2,
        compiler_params=pltpu.CompilerParams(vmem_limit_bytes=4 * 2**20),
        name="merge",
    )(parts)


def finish_kernel(energy_ref, image_ref, tgt_ref, dir_ref, sol_ref, res_ref):
    height = tgt_ref.shape[0]
    step = image_ref[height : height + 1, :] / jnp.sum(energy_ref[...], axis=0)
    sol_ref[...] = jnp.tile(step, (1, dir_ref.shape[1] // 128)) * dir_ref[...]
    res_ref[...] = tgt_ref[...] - step * image_ref[:height]


def finish(energies, image, target, direction):
    return pl.pallas_call(
        finish_kernel,
        out_shape=(
            jax.ShapeDtypeStruct(direction.shape, F32),
            jax.ShapeDtypeStruct(target.shape, F32),
        ),
        in_specs=[VMEM] * 4,
        out_specs=(VMEM,) * 2,
        compiler_params=pltpu.CompilerParams(vmem_limit_bytes=4 * 2**20),
        name="finish",
    )(energies, image, target, direction)


def body(design, rademacher, target, sample_rows, checksum_seeds):
    height, breadth = design.shape
    position = lax.axis_index(ROWS).astype(jnp.int32).reshape(1)
    drawn = share(sample_rows.reshape(1, 16), ROWS, SOURCES)
    mixed, back = mix(target.reshape(1, height), rademacher.reshape(1, height), design)
    near = pick(position, drawn, mixed.reshape(height, 2, 128), back.reshape(4, 2, 128))
    pieces = deal(exchange(near.reshape(ZA * Y, 264, 128), NEAR))
    rows, back = fold(exchange(pieces, FAR))
    rows = exchange(rows, FAR).reshape(ZB * 32, 128)
    images, direction, checksum = factor(
        exchange(gram(rows), NEAR), back, checksum_seeds.reshape(1, breadth), design
    )
    image, energy = merge(exchange(images, GRPS))
    solved, residual = finish(
        exchange(energy, ROWS), image, target.reshape(height // 128, 128), direction
    )
    return solved.reshape(breadth), residual.reshape(height), checksum.reshape(breadth)


def solution(mesh):
    fine = Mesh(mesh.devices.reshape(ZB, ZA, Y, X, C), ROWS + GRPS)
    in_specs = (P(ROWS, GRPS), P(ROWS), P(ROWS), P(ROWS, GRPS, None), P(GRPS))
    out_specs = (P(GRPS), P(ROWS), P(GRPS))
    return jax.shard_map(body, mesh=fine, in_specs=in_specs, out_specs=out_specs, check_vma=False)
```

```python
import functools

import jax
import jax.numpy as jnp
from jax import lax
from jax.experimental import pallas as pl
from jax.experimental.pallas import tpu as pltpu
from jax.sharding import Mesh, PartitionSpec as P

ZB, ZA, Y, X, C = 8, 2, 4, 4, 2
SOURCES = ZB * ZA * Y
FAR = "zb"
NEAR = ("za", "y")
ROWS = (FAR,) + NEAR
GRPS = ("x", "c")
F32 = jnp.float32
BF16 = jnp.bfloat16
VMEM = pl.BlockSpec(memory_space=pltpu.VMEM)
SMEM = pl.BlockSpec(memory_space=pltpu.SMEM)


def cost(flops, size):
    return pl.CostEstimate(flops=flops, bytes_accessed=size, transcendentals=0)


def parity_sign(bits):
    bits = jnp.bitwise_xor(bits, jnp.right_shift(bits, 8))
    bits = jnp.bitwise_xor(bits, jnp.right_shift(bits, 4))
    odd = jnp.bitwise_and(jnp.right_shift(0x6996, jnp.bitwise_and(bits, 15)), 1)
    return 1.0 - 2.0 * odd.astype(F32)


def split3(value):
    hi = value.astype(BF16)
    rest = value - hi.astype(F32)
    mid = rest.astype(BF16)
    lo = (rest - mid.astype(F32)).astype(BF16)
    return hi, mid, lo


def mix_kernel(tgt_ref, rad_ref, slab_ref, mixed_ref, back_ref, work_ref):
    height, breadth = slab_ref.shape
    block = 256
    blocks = height // block
    row = lax.broadcasted_iota(jnp.int32, (block, block), 0)
    lane = lax.broadcasted_iota(jnp.int32, (block, block), 1)
    table = parity_sign(jnp.bitwise_and(row, lane)) * 0.03125
    rows = jnp.concatenate(list(split3(tgt_ref[...])) + [jnp.zeros((13, height), BF16)], axis=0)
    back = jnp.zeros((16, breadth), F32)
    for place in range(blocks):
        at = place * block
        sign = 1.0 - 2.0 * rad_ref[:, at : at + block].astype(F32)
        left = (table * sign).astype(BF16)
        total = jnp.zeros((block, breadth), F32)
        for term in split3(slab_ref[at : at + block, :]):
            total = total + jnp.dot(left, term, preferred_element_type=F32)
            back = back + jnp.dot(rows[:, at : at + block], term, preferred_element_type=F32)
        work_ref[at : at + block, :] = total
    back = jnp.sum(back, axis=0, keepdims=True)
    for copy in range(4):
        back_ref[2 * copy : 2 * copy + 1, :] = back[:, :128]
        back_ref[2 * copy + 1 : 2 * copy + 2, :] = back[:, 128:]
    for chunk in range(block // 8):
        tiles = [work_ref[b * block + chunk * 8 : b * block + chunk * 8 + 8, :] for b in range(blocks)]
        stride = 1
        while stride < blocks:
            tiles = [
                tiles[b] + tiles[b ^ stride] if b & stride == 0 else tiles[b ^ stride] - tiles[b]
                for b in range(blocks)
            ]
            stride *= 2
        for b in range(blocks):
            at = 2 * (b * block + chunk * 8)
            mixed_ref[pl.ds(at, 8, stride=2), :] = tiles[b][:, :128]
            mixed_ref[pl.ds(at + 1, 8, stride=2), :] = tiles[b][:, 128:]


def mix(target, rademacher, design):
    height, breadth = design.shape
    return pl.pallas_call(
        mix_kernel,
        out_shape=(
            jax.ShapeDtypeStruct((2 * height, 128), F32),
            jax.ShapeDtypeStruct((8, 128), F32),
        ),
        in_specs=[VMEM] * 3,
        out_specs=(VMEM,) * 2,
        scratch_shapes=[pltpu.VMEM((height, breadth), F32)],
        compiler_params=pltpu.CompilerParams(vmem_limit_bytes=24 * 2**20),
        cost_estimate=cost(2**30, 2**23),
        name="mix",
    )(target, rademacher, design)


def pick_kernel(pos_ref, idx_ref, mixed_ref, back_ref, out_ref):
    per_owner = idx_ref.shape[2]
    owners = 128 // per_owner

    def one(piece, carry):
        for near in range(owners):
            owner = piece * owners + near
            odd = jnp.bitwise_and(owner, pos_ref[0])
            for shift in (4, 2, 1):
                odd = jnp.bitwise_xor(odd, jnp.right_shift(odd, shift))
            sign = (1 - 2 * jnp.bitwise_and(odd, 1)).astype(F32)
            for slot in range(per_owner):
                drawn = mixed_ref[idx_ref[owner, 0, slot]]
                out_ref[piece, near * per_owner + slot] = drawn * sign
        out_ref[piece, 128] = back_ref[0]
        return carry

    lax.fori_loop(0, out_ref.shape[0], one, 0)


def pick(position, drawn, mixed, back):
    return pl.pallas_call(
        pick_kernel,
        out_shape=jax.ShapeDtypeStruct((ZA * Y, 129, 2, 128), F32),
        in_specs=[SMEM] * 2 + [VMEM] * 2,
        out_specs=VMEM,
        compiler_params=pltpu.CompilerParams(vmem_limit_bytes=8 * 2**20),
        cost_estimate=cost(2**20, 2**21),
        name="pick",
    )(position, drawn, mixed, back)


def exchange(pieces, axes):
    return lax.all_to_all(pieces, axes, split_axis=0, concat_axis=0, tiled=True)


def share(value, axes, count):
    return exchange(jnp.broadcast_to(value[None], (count,) + value.shape), axes)


NB = 32


def spread_row(value, row):
    return jnp.broadcast_to(value[row : row + 1, :], (8, value.shape[1]))


def dot_nt(left, right):
    return lax.dot_general(left, right, (((1,), (1,)), ((), ())), preferred_element_type=F32)


def dot_tn(left, right):
    return lax.dot_general(left, right, (((0,), (0,)), ((), ())), preferred_element_type=F32)


def deal_kernel(parts_ref, out_ref):
    total = jnp.sum(parts_ref[...], axis=0)
    for copy in range(ZB):
        out_ref[copy, 0:16] = total[16 * copy : 16 * copy + 16]
        out_ref[copy, 16:17] = total[128:129]


def deal(parts):
    return pl.pallas_call(
        deal_kernel,
        out_shape=jax.ShapeDtypeStruct((ZB, 17, 2, 128), F32),
        in_specs=[VMEM],
        out_specs=VMEM,
        compiler_params=pltpu.CompilerParams(vmem_limit_bytes=8 * 2**20),
        name="deal",
    )(parts)


def fold_kernel(parts_ref, rows_ref, back_ref):
    total = jnp.sum(parts_ref[...], axis=0)
    for copy in range(ZB):
        rows_ref[copy] = total[0:16]
    back_ref[...] = total[16:17]


def fold(parts):
    return pl.pallas_call(
        fold_kernel,
        out_shape=(
            jax.ShapeDtypeStruct((ZB, 16, 2, 128), F32),
            jax.ShapeDtypeStruct((1, 2, 128), F32),
        ),
        in_specs=[VMEM],
        out_specs=(VMEM,) * 2,
        compiler_params=pltpu.CompilerParams(vmem_limit_bytes=4 * 2**20),
        name="fold",
    )(parts)


def gram_products(rows):
    hi, mid, lo = split3(rows)
    right = jnp.concatenate([hi, mid, hi, lo, hi, mid], axis=0)
    hi, mid, lo = split3(rows.T)
    left = jnp.concatenate([hi, hi, mid, hi, lo, mid], axis=1)
    top = jnp.dot(left[:128], right, preferred_element_type=F32)
    end = jnp.dot(left[128:], right[:, 128:], preferred_element_type=F32)
    return top[:, :128], top[:, 128:], end


def gram_kernel(rows_ref, out_ref):
    count = rows_ref.shape[0] // 2
    rows = [rows_ref[pl.ds(half, count, stride=2), :] for half in range(2)]
    first, corner, last = gram_products(jnp.concatenate(rows, axis=1))
    row = lax.broadcasted_iota(jnp.int32, (128, 128), 0)
    lane = lax.broadcasted_iota(jnp.int32, (128, 128), 1)
    mixed = jnp.where(row <= lane, first, last)
    diagonal = jnp.sum(jnp.where(row == lane, last, 0.0), axis=0, keepdims=True)
    for copy in range(ZA * Y):
        out_ref[copy, 0:128, :] = mixed
        out_ref[copy, 128:256, :] = corner
        out_ref[copy, 256:264, :] = jnp.broadcast_to(diagonal, (8, 128))


def gram(rows):
    return pl.pallas_call(
        gram_kernel,
        out_shape=jax.ShapeDtypeStruct((ZA * Y, 264, 128), F32),
        in_specs=[VMEM],
        out_specs=VMEM,
        cost_estimate=cost(2**27, 2**20),
        compiler_params=pltpu.CompilerParams(vmem_limit_bytes=4 * 2**20),
        name="gram",
    )(rows)


def factor_kernel(gram_ref, back_ref, seed_ref, slab_ref, image_ref, dir_ref, check_ref, work_ref):
    height, size = slab_ref.shape
    blocks = jnp.sum(gram_ref[...], axis=0)
    mixed, corner, diagonal = blocks[:128], blocks[128:256], blocks[256:257]
    turned = mixed.T
    row = lax.broadcasted_iota(jnp.int32, (128, 128), 0)
    lane = lax.broadcasted_iota(jnp.int32, (128, 128), 1)
    first = jnp.where(row <= lane, mixed, turned)
    last = jnp.where(row == lane, diagonal, jnp.where(row > lane, mixed, turned))
    gram = jnp.concatenate(
        [
            jnp.concatenate([first, corner], axis=1),
            jnp.concatenate([corner.T, last], axis=1),
        ],
        axis=0,
    )
    sub = lax.broadcasted_iota(jnp.int32, (128, size), 0)
    weights = seed_ref[...].astype(F32) * 0.0625
    weight_rows = jnp.where(sub == 1, jnp.broadcast_to(weights, (128, size)), 0.0).astype(BF16)
    back = jnp.concatenate([back_ref[0:1, :], back_ref[1:2, :]], axis=1)
    back_rows = jnp.where(sub == 0, jnp.broadcast_to(back, (128, size)), 0.0)
    eye = (
        lax.broadcasted_iota(jnp.int32, (size, size), 0)
        == lax.broadcasted_iota(jnp.int32, (size, size), 1)
    ).astype(BF16)
    extra = jnp.zeros((size, 128), F32)
    for term in split3(gram):
        extra = extra + dot_nt(term, weight_rows)
    for term in split3(back_rows):
        extra = extra + dot_nt(eye, term)
    work_ref[:, :size] = gram
    work_ref[:, size:] = extra

    wide = size + 128
    lane = lax.broadcasted_iota(jnp.int32, (NB, wide), 1)
    row = lax.broadcasted_iota(jnp.int32, (NB, wide), 0)
    half_row = lax.broadcasted_iota(jnp.int32, (8, 128), 0)
    wide_half = lax.broadcasted_iota(jnp.int32, (8, wide), 1)
    half_count = NB // 8
    tiles = wide // 128
    for block in range(size // NB):
        at = block * NB
        halves = [work_ref[at + 8 * h : at + 8 * h + 8, :] for h in range(half_count)]
        scales = [jnp.zeros((8, 128), F32)] * half_count
        for phase in range(2):
            base = 16 * phase
            begin = at + base
            cols = {
                (c, h): jnp.broadcast_to(halves[h][:, at + c : at + c + 1], (8, 128))
                for c in range(base, base + 16)
                for h in range(c // 8, half_count)
            }
            for h in range(2 * phase, half_count):
                unit = (wide_half - begin == half_row[:, :1] + (8 * h - base)).astype(F32)
                inside = (wide_half >= begin) & (wide_half < begin + 16)
                halves[h] = jnp.where(inside, unit, halves[h])
            pivot = spread_row(cols[base, base // 8], 0)
            for j in range(base, base + 16):
                inverse = 1.0 / pivot
                here = j // 8
                scales[here] = jnp.where(half_row == j % 8, pivot, scales[here])
                if j + 1 == NB:
                    break
                across = {
                    c: spread_row(cols[j, c // 8], c % 8) for c in range(j + 1, base + 16)
                }
                if j + 1 < base + 16:
                    pivot = (
                        spread_row(cols[j + 1, (j + 1) // 8], (j + 1) % 8)
                        - across[j + 1] * across[j + 1] * inverse
                    )
                source = jnp.tile(inverse, (1, tiles)) * spread_row(halves[here], j % 8)
                for h in range((j + 1) // 8, half_count):
                    below = cols[j, h]
                    if h == here:
                        below = jnp.where(half_row > j % 8, below, 0.0)
                    halves[h] = halves[h] - jnp.tile(below, (1, tiles)) * source
                    for c in range(j + 1, base + 16):
                        if c // 8 <= h:
                            cols[c, h] = cols[c, h] - below * (across[c] * inverse)
        panel = jnp.concatenate(
            [
                half * jnp.tile(lax.rsqrt(scale), (1, tiles))
                for half, scale in zip(halves, scales)
            ],
            axis=0,
        )
        work_ref[at : at + NB, :] = panel
        if at + NB < size:
            hi, mid, lo = split3(panel)
            zero = jnp.zeros((NB, size), BF16)
            keep = lane[:, :size] >= at + NB
            lhi, lmid, llo = [jnp.where(keep, term[:, :size], zero) for term in (hi, mid, lo)]
            left = jnp.concatenate([lhi, lhi, lmid, lhi, llo, lmid], axis=0)
            blank = (row < 16) & (lane >= at + 16) & (lane < at + NB)
            hi, mid, lo = [
                jnp.where(blank, jnp.zeros((NB, wide), BF16), term) for term in (hi, mid, lo)
            ]
            right = jnp.concatenate([hi, mid, hi, lo, hi, mid], axis=0)
            change = dot_tn(left, right)
            rest = size - at - NB
            wide_lane = lax.broadcasted_iota(jnp.int32, (rest, wide), 1)
            old = work_ref[at + NB :, :]
            old = jnp.where((wide_lane >= at) & (wide_lane < at + NB), 0.0, old)
            work_ref[at + NB :, :] = old - change[at + NB :, :]

    lower_inv = jnp.where(
        lax.broadcasted_iota(jnp.int32, (size, size), 0)
        >= lax.broadcasted_iota(jnp.int32, (size, size), 1),
        work_ref[:, :size],
        0.0,
    )
    half = work_ref[:, size : size + 1]
    check = work_ref[:, size + 1 : size + 2]
    direction = jnp.sum(lower_inv * half, axis=0, keepdims=True)
    diagonal = eye.astype(F32)
    check_ref[...] = jnp.sum(diagonal * check, axis=0, keepdims=True)
    dir_ref[...] = direction
    energy = jnp.sum(half * half, axis=0, keepdims=True)

    dhi, dmid, dlo = split3(direction)
    rows = jnp.concatenate([dhi, dmid, dlo, jnp.zeros((13, size), BF16)], axis=0)
    for part in range(height // 256):
        total = jnp.zeros((16, 256), F32)
        for term in split3(slab_ref[part * 256 : (part + 1) * 256, :]):
            total = total + dot_nt(rows, term)
        image = jnp.sum(total, axis=0, keepdims=True)
        for half in range(2):
            at = 2 * part + half
            image_ref[:, at : at + 1, :] = jnp.broadcast_to(
                image[None, :, half * 128 : (half + 1) * 128], (X * C, 1, 128)
            )
    image_ref[:, height // 128 :, :] = jnp.broadcast_to(energy[None], (X * C, 8, 128))


def factor(grams, back, seeds, design):
    height, breadth = design.shape
    return pl.pallas_call(
        factor_kernel,
        out_shape=(
            jax.ShapeDtypeStruct((X * C, height // 128 + 8, 128), F32),
            jax.ShapeDtypeStruct((1, breadth), F32),
            jax.ShapeDtypeStruct((1, breadth), F32),
        ),
        in_specs=[VMEM] * 4,
        out_specs=(VMEM,) * 3,
        scratch_shapes=[pltpu.VMEM((breadth, breadth + 128), F32)],
        compiler_params=pltpu.CompilerParams(vmem_limit_bytes=40 * 2**20),
        cost_estimate=cost(2**29, 2**22),
        name="factor",
    )(grams, back, seeds, design)


def merge_kernel(parts_ref, image_ref, energy_ref):
    image = jnp.sum(parts_ref[...], axis=0)
    image_ref[...] = image
    squares = jnp.sum(image[:-8] * image[:-8], axis=0, keepdims=True)
    energy = jnp.sum(squares, axis=1, keepdims=True)
    energy_ref[...] = jnp.broadcast_to(energy.reshape(1, 1, 1), energy_ref.shape)


def merge(parts):
    return pl.pallas_call(
        merge_kernel,
        out_shape=(
            jax.ShapeDtypeStruct(parts.shape[1:], F32),
            jax.ShapeDtypeStruct((SOURCES, 1, 128), F32),
        ),
        in_specs=[VMEM],
        out_specs=(VMEM,) * 2,
        compiler_params=pltpu.CompilerParams(vmem_limit_bytes=4 * 2**20),
        name="merge",
    )(parts)


def finish_kernel(energy_ref, image_ref, tgt_ref, dir_ref, sol_ref, res_ref):
    height = tgt_ref.shape[0]
    step = image_ref[height : height + 1, :] / jnp.sum(energy_ref[...], axis=0)
    sol_ref[...] = jnp.tile(step, (1, dir_ref.shape[1] // 128)) * dir_ref[...]
    res_ref[...] = tgt_ref[...] - step * image_ref[:height]


def finish(energies, image, target, direction):
    return pl.pallas_call(
        finish_kernel,
        out_shape=(
            jax.ShapeDtypeStruct(direction.shape, F32),
            jax.ShapeDtypeStruct(target.shape, F32),
        ),
        in_specs=[VMEM] * 4,
        out_specs=(VMEM,) * 2,
        compiler_params=pltpu.CompilerParams(vmem_limit_bytes=4 * 2**20),
        name="finish",
    )(energies, image, target, direction)


def body(design, rademacher, target, sample_rows, checksum_seeds):
    height, breadth = design.shape
    position = lax.axis_index(ROWS).astype(jnp.int32).reshape(1)
    drawn = share(sample_rows.reshape(1, 16), ROWS, SOURCES)
    mixed, back = mix(target.reshape(1, height), rademacher.reshape(1, height), design)
    near = pick(position, drawn, mixed.reshape(height, 2, 128), back.reshape(4, 2, 128))
    pieces = deal(exchange(near, NEAR))
    rows, back = fold(exchange(pieces, FAR))
    rows = exchange(rows.reshape(ZB, 32, 128), FAR).reshape(ZB * 32, 128)
    images, direction, checksum = factor(
        exchange(gram(rows), NEAR), back.reshape(2, 128), checksum_seeds.reshape(1, breadth), design
    )
    image, energy = merge(exchange(images, GRPS))
    solved, residual = finish(
        exchange(energy, ROWS), image, target.reshape(height // 128, 128), direction
    )
    return solved.reshape(breadth), residual.reshape(height), checksum.reshape(breadth)


def solution(mesh):
    fine = Mesh(mesh.devices.reshape(ZB, ZA, Y, X, C), ROWS + GRPS)
    in_specs = (P(ROWS, GRPS), P(ROWS), P(ROWS), P(ROWS, GRPS, None), P(GRPS))
    out_specs = (P(GRPS), P(ROWS), P(GRPS))
    return jax.shard_map(body, mesh=fine, in_specs=in_specs, out_specs=out_specs, check_vma=False)
```

```python
import functools

import jax
import jax.numpy as jnp
from jax import lax
from jax.experimental import pallas as pl
from jax.experimental.pallas import tpu as pltpu
from jax.sharding import Mesh, PartitionSpec as P

ZB, ZA, Y, X, C = 8, 2, 4, 4, 2
SOURCES = ZB * ZA * Y
FAR = "zb"
NEAR = ("za", "y")
ROWS = (FAR,) + NEAR
GRPS = ("x", "c")
F32 = jnp.float32
BF16 = jnp.bfloat16
VMEM = pl.BlockSpec(memory_space=pltpu.VMEM)
SMEM = pl.BlockSpec(memory_space=pltpu.SMEM)


def cost(flops, size):
    return pl.CostEstimate(flops=flops, bytes_accessed=size, transcendentals=0)


def parity_sign(bits):
    bits = jnp.bitwise_xor(bits, jnp.right_shift(bits, 8))
    bits = jnp.bitwise_xor(bits, jnp.right_shift(bits, 4))
    odd = jnp.bitwise_and(jnp.right_shift(0x6996, jnp.bitwise_and(bits, 15)), 1)
    return 1.0 - 2.0 * odd.astype(F32)


def split3(value):
    hi = value.astype(BF16)
    rest = value - hi.astype(F32)
    mid = rest.astype(BF16)
    lo = (rest - mid.astype(F32)).astype(BF16)
    return hi, mid, lo


def mix_kernel(tgt_ref, rad_ref, slab_ref, mixed_ref, back_ref, work_ref):
    height, breadth = slab_ref.shape
    block = 256
    blocks = height // block
    row = lax.broadcasted_iota(jnp.int32, (block, block), 0)
    lane = lax.broadcasted_iota(jnp.int32, (block, block), 1)
    table = parity_sign(jnp.bitwise_and(row, lane)) * 0.03125
    rows = jnp.concatenate(list(split3(tgt_ref[...])) + [jnp.zeros((13, height), BF16)], axis=0)
    back = jnp.zeros((16, breadth), F32)
    for place in range(blocks):
        at = place * block
        sign = 1.0 - 2.0 * rad_ref[:, at : at + block].astype(F32)
        left = (table * sign).astype(BF16)
        total = jnp.zeros((block, breadth), F32)
        for term in split3(slab_ref[at : at + block, :]):
            total = total + jnp.dot(left, term, preferred_element_type=F32)
            back = back + jnp.dot(rows[:, at : at + block], term, preferred_element_type=F32)
        work_ref[at : at + block, :] = total
    back = jnp.sum(back, axis=0, keepdims=True)
    for copy in range(4):
        back_ref[2 * copy : 2 * copy + 1, :] = back[:, :128]
        back_ref[2 * copy + 1 : 2 * copy + 2, :] = back[:, 128:]
    for chunk in range(block // 8):
        tiles = [work_ref[b * block + chunk * 8 : b * block + chunk * 8 + 8, :] for b in range(blocks)]
        stride = 1
        while stride < blocks:
            tiles = [
                tiles[b] + tiles[b ^ stride] if b & stride == 0 else tiles[b ^ stride] - tiles[b]
                for b in range(blocks)
            ]
            stride *= 2
        for b in range(blocks):
            at = 2 * (b * block + chunk * 8)
            mixed_ref[pl.ds(at, 8, stride=2), :] = tiles[b][:, :128]
            mixed_ref[pl.ds(at + 1, 8, stride=2), :] = tiles[b][:, 128:]


def mix(target, rademacher, design):
    height, breadth = design.shape
    return pl.pallas_call(
        mix_kernel,
        out_shape=(
            jax.ShapeDtypeStruct((2 * height, 128), F32),
            jax.ShapeDtypeStruct((8, 128), F32),
        ),
        in_specs=[VMEM] * 3,
        out_specs=(VMEM,) * 2,
        scratch_shapes=[pltpu.VMEM((height, breadth), F32)],
        compiler_params=pltpu.CompilerParams(vmem_limit_bytes=24 * 2**20),
        cost_estimate=cost(2**30, 2**23),
        name="mix",
    )(target, rademacher, design)


def pick_kernel(pos_ref, idx_ref, mixed_ref, back_ref, out_ref):
    per_owner = idx_ref.shape[2]
    owners = 128 // per_owner

    def one(piece, carry):
        for near in range(owners):
            owner = piece * owners + near
            odd = jnp.bitwise_and(owner, pos_ref[0])
            for shift in (4, 2, 1):
                odd = jnp.bitwise_xor(odd, jnp.right_shift(odd, shift))
            sign = (1 - 2 * jnp.bitwise_and(odd, 1)).astype(F32)
            for slot in range(per_owner):
                drawn = mixed_ref[idx_ref[owner, 0, slot]]
                out_ref[piece, near * per_owner + slot] = drawn * sign
        out_ref[piece, 128] = back_ref[0]
        return carry

    lax.fori_loop(0, out_ref.shape[0], one, 0)


def pick(position, drawn, mixed, back):
    return pl.pallas_call(
        pick_kernel,
        out_shape=jax.ShapeDtypeStruct((ZA * Y, 129, 2, 128), F32),
        in_specs=[SMEM] * 2 + [VMEM] * 2,
        out_specs=VMEM,
        compiler_params=pltpu.CompilerParams(vmem_limit_bytes=8 * 2**20),
        cost_estimate=cost(2**20, 2**21),
        name="pick",
    )(position, drawn, mixed, back)


def exchange(pieces, axes):
    return lax.all_to_all(pieces, axes, split_axis=0, concat_axis=0, tiled=True)


def share(value, axes, count):
    return exchange(jnp.broadcast_to(value[None], (count,) + value.shape), axes)


NB = 32


def spread_row(value, row):
    return jnp.broadcast_to(value[row : row + 1, :], (8, value.shape[1]))


def dot_nt(left, right):
    return lax.dot_general(left, right, (((1,), (1,)), ((), ())), preferred_element_type=F32)


def dot_tn(left, right):
    return lax.dot_general(left, right, (((0,), (0,)), ((), ())), preferred_element_type=F32)


def deal_kernel(parts_ref, out_ref):
    total = jnp.sum(parts_ref[...], axis=0)
    for copy in range(ZB):
        out_ref[copy, 0:16] = total[16 * copy : 16 * copy + 16]
        out_ref[copy, 16:17] = total[128:129]


def deal(parts):
    return pl.pallas_call(
        deal_kernel,
        out_shape=jax.ShapeDtypeStruct((ZB, 17, 2, 128), F32),
        in_specs=[VMEM],
        out_specs=VMEM,
        compiler_params=pltpu.CompilerParams(vmem_limit_bytes=8 * 2**20),
        name="deal",
    )(parts)


def fold_kernel(parts_ref, rows_ref, back_ref):
    total = jnp.sum(parts_ref[...], axis=0)
    for copy in range(ZB):
        rows_ref[copy] = total[0:16]
    back_ref[...] = total[16:17]


def fold(parts):
    return pl.pallas_call(
        fold_kernel,
        out_shape=(
            jax.ShapeDtypeStruct((ZB, 16, 2, 128), F32),
            jax.ShapeDtypeStruct((1, 2, 128), F32),
        ),
        in_specs=[VMEM],
        out_specs=(VMEM,) * 2,
        compiler_params=pltpu.CompilerParams(vmem_limit_bytes=4 * 2**20),
        name="fold",
    )(parts)


def gram_products(rows):
    hi, mid, lo = split3(rows)
    right = jnp.concatenate([hi, mid, hi, lo, hi, mid], axis=0)
    hi, mid, lo = split3(rows.T)
    left = jnp.concatenate([hi, hi, mid, hi, lo, mid], axis=1)
    top = jnp.dot(left[:128], right, preferred_element_type=F32)
    end = jnp.dot(left[128:], right[:, 128:], preferred_element_type=F32)
    return top[:, :128], top[:, 128:], end


def gram_kernel(rows_ref, out_ref):
    count = rows_ref.shape[0] // 2
    rows = [rows_ref[pl.ds(half, count, stride=2), :] for half in range(2)]
    first, corner, last = gram_products(jnp.concatenate(rows, axis=1))
    row = lax.broadcasted_iota(jnp.int32, (128, 128), 0)
    lane = lax.broadcasted_iota(jnp.int32, (128, 128), 1)
    mixed = jnp.where(row <= lane, first, last)
    diagonal = jnp.sum(jnp.where(row == lane, last, 0.0), axis=0, keepdims=True)
    for copy in range(ZA * Y):
        out_ref[copy, 0:128, :] = mixed
        out_ref[copy, 128:256, :] = corner
        out_ref[copy, 256:264, :] = jnp.broadcast_to(diagonal, (8, 128))


def gram(rows):
    return pl.pallas_call(
        gram_kernel,
        out_shape=jax.ShapeDtypeStruct((ZA * Y, 264, 128), F32),
        in_specs=[VMEM],
        out_specs=VMEM,
        cost_estimate=cost(2**27, 2**20),
        compiler_params=pltpu.CompilerParams(vmem_limit_bytes=4 * 2**20),
        name="gram",
    )(rows)


def factor_kernel(gram_ref, back_ref, seed_ref, slab_ref, image_ref, dir_ref, check_ref, work_ref):
    height, size = slab_ref.shape
    blocks = jnp.sum(gram_ref[...], axis=0)
    mixed, corner, diagonal = blocks[:128], blocks[128:256], blocks[256:257]
    turned = mixed.T
    row = lax.broadcasted_iota(jnp.int32, (128, 128), 0)
    lane = lax.broadcasted_iota(jnp.int32, (128, 128), 1)
    first = jnp.where(row <= lane, mixed, turned)
    last = jnp.where(row == lane, diagonal, jnp.where(row > lane, mixed, turned))
    gram = jnp.concatenate(
        [
            jnp.concatenate([first, corner], axis=1),
            jnp.concatenate([corner.T, last], axis=1),
        ],
        axis=0,
    )
    sub = lax.broadcasted_iota(jnp.int32, (128, size), 0)
    weights = seed_ref[...].astype(F32) * 0.0625
    weight_rows = jnp.where(sub == 1, jnp.broadcast_to(weights, (128, size)), 0.0).astype(BF16)
    back = jnp.concatenate([back_ref[0:1, :], back_ref[1:2, :]], axis=1)
    back_rows = jnp.where(sub == 0, jnp.broadcast_to(back, (128, size)), 0.0)
    eye = (
        lax.broadcasted_iota(jnp.int32, (size, size), 0)
        == lax.broadcasted_iota(jnp.int32, (size, size), 1)
    ).astype(BF16)
    extra = jnp.zeros((size, 128), F32)
    for term in split3(gram):
        extra = extra + dot_nt(term, weight_rows)
    for term in split3(back_rows):
        extra = extra + dot_nt(eye, term)
    work_ref[:, :size] = gram
    work_ref[:, size:] = extra

    wide = size + 128
    lane = lax.broadcasted_iota(jnp.int32, (NB, wide), 1)
    row = lax.broadcasted_iota(jnp.int32, (NB, wide), 0)
    half_row = lax.broadcasted_iota(jnp.int32, (8, 128), 0)
    wide_half = lax.broadcasted_iota(jnp.int32, (8, wide), 1)
    half_count = NB // 8
    tiles = wide // 128
    for block in range(size // NB):
        at = block * NB
        halves = [work_ref[at + 8 * h : at + 8 * h + 8, :] for h in range(half_count)]
        scales = [jnp.zeros((8, 128), F32)] * half_count
        for phase in range(2):
            base = 16 * phase
            begin = at + base
            cols = {
                (c, h): jnp.broadcast_to(halves[h][:, at + c : at + c + 1], (8, 128))
                for c in range(base, base + 16)
                for h in range(c // 8, half_count)
            }
            for h in range(2 * phase, half_count):
                unit = (wide_half - begin == half_row[:, :1] + (8 * h - base)).astype(F32)
                inside = (wide_half >= begin) & (wide_half < begin + 16)
                halves[h] = jnp.where(inside, unit, halves[h])

            def entry(i, j):
                return spread_row(cols[j, i // 8], i % 8)

            guards = {
                j: pl.reciprocal(entry(j, j), approx=True) for j in range(base, base + 16, 2)
            }
            first = [entry(base, base), entry(base + 1, base), entry(base + 1, base + 1)]
            for j in range(base, base + 16, 2):
                k, here = j + 1, j // 8
                aa, ab, bb = first
                part = aa * guards[j]
                scaled = bb * part - ab * (ab * guards[j])
                inverse = 1.0 / aa
                second = part * (1.0 / scaled)
                slope = ab * inverse
                scales[here] = jnp.where(half_row == j % 8, inverse, scales[here])
                scales[here] = jnp.where(half_row == k % 8, second, scales[here])
                later = range(k + 1, base + 16)
                left = {c: entry(c, j) for c in later}
                down = {c: entry(c, k) - slope * left[c] for c in later}
                if k + 1 < base + 16:
                    m, n = k + 1, k + 2
                    first = [
                        (entry(q, p) - left[p] * left[q] * inverse) - down[p] * down[q] * second
                        for p, q in ((m, m), (m, n), (n, n))
                    ]
                left = {c: left[c] * inverse for c in later}
                down = {c: down[c] * second for c in later}
                source = jnp.tile(inverse, (1, tiles)) * spread_row(halves[here], j % 8)
                other = spread_row(halves[here], k % 8) - jnp.tile(ab, (1, tiles)) * source
                other = jnp.tile(second, (1, tiles)) * other
                for h in range(here, half_count):
                    below = cols[j, h]
                    if h == here:
                        below = jnp.where(half_row > j % 8, below, 0.0)
                    lower = cols[k, h] - below * slope
                    if h == here:
                        lower = jnp.where(half_row > k % 8, lower, 0.0)
                    halves[h] = halves[h] - jnp.tile(below, (1, tiles)) * source
                    halves[h] = halves[h] - jnp.tile(lower, (1, tiles)) * other
                    for c in later:
                        if c // 8 <= h:
                            cols[c, h] = cols[c, h] - below * left[c] - lower * down[c]
        panel = jnp.concatenate(
            [
                half * jnp.tile(jnp.sqrt(scale), (1, tiles))
                for half, scale in zip(halves, scales)
            ],
            axis=0,
        )
        work_ref[at : at + NB, :] = panel
        if at + NB < size:
            hi, mid, lo = split3(panel)
            zero = jnp.zeros((NB, size), BF16)
            keep = lane[:, :size] >= at + NB
            lhi, lmid, llo = [jnp.where(keep, term[:, :size], zero) for term in (hi, mid, lo)]
            left = jnp.concatenate([lhi, lhi, lmid, lhi, llo, lmid], axis=0)
            blank = (row < 16) & (lane >= at + 16) & (lane < at + NB)
            hi, mid, lo = [
                jnp.where(blank, jnp.zeros((NB, wide), BF16), term) for term in (hi, mid, lo)
            ]
            right = jnp.concatenate([hi, mid, hi, lo, hi, mid], axis=0)
            change = dot_tn(left, right)
            rest = size - at - NB
            wide_lane = lax.broadcasted_iota(jnp.int32, (rest, wide), 1)
            old = work_ref[at + NB :, :]
            old = jnp.where((wide_lane >= at) & (wide_lane < at + NB), 0.0, old)
            work_ref[at + NB :, :] = old - change[at + NB :, :]

    lower_inv = jnp.where(
        lax.broadcasted_iota(jnp.int32, (size, size), 0)
        >= lax.broadcasted_iota(jnp.int32, (size, size), 1),
        work_ref[:, :size],
        0.0,
    )
    half = work_ref[:, size : size + 1]
    check = work_ref[:, size + 1 : size + 2]
    direction = jnp.sum(lower_inv * half, axis=0, keepdims=True)
    diagonal = eye.astype(F32)
    check_ref[...] = jnp.sum(diagonal * check, axis=0, keepdims=True)
    dir_ref[...] = direction
    energy = jnp.sum(half * half, axis=0, keepdims=True)

    dhi, dmid, dlo = split3(direction)
    rows = jnp.concatenate([dhi, dmid, dlo, jnp.zeros((13, size), BF16)], axis=0)
    for part in range(height // 256):
        total = jnp.zeros((16, 256), F32)
        for term in split3(slab_ref[part * 256 : (part + 1) * 256, :]):
            total = total + dot_nt(rows, term)
        image = jnp.sum(total, axis=0, keepdims=True)
        for half in range(2):
            at = 2 * part + half
            image_ref[:, at : at + 1, :] = jnp.broadcast_to(
                image[None, :, half * 128 : (half + 1) * 128], (X * C, 1, 128)
            )
    image_ref[:, height // 128 :, :] = jnp.broadcast_to(energy[None], (X * C, 8, 128))


def factor(grams, back, seeds, design):
    height, breadth = design.shape
    return pl.pallas_call(
        factor_kernel,
        out_shape=(
            jax.ShapeDtypeStruct((X * C, height // 128 + 8, 128), F32),
            jax.ShapeDtypeStruct((1, breadth), F32),
            jax.ShapeDtypeStruct((1, breadth), F32),
        ),
        in_specs=[VMEM] * 4,
        out_specs=(VMEM,) * 3,
        scratch_shapes=[pltpu.VMEM((breadth, breadth + 128), F32)],
        compiler_params=pltpu.CompilerParams(vmem_limit_bytes=40 * 2**20),
        cost_estimate=cost(2**29, 2**22),
        name="factor",
    )(grams, back, seeds, design)


def merge_kernel(parts_ref, image_ref, energy_ref):
    image = jnp.sum(parts_ref[...], axis=0)
    image_ref[...] = image
    squares = jnp.sum(image[:-8] * image[:-8], axis=0, keepdims=True)
    energy = jnp.sum(squares, axis=1, keepdims=True)
    energy_ref[...] = jnp.broadcast_to(energy.reshape(1, 1, 1), energy_ref.shape)


def merge(parts):
    return pl.pallas_call(
        merge_kernel,
        out_shape=(
            jax.ShapeDtypeStruct(parts.shape[1:], F32),
            jax.ShapeDtypeStruct((SOURCES, 1, 128), F32),
        ),
        in_specs=[VMEM],
        out_specs=(VMEM,) * 2,
        compiler_params=pltpu.CompilerParams(vmem_limit_bytes=4 * 2**20),
        name="merge",
    )(parts)


def finish_kernel(energy_ref, image_ref, tgt_ref, dir_ref, sol_ref, res_ref):
    height = tgt_ref.shape[0]
    step = image_ref[height : height + 1, :] / jnp.sum(energy_ref[...], axis=0)
    sol_ref[...] = jnp.tile(step, (1, dir_ref.shape[1] // 128)) * dir_ref[...]
    res_ref[...] = tgt_ref[...] - step * image_ref[:height]


def finish(energies, image, target, direction):
    return pl.pallas_call(
        finish_kernel,
        out_shape=(
            jax.ShapeDtypeStruct(direction.shape, F32),
            jax.ShapeDtypeStruct(target.shape, F32),
        ),
        in_specs=[VMEM] * 4,
        out_specs=(VMEM,) * 2,
        compiler_params=pltpu.CompilerParams(vmem_limit_bytes=4 * 2**20),
        name="finish",
    )(energies, image, target, direction)


def body(design, rademacher, target, sample_rows, checksum_seeds):
    height, breadth = design.shape
    position = lax.axis_index(ROWS).astype(jnp.int32).reshape(1)
    drawn = share(sample_rows.reshape(1, 16), ROWS, SOURCES)
    mixed, back = mix(target.reshape(1, height), rademacher.reshape(1, height), design)
    near = pick(position, drawn, mixed.reshape(height, 2, 128), back.reshape(4, 2, 128))
    pieces = deal(exchange(near, NEAR))
    rows, back = fold(exchange(pieces, FAR))
    rows = exchange(rows.reshape(ZB, 32, 128), FAR).reshape(ZB * 32, 128)
    images, direction, checksum = factor(
        exchange(gram(rows), NEAR), back.reshape(2, 128), checksum_seeds.reshape(1, breadth), design
    )
    image, energy = merge(exchange(images, GRPS))
    solved, residual = finish(
        exchange(energy, ROWS), image, target.reshape(height // 128, 128), direction
    )
    return solved.reshape(breadth), residual.reshape(height), checksum.reshape(breadth)


def solution(mesh):
    fine = Mesh(mesh.devices.reshape(ZB, ZA, Y, X, C), ROWS + GRPS)
    in_specs = (P(ROWS, GRPS), P(ROWS), P(ROWS), P(ROWS, GRPS, None), P(GRPS))
    out_specs = (P(GRPS), P(ROWS), P(GRPS))
    return jax.shard_map(body, mesh=fine, in_specs=in_specs, out_specs=out_specs, check_vma=False)
```

```python
import functools

import jax
import jax.numpy as jnp
from jax import lax
from jax.experimental import pallas as pl
from jax.experimental.pallas import tpu as pltpu
from jax.sharding import Mesh, PartitionSpec as P

ZB, ZA, Y, X, C = 8, 2, 4, 4, 2
SOURCES = ZB * ZA * Y
FAR = "zb"
NEAR = ("za", "y")
ROWS = (FAR,) + NEAR
GRPS = ("x", "c")
F32 = jnp.float32
BF16 = jnp.bfloat16
VMEM = pl.BlockSpec(memory_space=pltpu.VMEM)
SMEM = pl.BlockSpec(memory_space=pltpu.SMEM)


def cost(flops, size):
    return pl.CostEstimate(flops=flops, bytes_accessed=size, transcendentals=0)


def parity_sign(bits):
    bits = jnp.bitwise_xor(bits, jnp.right_shift(bits, 8))
    bits = jnp.bitwise_xor(bits, jnp.right_shift(bits, 4))
    odd = jnp.bitwise_and(jnp.right_shift(0x6996, jnp.bitwise_and(bits, 15)), 1)
    return 1.0 - 2.0 * odd.astype(F32)


def split3(value):
    hi = value.astype(BF16)
    rest = value - hi.astype(F32)
    mid = rest.astype(BF16)
    lo = (rest - mid.astype(F32)).astype(BF16)
    return hi, mid, lo


def mix_kernel(tgt_ref, rad_ref, slab_ref, mixed_ref, back_ref, work_ref):
    height, breadth = slab_ref.shape
    block = 256
    blocks = height // block
    row = lax.broadcasted_iota(jnp.int32, (block, block), 0)
    lane = lax.broadcasted_iota(jnp.int32, (block, block), 1)
    table = parity_sign(jnp.bitwise_and(row, lane)) * 0.03125
    rows = jnp.concatenate(list(split3(tgt_ref[...])) + [jnp.zeros((13, height), BF16)], axis=0)
    back = jnp.zeros((16, breadth), F32)
    for place in range(blocks):
        at = place * block
        sign = 1.0 - 2.0 * rad_ref[:, at : at + block].astype(F32)
        left = (table * sign).astype(BF16)
        total = jnp.zeros((block, breadth), F32)
        for term in split3(slab_ref[at : at + block, :]):
            total = total + jnp.dot(left, term, preferred_element_type=F32)
            back = back + jnp.dot(rows[:, at : at + block], term, preferred_element_type=F32)
        work_ref[at : at + block, :] = total
    back = jnp.sum(back, axis=0, keepdims=True)
    for copy in range(4):
        back_ref[2 * copy : 2 * copy + 1, :] = back[:, :128]
        back_ref[2 * copy + 1 : 2 * copy + 2, :] = back[:, 128:]
    for chunk in range(block // 8):
        tiles = [work_ref[b * block + chunk * 8 : b * block + chunk * 8 + 8, :] for b in range(blocks)]
        stride = 1
        while stride < blocks:
            tiles = [
                tiles[b] + tiles[b ^ stride] if b & stride == 0 else tiles[b ^ stride] - tiles[b]
                for b in range(blocks)
            ]
            stride *= 2
        for b in range(blocks):
            at = 2 * (b * block + chunk * 8)
            mixed_ref[pl.ds(at, 8, stride=2), :] = tiles[b][:, :128]
            mixed_ref[pl.ds(at + 1, 8, stride=2), :] = tiles[b][:, 128:]


def mix(target, rademacher, design):
    height, breadth = design.shape
    return pl.pallas_call(
        mix_kernel,
        out_shape=(
            jax.ShapeDtypeStruct((2 * height, 128), F32),
            jax.ShapeDtypeStruct((8, 128), F32),
        ),
        in_specs=[VMEM] * 3,
        out_specs=(VMEM,) * 2,
        scratch_shapes=[pltpu.VMEM((height, breadth), F32)],
        compiler_params=pltpu.CompilerParams(vmem_limit_bytes=24 * 2**20),
        cost_estimate=cost(2**30, 2**23),
        name="mix",
    )(target, rademacher, design)


def pick_kernel(pos_ref, idx_ref, mixed_ref, back_ref, out_ref):
    per_owner = idx_ref.shape[2]
    owners = 128 // per_owner

    def one(piece, carry):
        for near in range(owners):
            owner = piece * owners + near
            odd = jnp.bitwise_and(owner, pos_ref[0])
            for shift in (4, 2, 1):
                odd = jnp.bitwise_xor(odd, jnp.right_shift(odd, shift))
            sign = (1 - 2 * jnp.bitwise_and(odd, 1)).astype(F32)
            for slot in range(per_owner):
                drawn = mixed_ref[idx_ref[owner, 0, slot]]
                out_ref[piece, near * per_owner + slot] = drawn * sign
        out_ref[piece, 128] = back_ref[0]
        return carry

    lax.fori_loop(0, out_ref.shape[0], one, 0)


def pick(position, drawn, mixed, back):
    return pl.pallas_call(
        pick_kernel,
        out_shape=jax.ShapeDtypeStruct((ZA * Y, 129, 2, 128), F32),
        in_specs=[SMEM] * 2 + [VMEM] * 2,
        out_specs=VMEM,
        compiler_params=pltpu.CompilerParams(vmem_limit_bytes=8 * 2**20),
        cost_estimate=cost(2**20, 2**21),
        name="pick",
    )(position, drawn, mixed, back)


def exchange(pieces, axes):
    return lax.all_to_all(pieces, axes, split_axis=0, concat_axis=0, tiled=True)


def share(value, axes, count):
    return exchange(jnp.broadcast_to(value[None], (count,) + value.shape), axes)


NB = 32


def spread_row(value, row):
    return jnp.broadcast_to(value[row : row + 1, :], (8, value.shape[1]))


def dot_nt(left, right):
    return lax.dot_general(left, right, (((1,), (1,)), ((), ())), preferred_element_type=F32)


def dot_tn(left, right):
    return lax.dot_general(left, right, (((0,), (0,)), ((), ())), preferred_element_type=F32)


def deal_kernel(parts_ref, out_ref):
    total = jnp.sum(parts_ref[...], axis=0)
    for copy in range(ZB):
        out_ref[copy, 0:16] = total[16 * copy : 16 * copy + 16]
        out_ref[copy, 16:17] = total[128:129]


def deal(parts):
    return pl.pallas_call(
        deal_kernel,
        out_shape=jax.ShapeDtypeStruct((ZB, 17, 2, 128), F32),
        in_specs=[VMEM],
        out_specs=VMEM,
        compiler_params=pltpu.CompilerParams(vmem_limit_bytes=8 * 2**20),
        name="deal",
    )(parts)


def fold_kernel(parts_ref, rows_ref, back_ref):
    total = jnp.sum(parts_ref[...], axis=0)
    for copy in range(ZB):
        rows_ref[copy] = total[0:16]
    back_ref[...] = total[16:17]


def fold(parts):
    return pl.pallas_call(
        fold_kernel,
        out_shape=(
            jax.ShapeDtypeStruct((ZB, 16, 2, 128), F32),
            jax.ShapeDtypeStruct((1, 2, 128), F32),
        ),
        in_specs=[VMEM],
        out_specs=(VMEM,) * 2,
        compiler_params=pltpu.CompilerParams(vmem_limit_bytes=4 * 2**20),
        name="fold",
    )(parts)


def gram_products(rows):
    hi, mid, lo = split3(rows)
    right = jnp.concatenate([hi, mid, hi, lo, hi, mid], axis=0)
    hi, mid, lo = split3(rows.T)
    left = jnp.concatenate([hi, hi, mid, hi, lo, mid], axis=1)
    top = jnp.dot(left[:128], right, preferred_element_type=F32)
    end = jnp.dot(left[128:], right[:, 128:], preferred_element_type=F32)
    return top[:, :128], top[:, 128:], end


def gram_kernel(rows_ref, out_ref):
    count = rows_ref.shape[0] // 2
    rows = [rows_ref[pl.ds(half, count, stride=2), :] for half in range(2)]
    first, corner, last = gram_products(jnp.concatenate(rows, axis=1))
    row = lax.broadcasted_iota(jnp.int32, (128, 128), 0)
    lane = lax.broadcasted_iota(jnp.int32, (128, 128), 1)
    mixed = jnp.where(row <= lane, first, last)
    diagonal = jnp.sum(jnp.where(row == lane, last, 0.0), axis=0, keepdims=True)
    for copy in range(ZA * Y):
        out_ref[copy, 0:128, :] = mixed
        out_ref[copy, 128:256, :] = corner
        out_ref[copy, 256:264, :] = jnp.broadcast_to(diagonal, (8, 128))


def gram(rows):
    return pl.pallas_call(
        gram_kernel,
        out_shape=jax.ShapeDtypeStruct((ZA * Y, 264, 128), F32),
        in_specs=[VMEM],
        out_specs=VMEM,
        cost_estimate=cost(2**27, 2**20),
        compiler_params=pltpu.CompilerParams(vmem_limit_bytes=4 * 2**20),
        name="gram",
    )(rows)


def factor_kernel(gram_ref, back_ref, seed_ref, slab_ref, image_ref, dir_ref, check_ref, work_ref):
    height, size = slab_ref.shape
    blocks = jnp.sum(gram_ref[...], axis=0)
    mixed, corner, diagonal = blocks[:128], blocks[128:256], blocks[256:257]
    turned = mixed.T
    row = lax.broadcasted_iota(jnp.int32, (128, 128), 0)
    lane = lax.broadcasted_iota(jnp.int32, (128, 128), 1)
    first = jnp.where(row <= lane, mixed, turned)
    last = jnp.where(row == lane, diagonal, jnp.where(row > lane, mixed, turned))
    gram = jnp.concatenate(
        [
            jnp.concatenate([first, corner], axis=1),
            jnp.concatenate([corner.T, last], axis=1),
        ],
        axis=0,
    )
    sub = lax.broadcasted_iota(jnp.int32, (128, size), 0)
    weights = seed_ref[...].astype(F32) * 0.0625
    weight_rows = jnp.where(sub == 1, jnp.broadcast_to(weights, (128, size)), 0.0).astype(BF16)
    back = jnp.concatenate([back_ref[0:1, :], back_ref[1:2, :]], axis=1)
    back_rows = jnp.where(sub == 0, jnp.broadcast_to(back, (128, size)), 0.0)
    eye = (
        lax.broadcasted_iota(jnp.int32, (size, size), 0)
        == lax.broadcasted_iota(jnp.int32, (size, size), 1)
    ).astype(BF16)
    extra = jnp.zeros((size, 128), F32)
    for term in split3(gram):
        extra = extra + dot_nt(term, weight_rows)
    for term in split3(back_rows):
        extra = extra + dot_nt(eye, term)
    work_ref[:, :size] = gram
    work_ref[:, size:] = extra

    wide = size + 128
    lane = lax.broadcasted_iota(jnp.int32, (NB, wide), 1)
    row = lax.broadcasted_iota(jnp.int32, (NB, wide), 0)
    half_row = lax.broadcasted_iota(jnp.int32, (8, 128), 0)
    wide_half = lax.broadcasted_iota(jnp.int32, (8, wide), 1)
    half_count = NB // 8
    tiles = wide // 128
    for block in range(size // NB):
        at = block * NB
        halves = [work_ref[at + 8 * h : at + 8 * h + 8, :] for h in range(half_count)]
        scales = [jnp.zeros((8, 128), F32)] * half_count
        for phase in range(2):
            base = 16 * phase
            begin = at + base
            cols = {
                (c, h): jnp.broadcast_to(halves[h][:, at + c : at + c + 1], (8, 128))
                for c in range(base, base + 16)
                for h in range(c // 8, half_count)
            }
            for h in range(2 * phase, half_count):
                unit = (wide_half - begin == half_row[:, :1] + (8 * h - base)).astype(F32)
                inside = (wide_half >= begin) & (wide_half < begin + 16)
                halves[h] = jnp.where(inside, unit, halves[h])
            pivot = spread_row(cols[base, base // 8], 0)
            for j in range(base, base + 16):
                inverse = 1.0 / pivot
                here = j // 8
                scales[here] = jnp.where(half_row == j % 8, pivot, scales[here])
                if j + 1 == NB:
                    break
                across = {
                    c: spread_row(cols[j, c // 8], c % 8) for c in range(j + 1, base + 16)
                }
                if j + 1 < base + 16:
                    pivot = (
                        spread_row(cols[j + 1, (j + 1) // 8], (j + 1) % 8)
                        - across[j + 1] * across[j + 1] * inverse
                    )
                source = spread_row(halves[here], j % 8)
                for h in range((j + 1) // 8, half_count):
                    below = cols[j, h] * inverse
                    if h == here:
                        below = jnp.where(half_row > j % 8, below, 0.0)
                    halves[h] = halves[h] - jnp.tile(below, (1, tiles)) * source
                    for c in range(j + 1, base + 16):
                        if c // 8 <= h:
                            cols[c, h] = cols[c, h] - below * across[c]
        panel = jnp.concatenate(
            [
                half * jnp.tile(lax.rsqrt(scale), (1, tiles))
                for half, scale in zip(halves, scales)
            ],
            axis=0,
        )
        work_ref[at : at + NB, :] = panel
        if at + NB < size:
            hi, mid, lo = split3(panel)
            zero = jnp.zeros((NB, size), BF16)
            keep = lane[:, :size] >= at + NB
            lhi, lmid, llo = [jnp.where(keep, term[:, :size], zero) for term in (hi, mid, lo)]
            left = jnp.concatenate([lhi, lhi, lmid, lhi, llo, lmid], axis=0)
            blank = (row < 16) & (lane >= at + 16) & (lane < at + NB)
            hi, mid, lo = [
                jnp.where(blank, jnp.zeros((NB, wide), BF16), term) for term in (hi, mid, lo)
            ]
            right = jnp.concatenate([hi, mid, hi, lo, hi, mid], axis=0)
            change = dot_tn(left, right)
            rest = size - at - NB
            wide_lane = lax.broadcasted_iota(jnp.int32, (rest, wide), 1)
            old = work_ref[at + NB :, :]
            old = jnp.where((wide_lane >= at) & (wide_lane < at + NB), 0.0, old)
            work_ref[at + NB :, :] = old - change[at + NB :, :]

    lower_inv = jnp.where(
        lax.broadcasted_iota(jnp.int32, (size, size), 0)
        >= lax.broadcasted_iota(jnp.int32, (size, size), 1),
        work_ref[:, :size],
        0.0,
    )
    half = work_ref[:, size : size + 1]
    check = work_ref[:, size + 1 : size + 2]
    direction = jnp.sum(lower_inv * half, axis=0, keepdims=True)
    diagonal = eye.astype(F32)
    check_ref[...] = jnp.sum(diagonal * check, axis=0, keepdims=True)
    dir_ref[...] = direction
    energy = jnp.sum(half * half, axis=0, keepdims=True)

    dhi, dmid, dlo = split3(direction)
    rows = jnp.concatenate([dhi, dmid, dlo, jnp.zeros((13, size), BF16)], axis=0)
    for part in range(height // 256):
        total = jnp.zeros((16, 256), F32)
        for term in split3(slab_ref[part * 256 : (part + 1) * 256, :]):
            total = total + dot_nt(rows, term)
        image = jnp.sum(total, axis=0, keepdims=True)
        for half in range(2):
            at = 2 * part + half
            image_ref[:, at : at + 1, :] = jnp.broadcast_to(
                image[None, :, half * 128 : (half + 1) * 128], (X * C, 1, 128)
            )
    image_ref[:, height // 128 :, :] = jnp.broadcast_to(energy[None], (X * C, 8, 128))


def factor(grams, back, seeds, design):
    height, breadth = design.shape
    return pl.pallas_call(
        factor_kernel,
        out_shape=(
            jax.ShapeDtypeStruct((X * C, height // 128 + 8, 128), F32),
            jax.ShapeDtypeStruct((1, breadth), F32),
            jax.ShapeDtypeStruct((1, breadth), F32),
        ),
        in_specs=[VMEM] * 4,
        out_specs=(VMEM,) * 3,
        scratch_shapes=[pltpu.VMEM((breadth, breadth + 128), F32)],
        compiler_params=pltpu.CompilerParams(vmem_limit_bytes=40 * 2**20),
        cost_estimate=cost(2**29, 2**22),
        name="factor",
    )(grams, back, seeds, design)


def merge_kernel(parts_ref, image_ref, energy_ref):
    image = jnp.sum(parts_ref[...], axis=0)
    image_ref[...] = image
    squares = jnp.sum(image[:-8] * image[:-8], axis=0, keepdims=True)
    energy = jnp.sum(squares, axis=1, keepdims=True)
    energy_ref[...] = jnp.broadcast_to(energy.reshape(1, 1, 1), energy_ref.shape)


def merge(parts):
    return pl.pallas_call(
        merge_kernel,
        out_shape=(
            jax.ShapeDtypeStruct(parts.shape[1:], F32),
            jax.ShapeDtypeStruct((SOURCES, 1, 128), F32),
        ),
        in_specs=[VMEM],
        out_specs=(VMEM,) * 2,
        compiler_params=pltpu.CompilerParams(vmem_limit_bytes=4 * 2**20),
        name="merge",
    )(parts)


def finish_kernel(energy_ref, image_ref, tgt_ref, dir_ref, sol_ref, res_ref):
    height = tgt_ref.shape[0]
    step = image_ref[height : height + 1, :] / jnp.sum(energy_ref[...], axis=0)
    sol_ref[...] = jnp.tile(step, (1, dir_ref.shape[1] // 128)) * dir_ref[...]
    res_ref[...] = tgt_ref[...] - step * image_ref[:height]


def finish(energies, image, target, direction):
    return pl.pallas_call(
        finish_kernel,
        out_shape=(
            jax.ShapeDtypeStruct(direction.shape, F32),
            jax.ShapeDtypeStruct(target.shape, F32),
        ),
        in_specs=[VMEM] * 4,
        out_specs=(VMEM,) * 2,
        compiler_params=pltpu.CompilerParams(vmem_limit_bytes=4 * 2**20),
        name="finish",
    )(energies, image, target, direction)


def body(design, rademacher, target, sample_rows, checksum_seeds):
    height, breadth = design.shape
    position = lax.axis_index(ROWS).astype(jnp.int32).reshape(1)
    drawn = share(sample_rows.reshape(1, 16), ROWS, SOURCES)
    mixed, back = mix(target.reshape(1, height), rademacher.reshape(1, height), design)
    near = pick(position, drawn, mixed.reshape(height, 2, 128), back.reshape(4, 2, 128))
    pieces = deal(exchange(near, NEAR))
    rows, back = fold(exchange(pieces, FAR))
    rows = exchange(rows.reshape(ZB, 32, 128), FAR).reshape(ZB * 32, 128)
    images, direction, checksum = factor(
        exchange(gram(rows), NEAR), back.reshape(2, 128), checksum_seeds.reshape(1, breadth), design
    )
    image, energy = merge(exchange(images, GRPS))
    solved, residual = finish(
        exchange(energy, ROWS), image, target.reshape(height // 128, 128), direction
    )
    return solved.reshape(breadth), residual.reshape(height), checksum.reshape(breadth)


def solution(mesh):
    fine = Mesh(mesh.devices.reshape(ZB, ZA, Y, X, C), ROWS + GRPS)
    in_specs = (P(ROWS, GRPS), P(ROWS), P(ROWS), P(ROWS, GRPS, None), P(GRPS))
    out_specs = (P(GRPS), P(ROWS), P(GRPS))
    return jax.shard_map(body, mesh=fine, in_specs=in_specs, out_specs=out_specs, check_vma=False)
```

```python
import functools

import jax
import jax.numpy as jnp
from jax import lax
from jax.experimental import pallas as pl
from jax.experimental.pallas import tpu as pltpu
from jax.sharding import Mesh, PartitionSpec as P

ZB, ZA, Y, X, C = 8, 2, 4, 4, 2
SOURCES = ZB * ZA * Y
FAR = "zb"
NEAR = ("za", "y")
ROWS = (FAR,) + NEAR
GRPS = ("x", "c")
F32 = jnp.float32
BF16 = jnp.bfloat16
VMEM = pl.BlockSpec(memory_space=pltpu.VMEM)
SMEM = pl.BlockSpec(memory_space=pltpu.SMEM)


def cost(flops, size):
    return pl.CostEstimate(flops=flops, bytes_accessed=size, transcendentals=0)


def parity_sign(bits):
    bits = jnp.bitwise_xor(bits, jnp.right_shift(bits, 8))
    bits = jnp.bitwise_xor(bits, jnp.right_shift(bits, 4))
    odd = jnp.bitwise_and(jnp.right_shift(0x6996, jnp.bitwise_and(bits, 15)), 1)
    return 1.0 - 2.0 * odd.astype(F32)


def split3(value):
    hi = value.astype(BF16)
    rest = value - hi.astype(F32)
    mid = rest.astype(BF16)
    lo = (rest - mid.astype(F32)).astype(BF16)
    return hi, mid, lo


def mix_kernel(tgt_ref, rad_ref, slab_ref, mixed_ref, back_ref, work_ref):
    height, breadth = slab_ref.shape
    block = 256
    blocks = height // block
    row = lax.broadcasted_iota(jnp.int32, (block, block), 0)
    lane = lax.broadcasted_iota(jnp.int32, (block, block), 1)
    table = parity_sign(jnp.bitwise_and(row, lane)) * 0.03125
    rows = jnp.concatenate(list(split3(tgt_ref[...])) + [jnp.zeros((13, height), BF16)], axis=0)
    back = jnp.zeros((16, breadth), F32)
    for place in range(blocks):
        at = place * block
        sign = 1.0 - 2.0 * rad_ref[:, at : at + block].astype(F32)
        left = (table * sign).astype(BF16)
        total = jnp.zeros((block, breadth), F32)
        for term in split3(slab_ref[at : at + block, :]):
            total = total + jnp.dot(left, term, preferred_element_type=F32)
            back = back + jnp.dot(rows[:, at : at + block], term, preferred_element_type=F32)
        work_ref[at : at + block, :] = total
    back = jnp.sum(back, axis=0, keepdims=True)
    for copy in range(4):
        back_ref[2 * copy : 2 * copy + 1, :] = back[:, :128]
        back_ref[2 * copy + 1 : 2 * copy + 2, :] = back[:, 128:]
    for chunk in range(block // 8):
        tiles = [work_ref[b * block + chunk * 8 : b * block + chunk * 8 + 8, :] for b in range(blocks)]
        stride = 1
        while stride < blocks:
            tiles = [
                tiles[b] + tiles[b ^ stride] if b & stride == 0 else tiles[b ^ stride] - tiles[b]
                for b in range(blocks)
            ]
            stride *= 2
        for b in range(blocks):
            at = 2 * (b * block + chunk * 8)
            mixed_ref[pl.ds(at, 8, stride=2), :] = tiles[b][:, :128]
            mixed_ref[pl.ds(at + 1, 8, stride=2), :] = tiles[b][:, 128:]


def mix(target, rademacher, design):
    height, breadth = design.shape
    return pl.pallas_call(
        mix_kernel,
        out_shape=(
            jax.ShapeDtypeStruct((2 * height, 128), F32),
            jax.ShapeDtypeStruct((8, 128), F32),
        ),
        in_specs=[VMEM] * 3,
        out_specs=(VMEM,) * 2,
        scratch_shapes=[pltpu.VMEM((height, breadth), F32)],
        compiler_params=pltpu.CompilerParams(vmem_limit_bytes=24 * 2**20),
        cost_estimate=cost(2**30, 2**23),
        name="mix",
    )(target, rademacher, design)


def pick_kernel(pos_ref, idx_ref, mixed_ref, back_ref, out_ref):
    per_owner = idx_ref.shape[2]
    owners = 128 // per_owner

    def one(piece, carry):
        for near in range(owners):
            owner = piece * owners + near
            odd = jnp.bitwise_and(owner, pos_ref[0])
            for shift in (4, 2, 1):
                odd = jnp.bitwise_xor(odd, jnp.right_shift(odd, shift))
            sign = (1 - 2 * jnp.bitwise_and(odd, 1)).astype(F32)
            for slot in range(per_owner):
                drawn = mixed_ref[idx_ref[owner, 0, slot]]
                out_ref[piece, near * per_owner + slot] = drawn * sign
        out_ref[piece, 128] = back_ref[0]
        return carry

    lax.fori_loop(0, out_ref.shape[0], one, 0)


def pick(position, drawn, mixed, back):
    return pl.pallas_call(
        pick_kernel,
        out_shape=jax.ShapeDtypeStruct((ZA * Y, 129, 2, 128), F32),
        in_specs=[SMEM] * 2 + [VMEM] * 2,
        out_specs=VMEM,
        compiler_params=pltpu.CompilerParams(vmem_limit_bytes=8 * 2**20),
        cost_estimate=cost(2**20, 2**21),
        name="pick",
    )(position, drawn, mixed, back)


def exchange(pieces, axes):
    return lax.all_to_all(pieces, axes, split_axis=0, concat_axis=0, tiled=True)


def share(value, axes, count):
    return exchange(jnp.broadcast_to(value[None], (count,) + value.shape), axes)


NB = 32


def spread_row(value, row):
    return jnp.broadcast_to(value[row : row + 1, :], (8, value.shape[1]))


def dot_nt(left, right):
    return lax.dot_general(left, right, (((1,), (1,)), ((), ())), preferred_element_type=F32)


def dot_tn(left, right):
    return lax.dot_general(left, right, (((0,), (0,)), ((), ())), preferred_element_type=F32)


def deal_kernel(parts_ref, out_ref):
    total = jnp.sum(parts_ref[...], axis=0)
    for copy in range(ZB):
        out_ref[copy, 0:16] = total[16 * copy : 16 * copy + 16]
        out_ref[copy, 16:17] = total[128:129]


def deal(parts):
    return pl.pallas_call(
        deal_kernel,
        out_shape=jax.ShapeDtypeStruct((ZB, 17, 2, 128), F32),
        in_specs=[VMEM],
        out_specs=VMEM,
        compiler_params=pltpu.CompilerParams(vmem_limit_bytes=8 * 2**20),
        name="deal",
    )(parts)


def fold_kernel(parts_ref, rows_ref, back_ref):
    total = jnp.sum(parts_ref[...], axis=0)
    for copy in range(ZB):
        rows_ref[copy] = total[0:16]
    back_ref[...] = total[16:17]


def fold(parts):
    return pl.pallas_call(
        fold_kernel,
        out_shape=(
            jax.ShapeDtypeStruct((ZB, 16, 2, 128), F32),
            jax.ShapeDtypeStruct((1, 2, 128), F32),
        ),
        in_specs=[VMEM],
        out_specs=(VMEM,) * 2,
        compiler_params=pltpu.CompilerParams(vmem_limit_bytes=4 * 2**20),
        name="fold",
    )(parts)


def gram_products(rows):
    hi, mid, lo = split3(rows)
    right = jnp.concatenate([hi, mid, hi, lo, hi, mid], axis=0)
    hi, mid, lo = split3(rows.T)
    left = jnp.concatenate([hi, hi, mid, hi, lo, mid], axis=1)
    top = jnp.dot(left[:128], right, preferred_element_type=F32)
    end = jnp.dot(left[128:], right[:, 128:], preferred_element_type=F32)
    return top[:, :128], top[:, 128:], end


def gram_kernel(rows_ref, out_ref):
    count = rows_ref.shape[0] // 2
    rows = [rows_ref[pl.ds(half, count, stride=2), :] for half in range(2)]
    first, corner, last = gram_products(jnp.concatenate(rows, axis=1))
    row = lax.broadcasted_iota(jnp.int32, (128, 128), 0)
    lane = lax.broadcasted_iota(jnp.int32, (128, 128), 1)
    mixed = jnp.where(row <= lane, first, last)
    diagonal = jnp.sum(jnp.where(row == lane, last, 0.0), axis=0, keepdims=True)
    for copy in range(ZA * Y):
        out_ref[copy, 0:128, :] = mixed
        out_ref[copy, 128:256, :] = corner
        out_ref[copy, 256:264, :] = jnp.broadcast_to(diagonal, (8, 128))


def gram(rows):
    return pl.pallas_call(
        gram_kernel,
        out_shape=jax.ShapeDtypeStruct((ZA * Y, 264, 128), F32),
        in_specs=[VMEM],
        out_specs=VMEM,
        cost_estimate=cost(2**27, 2**20),
        compiler_params=pltpu.CompilerParams(vmem_limit_bytes=4 * 2**20),
        name="gram",
    )(rows)


def factor_kernel(gram_ref, back_ref, seed_ref, slab_ref, image_ref, dir_ref, check_ref, work_ref):
    height, size = slab_ref.shape
    blocks = jnp.sum(gram_ref[...], axis=0)
    mixed, corner, diagonal = blocks[:128], blocks[128:256], blocks[256:257]
    turned = mixed.T
    row = lax.broadcasted_iota(jnp.int32, (128, 128), 0)
    lane = lax.broadcasted_iota(jnp.int32, (128, 128), 1)
    first = jnp.where(row <= lane, mixed, turned)
    last = jnp.where(row == lane, diagonal, jnp.where(row > lane, mixed, turned))
    gram = jnp.concatenate(
        [
            jnp.concatenate([first, corner], axis=1),
            jnp.concatenate([corner.T, last], axis=1),
        ],
        axis=0,
    )
    sub = lax.broadcasted_iota(jnp.int32, (128, size), 0)
    weights = seed_ref[...].astype(F32) * 0.0625
    weight_rows = jnp.where(sub == 1, jnp.broadcast_to(weights, (128, size)), 0.0).astype(BF16)
    back = jnp.concatenate([back_ref[0:1, :], back_ref[1:2, :]], axis=1)
    back_rows = jnp.where(sub == 0, jnp.broadcast_to(back, (128, size)), 0.0)
    eye = (
        lax.broadcasted_iota(jnp.int32, (size, size), 0)
        == lax.broadcasted_iota(jnp.int32, (size, size), 1)
    ).astype(BF16)
    extra = jnp.zeros((size, 128), F32)
    for term in split3(gram):
        extra = extra + dot_nt(term, weight_rows)
    for term in split3(back_rows):
        extra = extra + dot_nt(eye, term)
    work_ref[:, :size] = gram
    work_ref[:, size:] = extra

    wide = size + 128
    lane = lax.broadcasted_iota(jnp.int32, (NB, wide), 1)
    row = lax.broadcasted_iota(jnp.int32, (NB, wide), 0)
    half_row = lax.broadcasted_iota(jnp.int32, (8, 128), 0)
    wide_half = lax.broadcasted_iota(jnp.int32, (8, wide), 1)
    half_count = NB // 8
    tiles = wide // 128
    for block in range(size // NB):
        at = block * NB
        halves = [work_ref[at + 8 * h : at + 8 * h + 8, :] for h in range(half_count)]
        scales = [jnp.zeros((8, 128), F32)] * half_count
        for phase in range(2):
            base = 16 * phase
            begin = at + base
            cols = {
                (c, h): jnp.broadcast_to(halves[h][:, at + c : at + c + 1], (8, 128))
                for c in range(base, base + 16)
                for h in range(c // 8, half_count)
            }
            for h in range(2 * phase, half_count):
                unit = (wide_half - begin == half_row[:, :1] + (8 * h - base)).astype(F32)
                inside = (wide_half >= begin) & (wide_half < begin + 16)
                halves[h] = jnp.where(inside, unit, halves[h])
            pivot = spread_row(cols[base, base // 8], 0)
            for j in range(base, base + 16):
                inverse = 1.0 / pivot
                here = j // 8
                scales[here] = jnp.where(half_row == j % 8, pivot, scales[here])
                if j + 1 == NB:
                    break
                across = {
                    c: spread_row(cols[j, c // 8], c % 8) for c in range(j + 1, base + 16)
                }
                if j + 1 < base + 16:
                    pivot = (
                        spread_row(cols[j + 1, (j + 1) // 8], (j + 1) % 8)
                        - across[j + 1] * across[j + 1] * inverse
                    )
                source = spread_row(halves[here], j % 8)
                for h in range((j + 1) // 8, half_count):
                    below = cols[j, h] * inverse
                    if h == here:
                        below = jnp.where(half_row > j % 8, below, 0.0)
                    halves[h] = halves[h] - jnp.tile(below, (1, tiles)) * source
                    for c in range(j + 1, base + 16):
                        if c // 8 <= h:
                            cols[c, h] = cols[c, h] - below * across[c]
        panel = jnp.concatenate(
            [
                half * jnp.tile(lax.rsqrt(scale), (1, tiles))
                for half, scale in zip(halves, scales)
            ],
            axis=0,
        )
        work_ref[at : at + NB, :] = panel
        if at + NB < size:
            hi, mid, lo = split3(panel)
            begin = 128 if at + NB >= 128 else 0
            zero = jnp.zeros((NB, size - begin), BF16)
            keep = lane[:, begin:size] >= at + NB
            lhi, lmid, llo = [
                jnp.where(keep, term[:, begin:size], zero) for term in (hi, mid, lo)
            ]
            left = jnp.concatenate([lhi, lhi, lmid, lhi, llo, lmid], axis=0)
            blank = (row < 16) & (lane >= at + 16) & (lane < at + NB)
            hi, mid, lo = [
                jnp.where(blank, jnp.zeros((NB, wide), BF16), term) for term in (hi, mid, lo)
            ]
            right = jnp.concatenate([hi, mid, hi, lo, hi, mid], axis=0)
            change = dot_tn(left, right)
            rest = size - at - NB
            tile = at // 128 * 128
            tile_lane = lax.broadcasted_iota(jnp.int32, (rest, 128), 1) + tile
            inside = (tile_lane >= at) & (tile_lane < at + NB)
            for start in range(0, wide, 128):
                old = work_ref[at + NB :, start : start + 128]
                if start == tile:
                    old = jnp.where(inside, 0.0, old)
                work_ref[at + NB :, start : start + 128] = (
                    old - change[at + NB - begin :, start : start + 128]
                )

    lower_inv = jnp.where(
        lax.broadcasted_iota(jnp.int32, (size, size), 0)
        >= lax.broadcasted_iota(jnp.int32, (size, size), 1),
        work_ref[:, :size],
        0.0,
    )
    half = work_ref[:, size : size + 1]
    check = work_ref[:, size + 1 : size + 2]
    direction = jnp.sum(lower_inv * half, axis=0, keepdims=True)
    diagonal = eye.astype(F32)
    check_ref[...] = jnp.sum(diagonal * check, axis=0, keepdims=True)
    dir_ref[...] = direction
    energy = jnp.sum(half * half, axis=0, keepdims=True)

    dhi, dmid, dlo = split3(direction)
    rows = jnp.concatenate([dhi, dmid, dlo, jnp.zeros((13, size), BF16)], axis=0)
    for part in range(height // 256):
        total = jnp.zeros((16, 256), F32)
        for term in split3(slab_ref[part * 256 : (part + 1) * 256, :]):
            total = total + dot_nt(rows, term)
        image = jnp.sum(total, axis=0, keepdims=True)
        for half in range(2):
            at = 2 * part + half
            image_ref[:, at : at + 1, :] = jnp.broadcast_to(
                image[None, :, half * 128 : (half + 1) * 128], (X * C, 1, 128)
            )
    image_ref[:, height // 128 :, :] = jnp.broadcast_to(energy[None], (X * C, 8, 128))


def factor(grams, back, seeds, design):
    height, breadth = design.shape
    return pl.pallas_call(
        factor_kernel,
        out_shape=(
            jax.ShapeDtypeStruct((X * C, height // 128 + 8, 128), F32),
            jax.ShapeDtypeStruct((1, breadth), F32),
            jax.ShapeDtypeStruct((1, breadth), F32),
        ),
        in_specs=[VMEM] * 4,
        out_specs=(VMEM,) * 3,
        scratch_shapes=[pltpu.VMEM((breadth, breadth + 128), F32)],
        compiler_params=pltpu.CompilerParams(vmem_limit_bytes=40 * 2**20),
        cost_estimate=cost(2**29, 2**22),
        name="factor",
    )(grams, back, seeds, design)


def merge_kernel(parts_ref, image_ref, energy_ref):
    image = jnp.sum(parts_ref[...], axis=0)
    image_ref[...] = image
    squares = jnp.sum(image[:-8] * image[:-8], axis=0, keepdims=True)
    energy = jnp.sum(squares, axis=1, keepdims=True)
    energy_ref[...] = jnp.broadcast_to(energy.reshape(1, 1, 1), energy_ref.shape)


def merge(parts):
    return pl.pallas_call(
        merge_kernel,
        out_shape=(
            jax.ShapeDtypeStruct(parts.shape[1:], F32),
            jax.ShapeDtypeStruct((SOURCES, 1, 128), F32),
        ),
        in_specs=[VMEM],
        out_specs=(VMEM,) * 2,
        compiler_params=pltpu.CompilerParams(vmem_limit_bytes=4 * 2**20),
        name="merge",
    )(parts)


def finish_kernel(energy_ref, image_ref, tgt_ref, dir_ref, sol_ref, res_ref):
    height = tgt_ref.shape[0]
    step = image_ref[height : height + 1, :] / jnp.sum(energy_ref[...], axis=0)
    sol_ref[...] = jnp.tile(step, (1, dir_ref.shape[1] // 128)) * dir_ref[...]
    res_ref[...] = tgt_ref[...] - step * image_ref[:height]


def finish(energies, image, target, direction):
    return pl.pallas_call(
        finish_kernel,
        out_shape=(
            jax.ShapeDtypeStruct(direction.shape, F32),
            jax.ShapeDtypeStruct(target.shape, F32),
        ),
        in_specs=[VMEM] * 4,
        out_specs=(VMEM,) * 2,
        compiler_params=pltpu.CompilerParams(vmem_limit_bytes=4 * 2**20),
        name="finish",
    )(energies, image, target, direction)


def body(design, rademacher, target, sample_rows, checksum_seeds):
    height, breadth = design.shape
    position = lax.axis_index(ROWS).astype(jnp.int32).reshape(1)
    drawn = share(sample_rows.reshape(1, 16), ROWS, SOURCES)
    mixed, back = mix(target.reshape(1, height), rademacher.reshape(1, height), design)
    near = pick(position, drawn, mixed.reshape(height, 2, 128), back.reshape(4, 2, 128))
    pieces = deal(exchange(near, NEAR))
    rows, back = fold(exchange(pieces, FAR))
    rows = exchange(rows.reshape(ZB, 32, 128), FAR).reshape(ZB * 32, 128)
    images, direction, checksum = factor(
        exchange(gram(rows), NEAR), back.reshape(2, 128), checksum_seeds.reshape(1, breadth), design
    )
    image, energy = merge(exchange(images, GRPS))
    solved, residual = finish(
        exchange(energy, ROWS), image, target.reshape(height // 128, 128), direction
    )
    return solved.reshape(breadth), residual.reshape(height), checksum.reshape(breadth)


def solution(mesh):
    fine = Mesh(mesh.devices.reshape(ZB, ZA, Y, X, C), ROWS + GRPS)
    in_specs = (P(ROWS, GRPS), P(ROWS), P(ROWS), P(ROWS, GRPS, None), P(GRPS))
    out_specs = (P(GRPS), P(ROWS), P(GRPS))
    return jax.shard_map(body, mesh=fine, in_specs=in_specs, out_specs=out_specs, check_vma=False)
```

```python
import functools

import jax
import jax.numpy as jnp
from jax import lax
from jax.experimental import pallas as pl
from jax.experimental.pallas import tpu as pltpu
from jax.sharding import Mesh, PartitionSpec as P

ZB, ZA, Y, X, C = 8, 2, 4, 4, 2
SOURCES = ZB * ZA * Y
FAR = "zb"
NEAR = ("za", "y")
ROWS = (FAR,) + NEAR
GRPS = ("x", "c")
F32 = jnp.float32
BF16 = jnp.bfloat16
VMEM = pl.BlockSpec(memory_space=pltpu.VMEM)
SMEM = pl.BlockSpec(memory_space=pltpu.SMEM)


def cost(flops, size):
    return pl.CostEstimate(flops=flops, bytes_accessed=size, transcendentals=0)


def parity_sign(bits):
    bits = jnp.bitwise_xor(bits, jnp.right_shift(bits, 8))
    bits = jnp.bitwise_xor(bits, jnp.right_shift(bits, 4))
    odd = jnp.bitwise_and(jnp.right_shift(0x6996, jnp.bitwise_and(bits, 15)), 1)
    return 1.0 - 2.0 * odd.astype(F32)


def split3(value):
    hi = value.astype(BF16)
    rest = value - hi.astype(F32)
    mid = rest.astype(BF16)
    lo = (rest - mid.astype(F32)).astype(BF16)
    return hi, mid, lo


def mix_kernel(tgt_ref, rad_ref, slab_ref, mixed_ref, back_ref, work_ref):
    height, breadth = slab_ref.shape
    block = 256
    blocks = height // block
    row = lax.broadcasted_iota(jnp.int32, (block, block), 0)
    lane = lax.broadcasted_iota(jnp.int32, (block, block), 1)
    table = parity_sign(jnp.bitwise_and(row, lane)) * 0.03125
    rows = jnp.concatenate(list(split3(tgt_ref[...])) + [jnp.zeros((13, height), BF16)], axis=0)
    back = jnp.zeros((16, breadth), F32)
    for place in range(blocks):
        at = place * block
        sign = 1.0 - 2.0 * rad_ref[:, at : at + block].astype(F32)
        left = (table * sign).astype(BF16)
        total = jnp.zeros((block, breadth), F32)
        for term in split3(slab_ref[at : at + block, :]):
            total = total + jnp.dot(left, term, preferred_element_type=F32)
            back = back + jnp.dot(rows[:, at : at + block], term, preferred_element_type=F32)
        work_ref[at : at + block, :] = total
    back = jnp.sum(back, axis=0, keepdims=True)
    for copy in range(4):
        back_ref[2 * copy : 2 * copy + 1, :] = back[:, :128]
        back_ref[2 * copy + 1 : 2 * copy + 2, :] = back[:, 128:]
    for chunk in range(block // 8):
        tiles = [work_ref[b * block + chunk * 8 : b * block + chunk * 8 + 8, :] for b in range(blocks)]
        stride = 1
        while stride < blocks:
            tiles = [
                tiles[b] + tiles[b ^ stride] if b & stride == 0 else tiles[b ^ stride] - tiles[b]
                for b in range(blocks)
            ]
            stride *= 2
        for b in range(blocks):
            at = 2 * (b * block + chunk * 8)
            mixed_ref[pl.ds(at, 8, stride=2), :] = tiles[b][:, :128]
            mixed_ref[pl.ds(at + 1, 8, stride=2), :] = tiles[b][:, 128:]


def mix(target, rademacher, design):
    height, breadth = design.shape
    return pl.pallas_call(
        mix_kernel,
        out_shape=(
            jax.ShapeDtypeStruct((2 * height, 128), F32),
            jax.ShapeDtypeStruct((8, 128), F32),
        ),
        in_specs=[VMEM] * 3,
        out_specs=(VMEM,) * 2,
        scratch_shapes=[pltpu.VMEM((height, breadth), F32)],
        compiler_params=pltpu.CompilerParams(vmem_limit_bytes=24 * 2**20),
        cost_estimate=cost(2**30, 2**23),
        name="mix",
    )(target, rademacher, design)


def pick_kernel(pos_ref, idx_ref, mixed_ref, back_ref, out_ref):
    per_owner = idx_ref.shape[2]
    owners = 128 // per_owner

    def one(piece, carry):
        for near in range(owners):
            owner = piece * owners + near
            odd = jnp.bitwise_and(owner, pos_ref[0])
            for shift in (4, 2, 1):
                odd = jnp.bitwise_xor(odd, jnp.right_shift(odd, shift))
            sign = (1 - 2 * jnp.bitwise_and(odd, 1)).astype(F32)
            for slot in range(per_owner):
                drawn = mixed_ref[idx_ref[owner, 0, slot]]
                out_ref[piece, near * per_owner + slot] = drawn * sign
        out_ref[piece, 128] = back_ref[0]
        return carry

    lax.fori_loop(0, out_ref.shape[0], one, 0, unroll=2)


def pick(position, drawn, mixed, back):
    return pl.pallas_call(
        pick_kernel,
        out_shape=jax.ShapeDtypeStruct((ZA * Y, 129, 2, 128), F32),
        in_specs=[SMEM] * 2 + [VMEM] * 2,
        out_specs=VMEM,
        compiler_params=pltpu.CompilerParams(vmem_limit_bytes=8 * 2**20),
        cost_estimate=cost(2**20, 2**21),
        name="pick",
    )(position, drawn, mixed, back)


def exchange(pieces, axes):
    return lax.all_to_all(pieces, axes, split_axis=0, concat_axis=0, tiled=True)


def share(value, axes, count):
    return exchange(jnp.broadcast_to(value[None], (count,) + value.shape), axes)


NB = 32


def spread_row(value, row):
    return jnp.broadcast_to(value[row : row + 1, :], (8, value.shape[1]))


def dot_nt(left, right):
    return lax.dot_general(left, right, (((1,), (1,)), ((), ())), preferred_element_type=F32)


def dot_tn(left, right):
    return lax.dot_general(left, right, (((0,), (0,)), ((), ())), preferred_element_type=F32)


def deal_kernel(parts_ref, out_ref):
    total = jnp.sum(parts_ref[...], axis=0)
    for copy in range(ZB):
        out_ref[copy, 0:16] = total[16 * copy : 16 * copy + 16]
        out_ref[copy, 16:17] = total[128:129]


def deal(parts):
    return pl.pallas_call(
        deal_kernel,
        out_shape=jax.ShapeDtypeStruct((ZB, 17, 2, 128), F32),
        in_specs=[VMEM],
        out_specs=VMEM,
        compiler_params=pltpu.CompilerParams(vmem_limit_bytes=8 * 2**20),
        name="deal",
    )(parts)


def fold_kernel(parts_ref, rows_ref, back_ref):
    total = jnp.sum(parts_ref[...], axis=0)
    for copy in range(ZB):
        rows_ref[copy] = total[0:16]
    back_ref[...] = total[16:17]


def fold(parts):
    return pl.pallas_call(
        fold_kernel,
        out_shape=(
            jax.ShapeDtypeStruct((ZB, 16, 2, 128), F32),
            jax.ShapeDtypeStruct((1, 2, 128), F32),
        ),
        in_specs=[VMEM],
        out_specs=(VMEM,) * 2,
        compiler_params=pltpu.CompilerParams(vmem_limit_bytes=4 * 2**20),
        name="fold",
    )(parts)


def gram_products(rows):
    hi, mid, lo = split3(rows)
    right = jnp.concatenate([hi, mid, hi, lo, hi, mid], axis=0)
    hi, mid, lo = split3(rows.T)
    left = jnp.concatenate([hi, hi, mid, hi, lo, mid], axis=1)
    top = jnp.dot(left[:128], right, preferred_element_type=F32)
    end = jnp.dot(left[128:], right[:, 128:], preferred_element_type=F32)
    return top[:, :128], top[:, 128:], end


def gram_kernel(rows_ref, out_ref):
    count = rows_ref.shape[0] // 2
    rows = [rows_ref[pl.ds(half, count, stride=2), :] for half in range(2)]
    first, corner, last = gram_products(jnp.concatenate(rows, axis=1))
    row = lax.broadcasted_iota(jnp.int32, (128, 128), 0)
    lane = lax.broadcasted_iota(jnp.int32, (128, 128), 1)
    mixed = jnp.where(row <= lane, first, last)
    diagonal = jnp.sum(jnp.where(row == lane, last, 0.0), axis=0, keepdims=True)
    for copy in range(ZA * Y):
        out_ref[copy, 0:128, :] = mixed
        out_ref[copy, 128:256, :] = corner
        out_ref[copy, 256:264, :] = jnp.broadcast_to(diagonal, (8, 128))


def gram(rows):
    return pl.pallas_call(
        gram_kernel,
        out_shape=jax.ShapeDtypeStruct((ZA * Y, 264, 128), F32),
        in_specs=[VMEM],
        out_specs=VMEM,
        cost_estimate=cost(2**27, 2**20),
        compiler_params=pltpu.CompilerParams(vmem_limit_bytes=4 * 2**20),
        name="gram",
    )(rows)


def factor_kernel(gram_ref, back_ref, seed_ref, slab_ref, image_ref, dir_ref, check_ref, work_ref):
    height, size = slab_ref.shape
    blocks = jnp.sum(gram_ref[...], axis=0)
    mixed, corner, diagonal = blocks[:128], blocks[128:256], blocks[256:257]
    turned = mixed.T
    row = lax.broadcasted_iota(jnp.int32, (128, 128), 0)
    lane = lax.broadcasted_iota(jnp.int32, (128, 128), 1)
    first = jnp.where(row <= lane, mixed, turned)
    last = jnp.where(row == lane, diagonal, jnp.where(row > lane, mixed, turned))
    gram = jnp.concatenate(
        [
            jnp.concatenate([first, corner], axis=1),
            jnp.concatenate([corner.T, last], axis=1),
        ],
        axis=0,
    )
    sub = lax.broadcasted_iota(jnp.int32, (128, size), 0)
    weights = seed_ref[...].astype(F32) * 0.0625
    weight_rows = jnp.where(sub == 1, jnp.broadcast_to(weights, (128, size)), 0.0).astype(BF16)
    back = jnp.concatenate([back_ref[0:1, :], back_ref[1:2, :]], axis=1)
    back_rows = jnp.where(sub == 0, jnp.broadcast_to(back, (128, size)), 0.0)
    eye = (
        lax.broadcasted_iota(jnp.int32, (size, size), 0)
        == lax.broadcasted_iota(jnp.int32, (size, size), 1)
    ).astype(BF16)
    extra = jnp.zeros((size, 128), F32)
    for term in split3(gram):
        extra = extra + dot_nt(term, weight_rows)
    for term in split3(back_rows):
        extra = extra + dot_nt(eye, term)
    work_ref[:, :size] = gram
    work_ref[:, size:] = extra

    wide = size + 128
    lane = lax.broadcasted_iota(jnp.int32, (NB, wide), 1)
    row = lax.broadcasted_iota(jnp.int32, (NB, wide), 0)
    half_row = lax.broadcasted_iota(jnp.int32, (8, 128), 0)
    wide_half = lax.broadcasted_iota(jnp.int32, (8, wide), 1)
    half_count = NB // 8
    tiles = wide // 128
    for block in range(size // NB):
        at = block * NB
        halves = [work_ref[at + 8 * h : at + 8 * h + 8, :] for h in range(half_count)]
        scales = [jnp.zeros((8, 128), F32)] * half_count
        for phase in range(2):
            base = 16 * phase
            begin = at + base
            cols = {
                (c, h): jnp.broadcast_to(halves[h][:, at + c : at + c + 1], (8, 128))
                for c in range(base, base + 16)
                for h in range(c // 8, half_count)
            }
            for h in range(2 * phase, half_count):
                unit = (wide_half - begin == half_row[:, :1] + (8 * h - base)).astype(F32)
                inside = (wide_half >= begin) & (wide_half < begin + 16)
                halves[h] = jnp.where(inside, unit, halves[h])
            pivot = spread_row(cols[base, base // 8], 0)
            for j in range(base, base + 16):
                inverse = 1.0 / pivot
                here = j // 8
                scales[here] = jnp.where(half_row == j % 8, pivot, scales[here])
                if j + 1 == NB:
                    break
                across = {
                    c: spread_row(cols[j, c // 8], c % 8) for c in range(j + 1, base + 16)
                }
                if j + 1 < base + 16:
                    pivot = (
                        spread_row(cols[j + 1, (j + 1) // 8], (j + 1) % 8)
                        - across[j + 1] * across[j + 1] * inverse
                    )
                source = spread_row(halves[here], j % 8)
                for h in range((j + 1) // 8, half_count):
                    below = cols[j, h] * inverse
                    if h == here:
                        below = jnp.where(half_row > j % 8, below, 0.0)
                    halves[h] = halves[h] - jnp.tile(below, (1, tiles)) * source
                    for c in range(j + 1, base + 16):
                        if c // 8 <= h:
                            cols[c, h] = cols[c, h] - below * across[c]
        panel = jnp.concatenate(
            [
                half * jnp.tile(lax.rsqrt(scale), (1, tiles))
                for half, scale in zip(halves, scales)
            ],
            axis=0,
        )
        work_ref[at : at + NB, :] = panel
        if at + NB < size:
            hi, mid, lo = split3(panel)
            begin = 128 if at + NB >= 128 else 0
            zero = jnp.zeros((NB, size - begin), BF16)
            keep = lane[:, begin:size] >= at + NB
            lhi, lmid, llo = [
                jnp.where(keep, term[:, begin:size], zero) for term in (hi, mid, lo)
            ]
            left = jnp.concatenate([lhi, lhi, lmid, lhi, llo, lmid], axis=0)
            blank = (row < 16) & (lane >= at + 16) & (lane < at + NB)
            hi, mid, lo = [
                jnp.where(blank, jnp.zeros((NB, wide), BF16), term) for term in (hi, mid, lo)
            ]
            right = jnp.concatenate([hi, mid, hi, lo, hi, mid], axis=0)
            change = dot_tn(left, right)
            rest = size - at - NB
            tile = at // 128 * 128
            tile_lane = lax.broadcasted_iota(jnp.int32, (rest, 128), 1) + tile
            inside = (tile_lane >= at) & (tile_lane < at + NB)
            for start in range(0, wide, 128):
                old = work_ref[at + NB :, start : start + 128]
                if start == tile:
                    old = jnp.where(inside, 0.0, old)
                work_ref[at + NB :, start : start + 128] = (
                    old - change[at + NB - begin :, start : start + 128]
                )

    lower_inv = jnp.where(
        lax.broadcasted_iota(jnp.int32, (size, size), 0)
        >= lax.broadcasted_iota(jnp.int32, (size, size), 1),
        work_ref[:, :size],
        0.0,
    )
    half = work_ref[:, size : size + 1]
    check = work_ref[:, size + 1 : size + 2]
    direction = jnp.sum(lower_inv * half, axis=0, keepdims=True)
    diagonal = eye.astype(F32)
    check_ref[...] = jnp.sum(diagonal * check, axis=0, keepdims=True)
    dir_ref[...] = direction
    energy = jnp.sum(half * half, axis=0, keepdims=True)

    dhi, dmid, dlo = split3(direction)
    rows = jnp.concatenate([dhi, dmid, dlo, jnp.zeros((13, size), BF16)], axis=0)
    for part in range(height // 256):
        total = jnp.zeros((16, 256), F32)
        for term in split3(slab_ref[part * 256 : (part + 1) * 256, :]):
            total = total + dot_nt(rows, term)
        image = jnp.sum(total, axis=0, keepdims=True)
        for half in range(2):
            at = 2 * part + half
            image_ref[:, at : at + 1, :] = jnp.broadcast_to(
                image[None, :, half * 128 : (half + 1) * 128], (X * C, 1, 128)
            )
    image_ref[:, height // 128 :, :] = jnp.broadcast_to(energy[None], (X * C, 8, 128))


def factor(grams, back, seeds, design):
    height, breadth = design.shape
    return pl.pallas_call(
        factor_kernel,
        out_shape=(
            jax.ShapeDtypeStruct((X * C, height // 128 + 8, 128), F32),
            jax.ShapeDtypeStruct((1, breadth), F32),
            jax.ShapeDtypeStruct((1, breadth), F32),
        ),
        in_specs=[VMEM] * 4,
        out_specs=(VMEM,) * 3,
        scratch_shapes=[pltpu.VMEM((breadth, breadth + 128), F32)],
        compiler_params=pltpu.CompilerParams(vmem_limit_bytes=40 * 2**20),
        cost_estimate=cost(2**29, 2**22),
        name="factor",
    )(grams, back, seeds, design)


def merge_kernel(parts_ref, image_ref, energy_ref):
    image = jnp.sum(parts_ref[...], axis=0)
    image_ref[...] = image
    squares = jnp.sum(image[:-8] * image[:-8], axis=0, keepdims=True)
    energy = jnp.sum(squares, axis=1, keepdims=True)
    energy_ref[...] = jnp.broadcast_to(energy.reshape(1, 1, 1), energy_ref.shape)


def merge(parts):
    return pl.pallas_call(
        merge_kernel,
        out_shape=(
            jax.ShapeDtypeStruct(parts.shape[1:], F32),
            jax.ShapeDtypeStruct((SOURCES, 1, 128), F32),
        ),
        in_specs=[VMEM],
        out_specs=(VMEM,) * 2,
        compiler_params=pltpu.CompilerParams(vmem_limit_bytes=4 * 2**20),
        name="merge",
    )(parts)


def finish_kernel(energy_ref, image_ref, tgt_ref, dir_ref, sol_ref, res_ref):
    height = tgt_ref.shape[0]
    step = image_ref[height : height + 1, :] / jnp.sum(energy_ref[...], axis=0)
    sol_ref[...] = jnp.tile(step, (1, dir_ref.shape[1] // 128)) * dir_ref[...]
    res_ref[...] = tgt_ref[...] - step * image_ref[:height]


def finish(energies, image, target, direction):
    return pl.pallas_call(
        finish_kernel,
        out_shape=(
            jax.ShapeDtypeStruct(direction.shape, F32),
            jax.ShapeDtypeStruct(target.shape, F32),
        ),
        in_specs=[VMEM] * 4,
        out_specs=(VMEM,) * 2,
        compiler_params=pltpu.CompilerParams(vmem_limit_bytes=4 * 2**20),
        name="finish",
    )(energies, image, target, direction)


def body(design, rademacher, target, sample_rows, checksum_seeds):
    height, breadth = design.shape
    position = lax.axis_index(ROWS).astype(jnp.int32).reshape(1)
    drawn = share(sample_rows.reshape(1, 16), ROWS, SOURCES)
    mixed, back = mix(target.reshape(1, height), rademacher.reshape(1, height), design)
    near = pick(position, drawn, mixed.reshape(height, 2, 128), back.reshape(4, 2, 128))
    pieces = deal(exchange(near, NEAR))
    rows, back = fold(exchange(pieces, FAR))
    rows = exchange(rows.reshape(ZB, 32, 128), FAR).reshape(ZB * 32, 128)
    images, direction, checksum = factor(
        exchange(gram(rows), NEAR), back.reshape(2, 128), checksum_seeds.reshape(1, breadth), design
    )
    image, energy = merge(exchange(images, GRPS))
    solved, residual = finish(
        exchange(energy, ROWS), image, target.reshape(height // 128, 128), direction
    )
    return solved.reshape(breadth), residual.reshape(height), checksum.reshape(breadth)


def solution(mesh):
    fine = Mesh(mesh.devices.reshape(ZB, ZA, Y, X, C), ROWS + GRPS)
    in_specs = (P(ROWS, GRPS), P(ROWS), P(ROWS), P(ROWS, GRPS, None), P(GRPS))
    out_specs = (P(GRPS), P(ROWS), P(GRPS))
    return jax.shard_map(body, mesh=fine, in_specs=in_specs, out_specs=out_specs, check_vma=False)
```
